128 devices in a mesh: batch: 16 (over y, z), seq: 8 (over x, core).
Axes of the slice: x: 4, y: 4, z: 4, core: 2. Of those that a mesh axis runs over, the one named last changes fastest.
Arguments:
- inputs: bfloat16 [32, 1024, 1088], P('batch', 'seq'), may hold values from -6 to 6
- out_grad: bfloat16 [32, 1024, 1088], P('batch', 'seq'), may hold values from -6 to 6
- segment_ids: int32 [32, 1024], P('batch', 'seq'), may hold values from 0 to 3, as said below
- qkv_weight: bfloat16 [1088, 3264], P('batch', 'seq'), may hold values from -0.1875 to 0.1875
- out_weight: bfloat16 [1088, 1088], P('batch', 'seq'), may hold values from -0.75 to 0.75
- up_weight: bfloat16 [1088, 4352], P('batch', 'seq'), may hold values from -0.1875 to 0.1875
- down_weight: bfloat16 [4352, 1088], P('batch', 'seq'), may hold values from -0.09375 to 0.09375
- norm_gains: bfloat16 [2, 1088], P(None, 'seq'), may hold values from 0.5 to 1.5
- norm_shifts: bfloat16 [2, 1088], P(None, 'seq'), may hold values from -2 to 2
- qv_bias: bfloat16 [2, 1088], P(None, 'seq'), may hold values from -2 to 2
- proj_bias: bfloat16 [2, 1088], P(None, 'seq'), may hold values from -2 to 2
- up_bias: bfloat16 [1, 4352], P(None, 'seq'), may hold values from -2 to 2
Outputs:
- layer_out: bfloat16 [32, 1024, 1088], P('batch', 'seq')
- input_grad: float32 [32, 1024, 1088], P('batch', 'seq')
- qkv_weight_grad: float32 [1088, 3264], P('batch', 'seq')
- out_weight_grad: float32 [1088, 1088], P('batch', 'seq')
- up_weight_grad: float32 [1088, 4352], P('batch', 'seq')
- down_weight_grad: float32 [4352, 1088], P('batch', 'seq')
- norm_gains_grad: float32 [2, 1088], P(None, 'seq')
- norm_shifts_grad: float32 [2, 1088], P(None, 'seq')
- qv_bias_grad: float32 [2, 1088], P(None, 'seq')
- proj_bias_grad: float32 [2, 1088], P(None, 'seq')
- up_bias_grad: float32 [1, 4352], P(None, 'seq')
The draws below stay inside these ranges and needn't reach their ends.
Inputs may be any that keep to these rules, and one draw needn't show every extreme that they name: `segment_ids`: within each sequence the document number starts at 0 at the first token, rises by one where a document starts, never falls and is at most 3; in each aligned group of 2 sequences one sequence, drawn from the seed, is a single document, and another reaches document number 3.
All inputs are finite; a program needn't handle non-finite values.
Results may differ from the reference program's by a relative error of at most 0.0089.
Values may be sent and summed in bfloat16 or wider, within the bound.
A program may use at most 192 MiB of HBM per device.

```python
import jax
import jax.numpy as jnp
from jax import lax

D = 1088
HEADS = 17
HEAD_DIM = 64
FF = 4352
SEQ_LEN = 1024
MICRO = 2
SEQS = 32


def draw_segment_ids(key, part):
    key = jax.random.fold_in(key, 11)
    key_starts, key_choice, key_forced = jax.random.split(key, 3)
    start_rate = max(SEQ_LEN // 3, 2)
    starts = jax.random.randint(key_starts, (SEQS, SEQ_LEN), 0, start_rate) == 0
    groups = SEQS // MICRO
    chosen = jax.random.randint(key_choice, (groups, 1), 0, MICRO)
    member = jnp.arange(MICRO)[None, :]
    single = (member == chosen).reshape(SEQS, 1)
    forced_row = (member == (chosen + 1) % MICRO).reshape(SEQS, 1)
    quarter = max(SEQ_LEN // 4, 1)
    offsets = jax.random.randint(key_forced, (SEQS, 3), 0, quarter)
    forced_places = (jnp.arange(1, 4)[None, :] * quarter + offsets).astype(jnp.int32)
    places = jnp.arange(SEQ_LEN)[None, :, None]
    forced = jnp.any(places == forced_places[:, None, :], axis=2) & forced_row
    after_first = jnp.arange(SEQ_LEN)[None, :] > 0
    flags = ((starts | forced) & after_first).astype(jnp.int32)
    start_flags = jnp.where(single, 0, flags)
    return jnp.minimum(jnp.cumsum(start_flags, axis=1), 3).astype(jnp.int32)


def levels(stream_key, dims, pieces, low, top_value):
    loudness, own = 1.0, jax.random.fold_in(stream_key, 6)
    for position, parts in pieces:
        draws = jnp.exp(jax.random.uniform(jax.random.fold_in(own, position), (parts,), jnp.float32, low / len(pieces), top_value / len(pieces)))
        loudness = loudness * jnp.repeat(draws, dims[position] // parts).reshape([-1 if axis == position else 1 for axis in range(len(dims))])
    return loudness


def gaussian(own_key, dims, scale, bound, pieces=(), kind=jnp.bfloat16):
    drawn = scale * jax.random.normal(own_key, dims, jnp.float32)
    if pieces:
        drawn = drawn * levels(own_key, dims, pieces, -0.22, 0.18)
    return jnp.clip(drawn, -bound, bound).astype(kind)


def setup_inputs(seed: int = 0) -> dict:
    keys = jax.random.split(jax.random.key(seed), 13)
    inputs = gaussian(keys[0], (SEQS, SEQ_LEN, D), 1.0, 6.0, ((0, 16), (1, 8)))
    out_grad = gaussian(keys[1], (SEQS, SEQ_LEN, D), 1.0, 6.0, ((0, 16), (1, 8)))
    segment_ids = draw_segment_ids(jax.random.fold_in(keys[12], 71), 0)
    qkv_weight = gaussian(keys[3], (D, 3 * D), D ** -0.5, 0.1875, ((0, 16), (1, 8)))
    out_weight = gaussian(keys[4], (D, D), (D // 16) ** -0.5, 0.75, ((0, 16), (1, 8)))
    up_weight = gaussian(keys[5], (D, FF), D ** -0.5, 0.1875, ((0, 16), (1, 8)))
    down_weight = gaussian(keys[6], (FF, D), FF ** -0.5, 0.09375, ((0, 16), (1, 8)))
    norm_gains = jnp.clip(1.0 + 0.1 * jax.random.normal(keys[7], (2, D), jnp.float32), 0.5, 1.5).astype(jnp.bfloat16)
    norm_shifts = gaussian(keys[8], (2, D), 0.3, 2.0, ((1, 8),))
    qv_bias = gaussian(keys[9], (2, D), 0.3, 2.0, ((1, 8),))
    proj_bias = gaussian(keys[10], (2, D), 0.3, 2.0, ((1, 8),))
    up_bias = gaussian(keys[11], (1, FF), 0.3, 2.0, ((1, 8),))
    return dict(inputs=inputs, out_grad=out_grad, segment_ids=segment_ids, qkv_weight=qkv_weight, out_weight=out_weight, up_weight=up_weight, down_weight=down_weight, norm_gains=norm_gains, norm_shifts=norm_shifts, qv_bias=qv_bias, proj_bias=proj_bias, up_bias=up_bias)


@jax.custom_vjp
def low(v):
    return lax.optimization_barrier(v.astype(jnp.bfloat16)).astype(jnp.float32)

@jax.custom_vjp
def low_back(v):
    return v

def low_keep(v):
    return (low(v), None)

def low_pass(kept, grad):
    return (grad,)

def back_keep(v):
    return (v, None)

def back_low(kept, grad):
    return (low(grad),)
low.defvjp(low_keep, low_pass)
low_back.defvjp(back_keep, back_low)
highest = lax.Precision.HIGHEST

def layer_norm(values, gain_row, shift_row):
    center = values - lax.optimization_barrier(jnp.mean(values, axis=-1, keepdims=True))
    spread = lax.optimization_barrier(jnp.mean(center * center, axis=-1, keepdims=True))
    return center * lax.rsqrt(spread + 1e-05) * gain_row + shift_row

def matmul(left, right):
    return jnp.dot(left, right, precision=highest, preferred_element_type=jnp.float32)

def block(hidden, documents, params):
    qkv_weight, out_weight, up_weight, down_weight, norm_gains, norm_shifts, qv_bias, proj_bias, up_bias = params
    length = hidden.shape[0]
    normed = low(layer_norm(hidden, norm_gains[0], norm_shifts[0]))
    projected = matmul(normed, qkv_weight)
    queries = low(low_back(projected[:, :D] + qv_bias[0]))
    key_rows = low(low_back(projected[:, D:2 * D]))
    value_rows = low(low_back(projected[:, 2 * D:] + qv_bias[1]))
    scores = jnp.einsum('qhd,khd->hqk', queries.reshape(length, HEADS, HEAD_DIM), key_rows.reshape(length, HEADS, HEAD_DIM), precision=highest) * HEAD_DIM ** (-0.5)
    scores = low_back(scores)
    places = jnp.arange(length)
    allowed = (documents[:, None] == documents[None, :]) & (places[None, :] <= places[:, None])
    scores = jnp.where(allowed[None], scores, -1e+30)
    soft_low = low(jax.nn.softmax(scores, axis=-1))
    attended = jnp.einsum('hqk,khd->qhd', soft_low, value_rows.reshape(length, HEADS, HEAD_DIM), precision=highest).reshape(length, D)
    attended = low(low_back(attended))
    branch = low_back(matmul(attended, out_weight) + proj_bias[0])
    middle = hidden + branch
    normed_two = low(layer_norm(middle, norm_gains[1], norm_shifts[1]))
    inner_pre = low_back(matmul(normed_two, up_weight) + up_bias[0])
    active = low(jax.nn.gelu(inner_pre, approximate=True))
    return middle + low_back(matmul(active, down_weight) + proj_bias[1])

def reference(inputs, out_grad, segment_ids, qkv_weight, out_weight, up_weight, down_weight, norm_gains, norm_shifts, qv_bias, proj_bias, up_bias):
    params = (qkv_weight.astype(jnp.float32), out_weight.astype(jnp.float32), up_weight.astype(jnp.float32), down_weight.astype(jnp.float32), norm_gains.astype(jnp.float32), norm_shifts.astype(jnp.float32), qv_bias.astype(jnp.float32), proj_bias.astype(jnp.float32), up_bias.astype(jnp.float32))
    checked = jax.checkpoint(block)

    def whole(hidden_all, weights):

        def one_sequence(paired):
            return checked(paired[0], paired[1], weights)
        return lax.map(one_sequence, (hidden_all, segment_ids))
    result, pullback = jax.vjp(whole, inputs.astype(jnp.float32), params)
    input_grad, grads = pullback(out_grad.astype(jnp.float32))
    return (result.astype(jnp.bfloat16), input_grad, grads[0], grads[1], grads[2], grads[3], grads[4], grads[5], grads[6], grads[7], grads[8])
```

```python
import jax
import jax.numpy as jnp
from jax import lax
from jax.sharding import PartitionSpec as P

D = 1088
HEADS = 17
HEAD_DIM = 64
FF = 4352
F32 = jnp.float32
BF16 = jnp.bfloat16
Z_GROUPS = [[4 * y + z for z in range(4)] for y in range(4)]
Y_GROUPS = [[4 * y + z for y in range(4)] for z in range(4)]


def normalize(values):
    center = values - jnp.mean(values, axis=-1, keepdims=True)
    spread = jnp.mean(center * center, axis=-1, keepdims=True)
    scale = lax.rsqrt(spread + 1e-05)
    return center * scale, scale


def norm_pull(grad, gain, unit, scale):
    scaled = grad * gain
    return scale * (
        scaled
        - jnp.mean(scaled, axis=-1, keepdims=True)
        - unit * jnp.mean(scaled * unit, axis=-1, keepdims=True)
    )


def gelu_tanh(values):
    return jax.nn.gelu(values, approximate=True)


def dot(left, right):
    return jnp.dot(left, right, preferred_element_type=F32)


def per_device(
    inputs, out_grad, segment_ids, qkv_weight, out_weight, up_weight, down_weight,
    norm_gains, norm_shifts, qv_bias, proj_bias, up_bias,
):
    seqs, rows, _ = inputs.shape
    tokens = seqs * rows
    first_row = lax.axis_index("seq") * rows
    scale = HEAD_DIM ** (-0.5)

    vec = jnp.concatenate(
        [norm_gains, norm_shifts, qv_bias, proj_bias, up_bias.reshape(4, 136)], axis=0
    )
    vec = lax.all_gather(vec, "seq", axis=0).astype(F32)
    pairs = vec[:, :8].transpose(1, 0, 2).reshape(8, D)
    gains, shifts, qv_rows, proj_rows = pairs[0:2], pairs[2:4], pairs[4:6], pairs[6:8]
    up_row = vec[:, 8:].reshape(FF)
    documents = lax.all_gather(segment_ids, "seq", axis=1, tiled=True)

    blob_a = jnp.concatenate([qkv_weight, out_weight, up_weight], axis=1)
    blob_b = down_weight.T
    blob_a = lax.all_gather(blob_a, "batch", axis=0, tiled=True)
    blob_b = lax.all_gather(blob_b, "batch", axis=1, tiled=True)
    whole_a = lax.all_gather(blob_a, "seq", axis=0)
    whole_b = lax.all_gather(blob_b, "seq", axis=0, tiled=True)
    w_qkv, w_out, w_up = whole_a[:, :, :408], whole_a[:, :, 408:544], whole_a[:, :, 544:]

    hidden = inputs.reshape(tokens, D).astype(F32)
    top_grad = out_grad.reshape(tokens, D)
    cotangent = top_grad.astype(F32)
    unit_one, scale_one = normalize(hidden)
    normed = (unit_one * gains[0] + shifts[0]).astype(BF16)
    projected = jnp.einsum("tk,skn->tsn", normed, w_qkv, preferred_element_type=F32).reshape(
        tokens, 3 * D
    )
    queries = (projected[:, :D] + qv_rows[0]).astype(BF16)
    key_rows = projected[:, D : 2 * D].astype(BF16)
    value_rows = (projected[:, 2 * D :] + qv_rows[1]).astype(BF16)

    key_value = jnp.concatenate([key_rows, value_rows], axis=1).reshape(seqs, rows, 2 * D)
    key_value = lax.all_gather(key_value, "seq", axis=1, tiled=True)
    total = key_value.shape[1]
    key_all = key_value[:, :, :D].reshape(seqs, total, HEADS, HEAD_DIM)
    value_all = key_value[:, :, D:].reshape(seqs, total, HEADS, HEAD_DIM)
    query_heads = queries.reshape(seqs, rows, HEADS, HEAD_DIM)
    query_docs = lax.dynamic_slice_in_dim(documents, first_row, rows, axis=1)
    allowed = (query_docs[:, :, None] == documents[:, None, :]) & (
        jnp.arange(total)[None, None, :] <= (first_row + jnp.arange(rows))[None, :, None]
    )
    scores = (
        jnp.einsum("bqhd,bkhd->bhqk", query_heads, key_all, preferred_element_type=F32) * scale
    )
    scores = jnp.where(allowed[:, None], scores, -1e30)
    peak = jnp.max(scores, axis=-1, keepdims=True)
    powers = jnp.exp(scores - peak)
    probs = powers / jnp.sum(powers, axis=-1, keepdims=True)
    soft_low = probs.astype(BF16)
    attended = (
        jnp.einsum("bhqk,bkhd->bqhd", soft_low, value_all, preferred_element_type=F32)
        .reshape(tokens, D)
        .astype(BF16)
    )
    branch = jnp.einsum("tk,skn->tsn", attended, w_out, preferred_element_type=F32)
    middle = hidden + branch.reshape(tokens, D) + proj_rows[0]
    unit_two, scale_two = normalize(middle)
    normed_two = (unit_two * gains[1] + shifts[1]).astype(BF16)
    inner_pre = (
        jnp.einsum("tk,skn->tsn", normed_two, w_up, preferred_element_type=F32).reshape(tokens, FF)
        + up_row
    )
    active, gelu_pull = jax.vjp(gelu_tanh, inner_pre)
    active = active.astype(BF16)
    layer_out = (
        middle
        + jnp.einsum("tf,df->td", active, whole_b, preferred_element_type=F32)
        + proj_rows[1]
    ).astype(BF16)

    down_in = dot(top_grad, whole_b)
    inner_grad = gelu_pull(down_in)[0].astype(BF16)
    inner_blocks = inner_grad.reshape(tokens, 8, 544)
    normed_two_grad = jnp.einsum("tsn,skn->tk", inner_blocks, w_up, preferred_element_type=F32)
    middle_grad = cotangent + norm_pull(normed_two_grad, gains[1], unit_two, scale_two)
    branch_grad = middle_grad.astype(BF16)
    branch_blocks = branch_grad.reshape(tokens, 8, 136)
    attended_grad = jnp.einsum(
        "tsn,skn->tk", branch_blocks, w_out, preferred_element_type=F32
    ).astype(BF16)
    attended_heads = attended_grad.reshape(seqs, rows, HEADS, HEAD_DIM)
    prob_grad = jnp.einsum("bqhd,bkhd->bhqk", attended_heads, value_all, preferred_element_type=F32)
    row_inner = jnp.sum(probs * prob_grad, axis=-1, keepdims=True)
    score_grad = (probs * (prob_grad - row_inner)).astype(BF16)
    query_grad = (
        jnp.einsum("bhqk,bkhd->bqhd", score_grad, key_all, preferred_element_type=F32) * scale
    ).reshape(tokens, D)
    key_terms = (
        jnp.einsum("bhqk,bqhd->bkhd", score_grad, query_heads, preferred_element_type=F32) * scale
    ).reshape(seqs, total, D)
    value_terms = jnp.einsum(
        "bhqk,bqhd->bkhd", soft_low, attended_heads, preferred_element_type=F32
    ).reshape(seqs, total, D)
    terms = jnp.concatenate([key_terms, value_terms], axis=2)
    terms = lax.psum_scatter(terms, "seq", scatter_dimension=1, tiled=True)
    qkv_grad = jnp.concatenate(
        [query_grad.astype(BF16), terms.reshape(tokens, 2 * D).astype(BF16)], axis=1
    )
    qkv_blocks = qkv_grad.reshape(tokens, 8, 408)
    normed_grad = jnp.einsum("tsn,skn->tk", qkv_blocks, w_qkv, preferred_element_type=F32)
    input_grad = middle_grad + norm_pull(normed_grad, gains[0], unit_one, scale_one)

    d_qkv = jnp.einsum("tk,tsn->skn", normed, qkv_blocks, preferred_element_type=F32)
    d_out = jnp.einsum("tk,tsn->skn", attended, branch_blocks, preferred_element_type=F32)
    d_up = jnp.einsum("tk,tsn->skn", normed_two, inner_blocks, preferred_element_type=F32)
    d_a = jnp.concatenate([d_qkv.astype(BF16), d_out.astype(BF16), d_up.astype(BF16)], axis=2)
    d_b = jnp.einsum("td,tf->df", top_grad, active, preferred_element_type=F32).astype(BF16)
    d_a = lax.psum_scatter(d_a, "seq", scatter_dimension=0)
    d_b = lax.psum_scatter(d_b, "seq", scatter_dimension=0, tiled=True)
    d_a = lax.psum_scatter(d_a, "batch", scatter_dimension=0, tiled=True).astype(F32)
    d_b = d_b.reshape(136, 16, 272).transpose(1, 0, 2)
    d_b = lax.psum_scatter(d_b, "batch", scatter_dimension=0).astype(F32)

    def column_sum(values):
        return jnp.sum(values, axis=0, dtype=F32)

    sums = jnp.stack(
        [
            column_sum(normed_grad * unit_one),
            column_sum(normed_two_grad * unit_two),
            column_sum(normed_grad),
            column_sum(normed_two_grad),
            column_sum(qkv_grad[:, :D]),
            column_sum(qkv_grad[:, 2 * D :]),
            column_sum(branch_grad),
            column_sum(top_grad),
        ]
    ).reshape(8, 8, 136)
    sums = jnp.concatenate(
        [sums.transpose(1, 0, 2), column_sum(inner_grad).reshape(8, 4, 136)], axis=1
    )
    sums = lax.psum_scatter(sums, "seq", scatter_dimension=0)
    sums = lax.psum(sums, "batch")
    return (
        layer_out.reshape(seqs, rows, D),
        input_grad.reshape(seqs, rows, D),
        d_a[:, :408],
        d_a[:, 408:544],
        d_a[:, 544:],
        d_b.T,
        sums[0:2],
        sums[2:4],
        sums[4:6],
        sums[6:8],
        sums[8:12].reshape(1, 544),
    )


def solution(mesh):
    tokens = P("batch", "seq", None)
    matrix = P("batch", "seq")
    vector = P(None, "seq")
    return jax.shard_map(
        per_device,
        mesh=mesh,
        in_specs=(tokens, tokens, matrix, matrix, matrix, matrix, matrix) + (vector,) * 5,
        out_specs=(tokens, tokens, matrix, matrix, matrix, matrix) + (vector,) * 5,
        check_vma=False,
    )
```

```python
import jax
import jax.numpy as jnp
from jax import lax
from jax.experimental import pallas as pl
from jax.experimental.pallas import tpu as pltpu
from jax.sharding import PartitionSpec as P

D = 1088
F32 = jnp.float32
BF16 = jnp.bfloat16
MESH = pl.DeviceIdType.MESH
A_ROWS, B_ROWS = 272, 144
CUT = 208


class Place:
    def __init__(self):
        batch, seq = lax.axis_index("batch"), lax.axis_index("seq")
        self.y, self.z = batch // 4, batch % 4
        self.x, self.c = seq // 2, seq % 2
        self.sibling = {"batch": batch, "seq": self.x * 2 + 1 - self.c}

    def peer(self, axis, step):
        spot = {"x": self.x, "y": self.y, "z": self.z}
        spot[axis] = (spot[axis] + step + 4) % 4
        return {"batch": spot["y"] * 4 + spot["z"], "seq": spot["x"] * 2 + self.c}


def greet(peers):
    barrier = pltpu.get_barrier_semaphore()
    for peer in peers:
        pl.semaphore_signal(barrier, inc=1, device_id=peer, device_id_type=MESH)
    pl.semaphore_wait(barrier, len(peers))


def all_peers(me):
    return [me.sibling] + [me.peer(axis, step) for axis, step in (
        ("x", 1), ("x", 3), ("y", 1), ("y", 3), ("z", 1), ("z", 2), ("z", 3))]


class Sender:
    def __init__(self, send_sems, recv_sems):
        self.send_sems, self.recv_sems, self.made = send_sems, recv_sems, []

    def __call__(self, source, target, peer):
        index = len(self.made)
        copy = pltpu.make_async_remote_copy(
            src_ref=source, dst_ref=target, send_sem=self.send_sems.at[index],
            recv_sem=self.recv_sems.at[index], device_id=peer, device_id_type=MESH)
        copy.start()
        self.made.append(copy)
        return copy


def merge_rows(stacked):
    row = lax.broadcasted_iota(jnp.int32, (A_ROWS, 320), 0)
    col = lax.broadcasted_iota(jnp.int32, (A_ROWS, 320), 1)
    pick = jnp.where(col == row + 12 * (row // 68), 1.0, 0.0).astype(BF16)
    return jnp.dot(pick, stacked, preferred_element_type=F32).astype(BF16)


def merge_columns(slots):
    total = None
    for z in range(4):
        row = lax.broadcasted_iota(jnp.int32, (384, D), 0)
        col = lax.broadcasted_iota(jnp.int32, (384, D), 1)
        pick = jnp.where((col == row + 272 * z) & (row < 272), 1.0, 0.0).astype(BF16)
        term = jnp.dot(slots[z], pick, preferred_element_type=F32)
        total = term if total is None else total + term
    return total.astype(BF16)


GATHER_COPIES = 120


def gather_kernel(a_ref, b_ref, ga, gb, za, zb, mine_a, mine_b, send_sems, recv_sems, local_sems):
    me = Place()
    greet(all_peers(me))
    send = Sender(send_sems, recv_sems)
    first = []
    for step in (1, 2, 3):
        peer = me.peer("z", step)
        first.append(send(a_ref, za.at[me.z], peer))
        first.append(send(b_ref, zb.at[me.z], peer))
    za[me.z] = a_ref[...]
    zb[me.z] = b_ref[...]
    for copy in first:
        copy.wait_recv()
    mine_a[...] = merge_rows(za[...].reshape(320, D))
    mine_b[...] = merge_columns(zb)

    def spot(part, step_x, step_y):
        x, y = (me.x + step_x) % 4, (me.y + step_y) % 4
        if part == "b":
            return gb.at[y, 2 * x + me.c]
        low, rows = part
        return ga.at[2 * x + me.c, pl.ds(pl.multiple_of(y * A_ROWS + low, 16), rows)]

    own = [pltpu.make_async_copy(mine_a, spot((0, A_ROWS), 0, 0), local_sems.at[0]),
           pltpu.make_async_copy(mine_b, spot("b", 0, 0), local_sems.at[1])]
    for copy in own:
        copy.start()
    whole = {0: [(0, CUT)], 1: [(CUT, A_ROWS - CUT), "b"]}
    split = {0: [(0, 96), (96, CUT - 96)], 1: [(CUT, A_ROWS - CUT), "b"]}

    def source(part, steps):
        if steps != (0, 0):
            return spot(part, *steps)
        if part == "b":
            return mine_b
        return mine_a.at[pl.ds(part[0], part[1])]

    def move(axis, steps, by):
        return ((steps[0] + by) % 4, steps[1]) if axis == "x" else (steps[0], (steps[1] + by) % 4)

    crossed = []

    def to_sibling(part, steps):
        crossed.append(send(source(part, steps), spot(part, *steps), me.sibling))

    def begin(half, axis, steps):
        return {by: [send(source(part, steps), spot(part, *steps), me.peer(axis, by))
                     for part in whole[half]] for by in (1, 3)}

    def forward(half, axis, steps, sent, flip):
        ends = []
        for by, which in ((1, flip), (3, 1 - flip)):
            origin = move(axis, steps, -by)
            for copy in sent[by]:
                copy.wait_recv()
            part = split[half][which]
            ends.append((send(spot(part, *origin), spot(part, *origin), me.peer(axis, by)), part))
        return ends

    def arrived(half, axis, steps):
        for by in (1, 3):
            for part in whole[half]:
                to_sibling(part, move(axis, steps, by))

    def finish(half, axis, steps, ends):
        for copy, part in ends:
            copy.wait_recv()
        for part in whole[half]:
            to_sibling(part, move(axis, steps, 2))

    axes = {0: ("x", "y"), 1: ("y", "x")}
    first = {half: begin(half, axes[half][0], (0, 0)) for half in (0, 1)}
    second = {(half, 0): begin(half, axes[half][1], (0, 0)) for half in (0, 1)}
    to_sibling((0, A_ROWS), (0, 0))
    to_sibling("b", (0, 0))
    ends = {}
    for half in (0, 1):
        axis = axes[half][0]
        ends[half] = forward(half, axis, (0, 0), first[half], half)
        for by in (1, 3):
            second[half, by] = begin(half, axes[half][1], move(axis, (0, 0), by))
    for half in (0, 1):
        arrived(half, axes[half][0], (0, 0))
    tails = {}
    for half in (0, 1):
        tails[half, 0] = forward(half, axes[half][1], (0, 0), second[half, 0], 0)
        arrived(half, axes[half][1], (0, 0))
    for half in (0, 1):
        axis = axes[half][0]
        finish(half, axis, (0, 0), ends[half])
        second[half, 2] = begin(half, axes[half][1], move(axis, (0, 0), 2))
    order = [(half, by) for by in (1, 3, 2) for half in (0, 1)]
    done = [(half, 0) for half in (0, 1)]
    for half, by in order:
        steps = move(axes[half][0], (0, 0), by)
        tails[half, by] = forward(half, axes[half][1], steps, second[half, by], by % 2)
        arrived(half, axes[half][1], steps)
        if done:
            late, late_by = done.pop(0)
            finish(late, axes[late][1], move(axes[late][0], (0, 0), late_by), tails[late, late_by])
        done.append((half, by))
    for late, late_by in done:
        finish(late, axes[late][1], move(axes[late][0], (0, 0), late_by), tails[late, late_by])
    for copy in crossed:
        copy.wait_recv()
    for copy in send.made:
        copy.wait_send()
    for copy in own:
        copy.wait()


def gather_weights(blob_a, blob_b):
    return pl.pallas_call(
        gather_kernel,
        out_shape=(jax.ShapeDtypeStruct((8, D, D), BF16),
                   jax.ShapeDtypeStruct((4, 8, B_ROWS, D), BF16)),
        in_specs=[pl.BlockSpec(memory_space=pltpu.VMEM)] * 2,
        out_specs=(pl.BlockSpec(memory_space=pl.ANY),) * 2,
        scratch_shapes=[
            pltpu.VMEM((4, 80, D), BF16), pltpu.VMEM((4, B_ROWS, 384), BF16),
            pltpu.VMEM((A_ROWS, D), BF16), pltpu.VMEM((B_ROWS, D), BF16),
            pltpu.SemaphoreType.DMA((GATHER_COPIES,)), pltpu.SemaphoreType.DMA((GATHER_COPIES,)),
            pltpu.SemaphoreType.DMA((2,)),
        ],
        compiler_params=pltpu.CompilerParams(
            collective_id=0, has_side_effects=True, vmem_limit_bytes=40 * 2**20),
    )(blob_a, blob_b)


NT = (((1,), (1,)), ((), ()))


class Group:
    def __init__(self):
        self.batch, self.me = lax.axis_index("batch"), lax.axis_index("seq")

    def peer(self, seq):
        return {"batch": self.batch, "seq": seq}

    def other(self, step):
        return (self.me + step) % 8


def push(source, target, sems, index, peer):
    return pltpu.make_async_remote_copy(
        src_ref=source, dst_ref=target, send_sem=sems.at[(0,) + index],
        recv_sem=sems.at[(1,) + index], device_id=peer, device_id_type=MESH)


def turned(value):
    return value.astype(F32).T


def masked(scores, bounds, seq, block):
    rows = lax.broadcasted_iota(jnp.int32, scores.shape, 0)
    spot = block * 256 + lax.broadcasted_iota(jnp.int32, (1, 256), 1)
    start = jnp.zeros((1, 256), jnp.int32)
    for n in range(3):
        bound = bounds[seq, n]
        start = jnp.where(spot >= bound, bound, start)
    return jnp.where((rows <= spot) & (rows >= start), scores, -1e30)


def chances(keys, query, bounds, seq, block):
    scores = lax.dot_general(keys, query, NT, preferred_element_type=F32)
    scores = masked(scores, bounds, seq, block)
    powers = jnp.exp(scores - jnp.max(scores, axis=0, keepdims=True))
    return powers * (1.0 / jnp.sum(powers, axis=0, keepdims=True))


def head_part(value, head):
    lane = lax.broadcasted_iota(jnp.int32, value.shape, 1)
    return jnp.where((lane < 64) == (head == 0), value, jnp.zeros_like(value))


def attend(queries, keys, values, bounds, seq, heads, store):
    queries = queries * 0.125
    value_t = turned(values).astype(BF16)
    for block in range(4):
        rows = slice(block * 256, block * 256 + 256)
        size = block * 256 + 256
        parts = []
        for head in range(heads):
            low = chances(keys[:size], head_part(queries[rows], head), bounds, seq, block).astype(BF16)
            parts.append(jnp.dot(value_t[:, :size], low, preferred_element_type=F32))
        whole = parts[0] if heads == 1 else jnp.concatenate([parts[0][:64], parts[1][64:]], axis=0)
        store(block, whole.T.astype(BF16).reshape(2, 128, 128))


def attend_kernel(pack, bounds, att, got, got8, out, out8, in_sems, in8_sems, back_sems, back8_sems):
    g = Group()
    greet([g.peer(g.other(step)) for step in range(1, 8)])

    def in_copy(step):
        return push(pack.at[g.other(step)], got.at[g.me], in_sems, (step - 1,), g.peer(g.other(step)))

    def in8_copy(extra, source):
        return pltpu.make_async_remote_copy(
            src_ref=pack.at[8, :, extra], dst_ref=got8.at[source], send_sem=in8_sems.at[8 + extra],
            recv_sem=in8_sems.at[source], device_id=g.peer(4 * extra), device_id_type=MESH)

    for step in (4, 3, 5, 2, 6, 1, 7):
        in_copy(step).start()
    for extra in (0, 1):
        @pl.when(g.me != 4 * extra)
        def _():
            in8_copy(extra, g.me).start()

        @pl.when(g.me == 4 * extra)
        def _():
            got8[g.me] = pack[8, :, extra]
    got[g.me] = pack[g.me]
    for step in range(1, 8):
        in_copy(step).wait_recv()

    def back_copy(seq, step):
        return push(out.at[g.other(step), seq], att.at[g.me, seq], back_sems, (seq, step - 1),
                    g.peer(g.other(step)))

    def pair(seq, carry):
        def store(block, value):
            out[pl.ds(2 * block, 2), seq] = value
        part = lambda kind: got[:, kind, seq].reshape(1024, 128)
        attend(part(0), part(1), part(2), bounds, seq, 2, store)
        for step in (4, 3, 5, 2, 6, 1, 7):
            back_copy(seq, step).start()
        return carry

    lax.fori_loop(0, 2, pair, 0)
    att[g.me] = out[g.me]

    def back8_copy(extra, step):
        return pltpu.make_async_remote_copy(
            src_ref=out8.at[g.other(step)], dst_ref=att.at[8, extra], send_sem=back8_sems.at[1 + step],
            recv_sem=back8_sems.at[extra], device_id=g.peer(g.other(step)), device_id_type=MESH)

    for extra in (0, 1):
        @pl.when(g.me == 4 * extra)
        def _():
            for step in range(1, 8):
                in8_copy(extra, g.other(step)).wait_recv()

            def store(block, value):
                out8[pl.ds(2 * block, 2)] = value
            part = lambda kind: got8[:, kind].reshape(1024, 128)
            attend(part(0), part(1), part(2), bounds, extra, 1, store)
            for step in range(1, 8):
                back8_copy(extra, step).start()
            att[8, extra] = out8[g.me]
            for step in range(1, 8):
                back8_copy(extra, step).wait_send()

        @pl.when(g.me != 4 * extra)
        def _():
            in8_copy(extra, g.me).wait_send()
            back8_copy(extra, 1).wait_recv()
    for step in range(1, 8):
        in_copy(step).wait_send()
        for seq in (0, 1):
            back_copy(seq, step).wait_recv()
            back_copy(seq, step).wait_send()


def attend_forward(pack, bounds):
    tile = (128, 128)
    vmem = pltpu.VMEM
    return pl.pallas_call(
        attend_kernel,
        out_shape=(jax.ShapeDtypeStruct((9, 2) + tile, BF16),
                   jax.ShapeDtypeStruct((8, 3, 2) + tile, BF16),
                   jax.ShapeDtypeStruct((8, 3) + tile, BF16)),
        in_specs=[pl.BlockSpec(memory_space=vmem), pl.BlockSpec(memory_space=pltpu.SMEM)],
        out_specs=(pl.BlockSpec(memory_space=vmem),) * 3,
        scratch_shapes=[
            vmem((8, 2) + tile, BF16), vmem((8,) + tile, BF16),
            pltpu.SemaphoreType.DMA((2, 7)), pltpu.SemaphoreType.DMA((10,)),
            pltpu.SemaphoreType.DMA((2, 2, 7)), pltpu.SemaphoreType.DMA((9,))],
        compiler_params=pltpu.CompilerParams(
            collective_id=1, has_side_effects=True, vmem_limit_bytes=40 * 2**20),
    )(pack, bounds)


def attend_pull(queries, keys, values, grads, bounds, seq, heads, key_sum, value_sum, store):
    queries = queries * 0.125
    key_t = turned(keys).astype(BF16)
    key_sum[...] = jnp.zeros_like(key_sum)
    value_sum[...] = jnp.zeros_like(value_sum)
    for block in range(4):
        rows = slice(block * 256, block * 256 + 256)
        size = block * 256 + 256
        parts = []
        for head in range(heads):
            query, grad = head_part(queries[rows], head), head_part(grads[rows], head)
            probs = chances(keys[:size], query, bounds, seq, block)
            change = lax.dot_general(values[:size], grad, NT, preferred_element_type=F32)
            inner = jnp.sum(probs * change, axis=0, keepdims=True)
            slope = (probs * (change - inner)).astype(BF16)
            value_sum[:size] += jnp.dot(probs.astype(BF16), grad, preferred_element_type=F32)
            key_sum[:size] += jnp.dot(slope, query, preferred_element_type=F32)
            parts.append(jnp.dot(key_t[:, :size], slope, preferred_element_type=F32))
        whole = parts[0] if heads == 1 else jnp.concatenate([parts[0][:64], parts[1][64:]], axis=0)
        store(0, block, (whole.T * 0.125).astype(BF16).reshape(2, 128, 128))
    for kind, total in ((1, key_sum), (2, value_sum)):
        for block in range(4):
            store(kind, block, total[block * 256 : block * 256 + 256].astype(BF16).reshape(2, 128, 128))


def pull_kernel(pack, got, got8, bounds, back, grad, grad8, out, out8, key_sum, value_sum,
                in_sems, in8_sems, back_sems, back8_sems):
    g = Group()
    greet([g.peer(g.other(step)) for step in range(1, 8)])

    def in_copy(step):
        return push(pack.at[g.other(step)], grad.at[g.me], in_sems, (step - 1,), g.peer(g.other(step)))

    def in8_copy(extra, source):
        return pltpu.make_async_remote_copy(
            src_ref=pack.at[8, extra], dst_ref=grad8.at[source], send_sem=in8_sems.at[8 + extra],
            recv_sem=in8_sems.at[source], device_id=g.peer(4 * extra), device_id_type=MESH)

    for step in (4, 3, 5, 2, 6, 1, 7):
        in_copy(step).start()
    for extra in (0, 1):
        @pl.when(g.me != 4 * extra)
        def _():
            in8_copy(extra, g.me).start()

        @pl.when(g.me == 4 * extra)
        def _():
            grad8[g.me] = pack[8, extra]
    grad[g.me] = pack[g.me]
    for step in range(1, 8):
        in_copy(step).wait_recv()

    def back_copy(seq, step):
        return push(out.at[g.other(step), seq], back.at[g.me, seq], back_sems, (seq, step - 1),
                    g.peer(g.other(step)))

    def pair(seq, carry):
        def store(kind, block, value):
            out[pl.ds(2 * block, 2), seq, kind] = value
        part = lambda kind: got[:, kind, seq].reshape(1024, 128)
        attend_pull(part(0), part(1), part(2), grad[:, seq].reshape(1024, 128), bounds, seq, 2,
                    key_sum, value_sum, store)
        for step in (4, 3, 5, 2, 6, 1, 7):
            back_copy(seq, step).start()
        return carry

    lax.fori_loop(0, 2, pair, 0)
    back[g.me] = out[g.me]

    def back8_copy(extra, step):
        return pltpu.make_async_remote_copy(
            src_ref=out8.at[g.other(step)], dst_ref=back.at[8, extra], send_sem=back8_sems.at[1 + step],
            recv_sem=back8_sems.at[extra], device_id=g.peer(g.other(step)), device_id_type=MESH)

    for extra in (0, 1):
        @pl.when(g.me == 4 * extra)
        def _():
            for step in range(1, 8):
                in8_copy(extra, g.other(step)).wait_recv()

            def store(kind, block, value):
                out8[pl.ds(2 * block, 2), kind] = value
            part = lambda kind: got8[:, kind].reshape(1024, 128)
            attend_pull(part(0), part(1), part(2), grad8[...].reshape(1024, 128), bounds, extra, 1,
                        key_sum, value_sum, store)
            for step in range(1, 8):
                back8_copy(extra, step).start()
            back[8, extra] = out8[g.me]
            for step in range(1, 8):
                back8_copy(extra, step).wait_send()

        @pl.when(g.me != 4 * extra)
        def _():
            in8_copy(extra, g.me).wait_send()
            back8_copy(extra, 1).wait_recv()
    for step in range(1, 8):
        in_copy(step).wait_send()
        for seq in (0, 1):
            back_copy(seq, step).wait_recv()
            back_copy(seq, step).wait_send()


def attend_backward(pack, got, got8, bounds):
    tile = (128, 128)
    vmem = pltpu.VMEM
    return pl.pallas_call(
        pull_kernel,
        out_shape=jax.ShapeDtypeStruct((9, 2, 3) + tile, BF16),
        in_specs=[pl.BlockSpec(memory_space=vmem)] * 3 + [pl.BlockSpec(memory_space=pltpu.SMEM)],
        out_specs=pl.BlockSpec(memory_space=vmem),
        scratch_shapes=[
            vmem((8, 2) + tile, BF16), vmem((8,) + tile, BF16),
            vmem((8, 2, 3) + tile, BF16), vmem((8, 3) + tile, BF16),
            vmem((1024, 128), F32), vmem((1024, 128), F32),
            pltpu.SemaphoreType.DMA((2, 7)), pltpu.SemaphoreType.DMA((10,)),
            pltpu.SemaphoreType.DMA((2, 2, 7)), pltpu.SemaphoreType.DMA((9,))],
        compiler_params=pltpu.CompilerParams(
            collective_id=2, has_side_effects=True, vmem_limit_bytes=50 * 2**20),
    )(pack, got, got8, bounds)


def reduce_kernel(xt, yb, tt, act, extra, out_a, out_b,
                  sib_out1, sib_out2, sib_in1, sib_in2,
                  in_opp1, in_opp2, in_side1, in_side2,
                  acc1, acc2, end1, end2, in_end1, in_end2, in_mid1, in_mid2,
                  zout_a, zout_b, zin_a, zin_b,
                  sib_sems, opp_sems, side_sems, mid_sems, end_sems, z_sems):
    me = Place()
    greet(all_peers(me))

    def part1(xb, yy, parity):
        column = 2 * xb + parity
        rows = pl.ds(pl.multiple_of(yy * A_ROWS, 16), CUT)
        return outer(column, rows)

    def outer(column, rows):
        one = jnp.dot(xt[0, rows], yb[column, :, 0:512], preferred_element_type=F32)
        two = jnp.dot(xt[1, rows], yb[column, :, 384:640], preferred_element_type=F32)
        three = jnp.dot(xt[2, rows], yb[column, :, 512:], preferred_element_type=F32)
        lane = lax.broadcasted_iota(jnp.int32, (one.shape[0], 128), 1)
        return jnp.concatenate([
            one[:, :384],
            jnp.where(lane < 24, one[:, 384:512], two[:, :128]),
            jnp.where(lane < 32, two[:, 128:], three[:, :128]),
            three[:, 128:]], axis=1)

    def part2(xb, yy, parity):
        column = 2 * xb + parity
        rows = pl.ds(pl.multiple_of(yy * A_ROWS + CUT, 16), A_ROWS - CUT)
        lower = jnp.dot(tt[column], act[yy], preferred_element_type=F32)
        lower = jnp.concatenate([lower[:136], extra[column]], axis=0)
        return jnp.concatenate([outer(column, rows), lower], axis=0)

    def turn(value, by):
        return (value + by) % 4

    def copy(source, target, sems, index, peer):
        return pltpu.make_async_remote_copy(
            src_ref=source, dst_ref=target, send_sem=sems.at[(0,) + index],
            recv_sem=sems.at[(1,) + index], device_id=peer, device_id_type=MESH)

    blocks = {
        0: dict(part=lambda step, o, par: part1(turn(me.x, step), turn(me.y, o), par),
                axes=("x", "y"), cut=96, sib_out=sib_out1, sib_in=sib_in1, in_opp=in_opp1,
                in_side=in_side1, acc=acc1, end=end1, in_end=in_end1, in_mid=in_mid1),
        1: dict(part=lambda step, o, par: part2(turn(me.x, o), turn(me.y, step), par),
                axes=("y", "x"), cut=64, sib_out=sib_out2, sib_in=sib_in2, in_opp=in_opp2,
                in_side=in_side2, acc=acc2, end=end2, in_end=in_end2, in_mid=in_mid2),
    }

    def sib_copy(half, step, o):
        b = blocks[half]
        return copy(b["sib_out"].at[o], b["sib_in"].at[step, o], sib_sems, (half, step, o), me.sibling)

    def cross(step, before):
        def body(o, carry):
            for half in (0, 1):
                b = blocks[half]
                if before is not None:
                    sib_copy(half, before, o).wait_send()
                b["sib_out"][o] = b["part"](step, o, 1 - me.c).astype(BF16)
                sib_copy(half, step, o).start()
            return carry
        lax.fori_loop(0, 4, body, 0)

    def mine(half, step, o):
        b = blocks[half]
        value = b["part"](step, o, me.c)
        sib_copy(half, step, o).wait_recv()
        return value + b["sib_in"][step, o].astype(F32)

    def ends_of(half, which):
        b = blocks[half]
        total = CUT
        return pl.ds(0, b["cut"]) if which == 0 else pl.ds(b["cut"], total - b["cut"])

    def opp_copy(half, o, which):
        b = blocks[half]
        rows = ends_of(half, which)
        return copy(b["sib_in"].at[2, o, rows], b["in_opp"].at[o, rows], opp_sems, (half, o, which),
                    me.peer(b["axes"][0], 1 if which == 0 else 3))

    def side_copy(half, o, which):
        b = blocks[half]
        return copy(b["sib_in"].at[1 + 2 * which, o], b["in_side"].at[which, o], side_sems, (half, o, which),
                    me.peer(b["axes"][0], 1 if which == 0 else 3))

    def mid_copy(half, which):
        b = blocks[half]
        rows = ends_of(half, which)
        return copy(b["end"].at[2, rows], b["in_mid"].at[rows], mid_sems, (half, which),
                    me.peer(b["axes"][1], 1 if which == 0 else 3))

    def end_copy(half, which):
        b = blocks[half]
        return copy(b["end"].at[which], b["in_end"].at[which], end_sems, (half, which),
                    me.peer(b["axes"][1], 1 if which == 0 else 3))

    def loop(body):
        lax.fori_loop(0, 4, lambda o, carry: (body(o), carry)[1], 0)

    def opposite(o):
        for half in (0, 1):
            blocks[half]["sib_in"][2, o] = mine(half, 2, o).astype(BF16)
            for which in (0, 1):
                opp_copy(half, o, which).start()

    def sides(o):
        for half in (0, 1):
            b = blocks[half]
            cut = b["cut"]
            for which in (0, 1):
                value = mine(half, 1 if which == 0 else 3, o)
                opp_copy(half, o, which).wait_recv()
                if which == 0:
                    value = jnp.concatenate(
                        [value[:cut] + b["in_opp"][o, :cut].astype(F32), value[cut:]], axis=0)
                else:
                    value = jnp.concatenate(
                        [value[:cut], value[cut:] + b["in_opp"][o, cut:].astype(F32)], axis=0)
                b["sib_in"][1 + 2 * which, o] = value.astype(BF16)
                side_copy(half, o, which).start()

    def own(o):
        for half in (0, 1):
            b = blocks[half]
            value = mine(half, 0, o)
            for which in (0, 1):
                side_copy(half, o, which).wait_recv()
                value = value + b["in_side"][which, o].astype(F32)
            b["acc"][o] = value

    cross(2, None)
    loop(opposite)
    cross(1, 2)
    cross(3, 1)
    loop(sides)
    cross(0, 3)
    loop(own)
    for half in (0, 1):
        b = blocks[half]
        b["end"][2] = b["acc"][2].astype(BF16)
        for which in (0, 1):
            mid_copy(half, which).start()
    for half in (0, 1):
        b = blocks[half]
        cut = b["cut"]
        for which in (0, 1):
            value = b["acc"][1 if which == 0 else 3]
            mid_copy(half, which).wait_recv()
            if which == 0:
                value = jnp.concatenate([value[:cut] + b["in_mid"][:cut].astype(F32), value[cut:]], axis=0)
            else:
                value = jnp.concatenate([value[:cut], value[cut:] + b["in_mid"][cut:].astype(F32)], axis=0)
            b["end"][which] = value.astype(BF16)
            end_copy(half, which).start()
    final = []
    for half in (0, 1):
        b = blocks[half]
        value = b["acc"][0]
        for which in (0, 1):
            end_copy(half, which).wait_recv()
            value = value + b["in_end"][which].astype(F32)
        final.append(value.astype(BF16))
    block_a = jnp.concatenate([final[0], final[1][:64]], axis=0)
    block_b = final[1][64:]

    def slices(z):
        row = lax.broadcasted_iota(jnp.int32, (80, A_ROWS), 0)
        col = lax.broadcasted_iota(jnp.int32, (80, A_ROWS), 1)
        pick = jnp.where((col == row + 68 * z) & (row < 68), 1.0, 0.0).astype(BF16)
        row = lax.broadcasted_iota(jnp.int32, (D, 384), 0)
        col = lax.broadcasted_iota(jnp.int32, (D, 384), 1)
        pick_b = jnp.where((row == col + 272 * z) & (col < 272), 1.0, 0.0).astype(BF16)
        lower = jnp.dot(block_b, pick_b, preferred_element_type=F32)
        row = lax.broadcasted_iota(jnp.int32, (B_ROWS, 384), 0)
        lower = jnp.where(row < 136, lower, block_b[:, :384].astype(F32))
        return jnp.dot(pick, block_a, preferred_element_type=F32), lower

    def z_copies(step):
        peer = me.peer("z", step)
        return (copy(zout_a.at[step - 1], zin_a.at[step - 1], z_sems, (0, step - 1), peer),
                copy(zout_b.at[step - 1], zin_b.at[step - 1], z_sems, (1, step - 1), peer))

    for step in (2, 1, 3):
        upper, lower = slices(turn(me.z, step))
        zout_a[step - 1] = upper.astype(BF16)
        zout_b[step - 1] = lower.astype(BF16)
        for c in z_copies(step):
            c.start()
    upper, lower = slices(me.z)
    for step in (1, 2, 3):
        for c in z_copies(step):
            c.wait_recv()
        upper = upper + zin_a[step - 1].astype(F32)
        lower = lower + zin_b[step - 1].astype(F32)
    out_a[...] = upper
    out_b[...] = lower

    def drain(o):
        for half in (0, 1):
            sib_copy(half, 0, o).wait_send()
            for which in (0, 1):
                opp_copy(half, o, which).wait_send()
                side_copy(half, o, which).wait_send()

    loop(drain)
    for half in (0, 1):
        for which in (0, 1):
            mid_copy(half, which).wait_send()
            end_copy(half, which).wait_send()
    for step in (1, 2, 3):
        for c in z_copies(step):
            c.wait_send()


def reduce_weights(xt, yb, tt, act, extra):
    half = (CUT, D)
    vmem = pltpu.VMEM
    pair = lambda *lead: [vmem(lead + half, BF16), vmem(lead + half, BF16)]
    return pl.pallas_call(
        reduce_kernel,
        out_shape=(jax.ShapeDtypeStruct((80, D), F32), jax.ShapeDtypeStruct((B_ROWS, 384), F32)),
        in_specs=[pl.BlockSpec(memory_space=vmem)] * 5,
        out_specs=(pl.BlockSpec(memory_space=vmem),) * 2,
        scratch_shapes=(
            pair(4) + pair(4, 4) + pair(4) + pair(2, 4)
            + [vmem((4,) + half, F32)] * 2 + pair(3) + pair(2) + pair()
            + [vmem((3, 80, D), BF16), vmem((3, B_ROWS, 384), BF16)] * 2
            + [pltpu.SemaphoreType.DMA((2, 2, 4, 4)), pltpu.SemaphoreType.DMA((2, 2, 4, 2)),
               pltpu.SemaphoreType.DMA((2, 2, 4, 2)), pltpu.SemaphoreType.DMA((2, 2, 2)),
               pltpu.SemaphoreType.DMA((2, 2, 2)), pltpu.SemaphoreType.DMA((2, 2, 3))]),
        compiler_params=pltpu.CompilerParams(
            collective_id=3, has_side_effects=True, vmem_limit_bytes=63 * 2**20),
    )(xt, yb, tt, act, extra)


HEADS = 17
FF = 4352


def normalize(values):
    center = values - jnp.mean(values, axis=-1, keepdims=True)
    spread = jnp.mean(center * center, axis=-1, keepdims=True)
    scale = lax.rsqrt(spread + 1e-05)
    return center * scale, scale


def norm_pull(grad, gain, unit, scale):
    scaled = grad * gain
    return scale * (
        scaled
        - jnp.mean(scaled, axis=-1, keepdims=True)
        - unit * jnp.mean(scaled * unit, axis=-1, keepdims=True)
    )


def gelu_tanh(values):
    return jax.nn.gelu(values, approximate=True)


def dot(left, right):
    return jnp.dot(left, right, preferred_element_type=F32)


def pairs_out(rows):
    rows = jnp.pad(rows, [(0, 0)] * (rows.ndim - 1) + [(0, 64)])
    return jnp.moveaxis(rows.reshape(rows.shape[:-1] + (9, 128)), -2, 0)


def pairs_in(packed):
    rows = jnp.moveaxis(packed, 0, -2)
    return rows.reshape(rows.shape[:-2] + (1152,))[..., :D]


def per_device(
    inputs, out_grad, segment_ids, qkv_weight, out_weight, up_weight, down_weight,
    norm_gains, norm_shifts, qv_bias, proj_bias, up_bias,
):
    seqs, rows, _ = inputs.shape
    tokens = seqs * rows
    batch = lax.axis_index("batch")

    blob_a = jnp.concatenate([qkv_weight, out_weight, up_weight], axis=1)
    blob_a = jnp.pad(blob_a, ((0, 12), (0, 0)))
    counts = jnp.sum(segment_ids[:, :, None] < jnp.arange(1, 4)[None, None, :], axis=1)
    counts = jnp.pad(counts.astype(BF16).reshape(1, 6), ((0, 3), (0, 130)))
    vec = jnp.concatenate([norm_gains, norm_shifts, qv_bias, proj_bias], axis=0)
    vec = jnp.concatenate(
        [vec, jnp.concatenate([up_bias.reshape(4, 136), counts], axis=0)], axis=1
    )
    blob_b = jnp.concatenate([down_weight.T, vec], axis=0)
    blob_b = jnp.pad(blob_b, ((0, 0), (0, 112)))
    whole_a, whole_b = gather_weights(blob_a, blob_b)
    vec = lax.dynamic_slice(whole_b, (batch // 4, 0, 136, 272 * (batch % 4)), (1, 8, 8, 272))
    vec = vec[0].astype(F32)
    lines = vec[:, :, :136].transpose(1, 0, 2).reshape(8, D)
    gains, shifts, qv_rows, proj_rows = lines[0:2], lines[2:4], lines[4:6], lines[6:8]
    up_row = vec[:, :4, 136:].reshape(FF)
    bounds = jnp.sum(vec[:, 4, 136:142], axis=0).astype(jnp.int32).reshape(2, 3)
    w_qkv, w_out, w_up = whole_a[:, :, :408], whole_a[:, :, 408:544], whole_a[:, :, 544:]

    hidden = inputs.reshape(tokens, D).astype(F32)
    top_grad = out_grad.reshape(tokens, D)
    cotangent = top_grad.astype(F32)
    unit_one, scale_one = normalize(hidden)
    normed = (unit_one * gains[0] + shifts[0]).astype(BF16)
    projected = jnp.einsum("tk,skn->tsn", normed, w_qkv, preferred_element_type=F32).reshape(
        tokens, 3, D
    )
    shift = jnp.stack([qv_rows[0], jnp.zeros((D,), F32), qv_rows[1]])
    projected = (projected + shift).astype(BF16).reshape(seqs, rows, 3, D).transpose(2, 0, 1, 3)
    att, got, got8 = attend_forward(pairs_out(projected), bounds)
    attended = pairs_in(att).reshape(tokens, D)
    branch = jnp.einsum("tk,skn->tsn", attended, w_out, preferred_element_type=F32)
    middle = hidden + branch.reshape(tokens, D) + proj_rows[0]
    unit_two, scale_two = normalize(middle)
    normed_two = (unit_two * gains[1] + shifts[1]).astype(BF16)
    inner_pre = (
        jnp.einsum("tk,skn->tsn", normed_two, w_up, preferred_element_type=F32).reshape(tokens, FF)
        + up_row
    )
    active, gelu_pull = jax.vjp(gelu_tanh, inner_pre)
    active = active.astype(BF16).reshape(tokens, 4, D).transpose(1, 0, 2)
    downs = whole_b.reshape(4, 8 * B_ROWS, D)
    branch = sum(
        lax.dot_general(active[y], downs[y], (((1,), (1,)), ((), ())), preferred_element_type=F32)
        for y in range(4)
    )
    branch = branch.reshape(tokens, 8, B_ROWS)[:, :, :136].reshape(tokens, D)
    layer_out = (middle + branch + proj_rows[1]).astype(BF16)

    top_blocks = jnp.pad(top_grad.reshape(tokens, 8, 136), ((0, 0), (0, 0), (0, 8)))
    top_pad = top_blocks.reshape(tokens, 8 * B_ROWS)
    down_in = jnp.concatenate([dot(top_pad, downs[y]) for y in range(4)], axis=1)
    inner_grad = gelu_pull(down_in)[0].astype(BF16)
    inner_blocks = inner_grad.reshape(tokens, 8, 544)
    normed_two_grad = jnp.einsum("tsn,skn->tk", inner_blocks, w_up, preferred_element_type=F32)
    middle_grad = cotangent + norm_pull(normed_two_grad, gains[1], unit_two, scale_two)
    branch_grad = middle_grad.astype(BF16)
    branch_blocks = branch_grad.reshape(tokens, 8, 136)
    attended_grad = jnp.einsum(
        "tsn,skn->tk", branch_blocks, w_out, preferred_element_type=F32
    ).astype(BF16)
    back = attend_backward(
        pairs_out(attended_grad.reshape(seqs, rows, D)), got, got8, bounds
    )
    qkv_grad = pairs_in(back).transpose(0, 2, 1, 3).reshape(tokens, 3 * D)
    qkv_blocks = qkv_grad.reshape(tokens, 8, 408)
    normed_grad = jnp.einsum("tsn,skn->tk", qkv_blocks, w_qkv, preferred_element_type=F32)
    input_grad = middle_grad + norm_pull(normed_grad, gains[0], unit_one, scale_one)

    def column_sum(values):
        return jnp.sum(values, axis=0, dtype=F32)

    sums = jnp.stack(
        [
            column_sum(normed_grad * unit_one),
            column_sum(normed_two_grad * unit_two),
            column_sum(normed_grad),
            column_sum(normed_two_grad),
            column_sum(qkv_grad[:, :D]),
            column_sum(qkv_grad[:, 2 * D :]),
            column_sum(branch_grad),
            column_sum(top_grad),
        ]
    ).reshape(8, 8, 136)
    up_sums = jnp.pad(column_sum(inner_grad).reshape(8, 4, 136), ((0, 0), (0, 4), (0, 0)))
    extra = jnp.concatenate([sums.transpose(1, 0, 2), up_sums], axis=2)
    extra = jnp.pad(extra, ((0, 0), (0, 0), (0, D - 272)))
    left = jnp.stack([normed.T, attended.T, normed_two.T])
    right = jnp.concatenate([qkv_blocks, branch_blocks, inner_blocks], axis=2).transpose(1, 0, 2)
    out_a, out_b = reduce_weights(left, right, top_blocks.transpose(1, 2, 0), active, extra)
    return (
        layer_out.reshape(seqs, rows, D),
        input_grad.reshape(seqs, rows, D),
        out_a[:68, :408],
        out_a[:68, 408:544],
        out_a[:68, 544:],
        out_b[:136, :272].T,
        out_b[136:138, :136],
        out_b[138:140, :136],
        out_b[140:142, :136],
        out_b[142:144, :136],
        out_b[136:140, 136:272].reshape(1, 544),
    )


def solution(mesh):
    tokens = P("batch", "seq", None)
    matrix = P("batch", "seq")
    vector = P(None, "seq")
    return jax.shard_map(
        per_device,
        mesh=mesh,
        in_specs=(tokens, tokens, matrix, matrix, matrix, matrix, matrix) + (vector,) * 5,
        out_specs=(tokens, tokens, matrix, matrix, matrix, matrix) + (vector,) * 5,
        check_vma=False,
    )
```

```python
import jax
import jax.numpy as jnp
from jax import lax
from jax.experimental import pallas as pl
from jax.experimental.pallas import tpu as pltpu
from jax.sharding import PartitionSpec as P

D = 1088
WIDE = 1152
F32 = jnp.float32
BF16 = jnp.bfloat16
MESH = pl.DeviceIdType.MESH
A_ROWS, B_ROWS = 272, 144
CUT = 208


class Place:
    def __init__(self):
        batch, seq = lax.axis_index("batch"), lax.axis_index("seq")
        self.y, self.z = batch // 4, batch % 4
        self.x, self.c = seq // 2, seq % 2
        self.sibling = {"batch": batch, "seq": self.x * 2 + 1 - self.c}

    def peer(self, axis, step):
        spot = {"x": self.x, "y": self.y, "z": self.z}
        spot[axis] = (spot[axis] + step + 4) % 4
        return {"batch": spot["y"] * 4 + spot["z"], "seq": spot["x"] * 2 + self.c}


def greet(peers):
    barrier = pltpu.get_barrier_semaphore()
    for peer in peers:
        pl.semaphore_signal(barrier, inc=1, device_id=peer, device_id_type=MESH)
    pl.semaphore_wait(barrier, len(peers))


def all_peers(me):
    return [me.sibling] + [me.peer(axis, step) for axis, step in (
        ("x", 1), ("x", 3), ("y", 1), ("y", 3), ("z", 1), ("z", 2), ("z", 3))]


class Sender:
    def __init__(self, send_sems, recv_sems):
        self.send_sems, self.recv_sems, self.made = send_sems, recv_sems, []

    def __call__(self, source, target, peer):
        index = len(self.made)
        copy = pltpu.make_async_remote_copy(
            src_ref=source, dst_ref=target, send_sem=self.send_sems.at[index],
            recv_sem=self.recv_sems.at[index], device_id=peer, device_id_type=MESH)
        copy.start()
        self.made.append(copy)
        return copy


def merge_rows(stacked):
    row = lax.broadcasted_iota(jnp.int32, (A_ROWS, 320), 0)
    col = lax.broadcasted_iota(jnp.int32, (A_ROWS, 320), 1)
    pick = jnp.where(col == row + 12 * (row // 68), 1.0, 0.0).astype(BF16)
    return jnp.dot(pick, stacked, preferred_element_type=F32).astype(BF16)


def merge_columns(slots):
    total = None
    for z in range(4):
        row = lax.broadcasted_iota(jnp.int32, (384, D), 0)
        col = lax.broadcasted_iota(jnp.int32, (384, D), 1)
        pick = jnp.where((col == row + 272 * z) & (row < 272), 1.0, 0.0).astype(BF16)
        term = jnp.dot(slots[z], pick, preferred_element_type=F32)
        total = term if total is None else total + term
    return total.astype(BF16)


GATHER_COPIES = 120


def gather_kernel(a_ref, b_ref, ga, gb, za, zb, mine_a, mine_b, send_sems, recv_sems, local_sems):
    me = Place()
    greet(all_peers(me))
    send = Sender(send_sems, recv_sems)
    first = []
    for step in (1, 2, 3):
        peer = me.peer("z", step)
        first.append(send(a_ref, za.at[me.z], peer))
        first.append(send(b_ref, zb.at[me.z], peer))
    za[me.z] = a_ref[...]
    zb[me.z] = b_ref[...]
    for copy in first:
        copy.wait_recv()
    mine_a[...] = merge_rows(za[...].reshape(320, WIDE))
    mine_b[...] = merge_columns(zb)

    def spot(part, step_x, step_y):
        x, y = (me.x + step_x) % 4, (me.y + step_y) % 4
        if part == "b":
            return gb.at[y, 2 * x + me.c]
        low, rows = part
        return ga.at[2 * x + me.c, pl.ds(pl.multiple_of(y * A_ROWS + low, 16), rows)]

    own = [pltpu.make_async_copy(mine_a, spot((0, A_ROWS), 0, 0), local_sems.at[0]),
           pltpu.make_async_copy(mine_b, spot("b", 0, 0), local_sems.at[1])]
    for copy in own:
        copy.start()
    whole = {0: [(0, CUT)], 1: [(CUT, A_ROWS - CUT), "b"]}
    split = {0: [(0, 96), (96, CUT - 96)], 1: [(CUT, A_ROWS - CUT), "b"]}

    def source(part, steps):
        if steps != (0, 0):
            return spot(part, *steps)
        if part == "b":
            return mine_b
        return mine_a.at[pl.ds(part[0], part[1])]

    def move(axis, steps, by):
        return ((steps[0] + by) % 4, steps[1]) if axis == "x" else (steps[0], (steps[1] + by) % 4)

    crossed = []

    def to_sibling(part, steps):
        crossed.append(send(source(part, steps), spot(part, *steps), me.sibling))

    def begin(half, axis, steps):
        return {by: [send(source(part, steps), spot(part, *steps), me.peer(axis, by))
                     for part in whole[half]] for by in (1, 3)}

    def forward(half, axis, steps, sent, flip):
        ends = []
        for by, which in ((1, flip), (3, 1 - flip)):
            origin = move(axis, steps, -by)
            for copy in sent[by]:
                copy.wait_recv()
            part = split[half][which]
            ends.append((send(spot(part, *origin), spot(part, *origin), me.peer(axis, by)), part))
        return ends

    def arrived(half, axis, steps):
        for by in (1, 3):
            for part in whole[half]:
                to_sibling(part, move(axis, steps, by))

    def finish(half, axis, steps, ends):
        for copy, part in ends:
            copy.wait_recv()
        for part in whole[half]:
            to_sibling(part, move(axis, steps, 2))

    axes = {0: ("x", "y"), 1: ("y", "x")}
    first = {half: begin(half, axes[half][0], (0, 0)) for half in (0, 1)}
    second = {(half, 0): begin(half, axes[half][1], (0, 0)) for half in (0, 1)}
    to_sibling((0, A_ROWS), (0, 0))
    to_sibling("b", (0, 0))
    ends = {}
    for half in (0, 1):
        axis = axes[half][0]
        ends[half] = forward(half, axis, (0, 0), first[half], half)
        for by in (1, 3):
            second[half, by] = begin(half, axes[half][1], move(axis, (0, 0), by))
    for half in (0, 1):
        arrived(half, axes[half][0], (0, 0))
    tails = {}
    for half in (0, 1):
        tails[half, 0] = forward(half, axes[half][1], (0, 0), second[half, 0], 0)
        arrived(half, axes[half][1], (0, 0))
    for half in (0, 1):
        axis = axes[half][0]
        finish(half, axis, (0, 0), ends[half])
        second[half, 2] = begin(half, axes[half][1], move(axis, (0, 0), 2))
    order = [(half, by) for by in (1, 3, 2) for half in (0, 1)]
    done = [(half, 0) for half in (0, 1)]
    for half, by in order:
        steps = move(axes[half][0], (0, 0), by)
        tails[half, by] = forward(half, axes[half][1], steps, second[half, by], by % 2)
        arrived(half, axes[half][1], steps)
        if done:
            late, late_by = done.pop(0)
            finish(late, axes[late][1], move(axes[late][0], (0, 0), late_by), tails[late, late_by])
        done.append((half, by))
    for late, late_by in done:
        finish(late, axes[late][1], move(axes[late][0], (0, 0), late_by), tails[late, late_by])
    for copy in crossed:
        copy.wait_recv()
    for copy in send.made:
        copy.wait_send()
    for copy in own:
        copy.wait()


def gather_weights(blob_a, blob_b):
    return pl.pallas_call(
        gather_kernel,
        out_shape=(jax.ShapeDtypeStruct((8, D, WIDE), BF16),
                   jax.ShapeDtypeStruct((4, 8, B_ROWS, D), BF16)),
        in_specs=[pl.BlockSpec(memory_space=pltpu.VMEM)] * 2,
        out_specs=(pl.BlockSpec(memory_space=pl.ANY),) * 2,
        scratch_shapes=[
            pltpu.VMEM((4, 80, WIDE), BF16), pltpu.VMEM((4, B_ROWS, 384), BF16),
            pltpu.VMEM((A_ROWS, WIDE), BF16), pltpu.VMEM((B_ROWS, D), BF16),
            pltpu.SemaphoreType.DMA((GATHER_COPIES,)), pltpu.SemaphoreType.DMA((GATHER_COPIES,)),
            pltpu.SemaphoreType.DMA((2,)),
        ],
        compiler_params=pltpu.CompilerParams(
            collective_id=0, has_side_effects=True, vmem_limit_bytes=40 * 2**20),
    )(blob_a, blob_b)


NT = (((1,), (1,)), ((), ()))


def normalize(values):
    center = values - jnp.mean(values, axis=-1, keepdims=True)
    spread = jnp.mean(center * center, axis=-1, keepdims=True)
    scale = lax.rsqrt(spread + 1e-05)
    return center * scale, scale


def norm_pull(grad, gain, unit, scale):
    scaled = grad * gain
    return scale * (
        scaled
        - jnp.mean(scaled, axis=-1, keepdims=True)
        - unit * jnp.mean(scaled * unit, axis=-1, keepdims=True)
    )


def dot(left, right):
    return jnp.dot(left, right, preferred_element_type=F32)


def dot_t(left, right):
    return lax.dot_general(left, right, NT, preferred_element_type=F32)


def widen(value):
    return jnp.concatenate([value, jnp.zeros((value.shape[0], WIDE - D), value.dtype)], axis=1)


def shift_lanes(tiles, value, source, width, target):
    turn = (target - source) % 128
    low, high = source // 128, -(-(source + width) // 128)
    part = value[:, low * 128 : high * 128]
    if turn:
        part = jnp.concatenate([part, jnp.zeros((part.shape[0], 128), part.dtype)], axis=1)
        part = pltpu.roll(part, turn, 1)
    start = source - low * 128 + turn
    for spot in range(start // 128, -(-(start + width) // 128)):
        tile = part[:, spot * 128 : spot * 128 + 128]
        first, last = start - spot * 128, start + width - spot * 128
        if first > 0 or last < 128:
            lane = lax.broadcasted_iota(jnp.int32, tile.shape, 1)
            tile = jnp.where((lane >= first) & (lane < last), tile, 0.0)
        place = (target - start) // 128 + spot
        tiles[place] = tiles[place] + tile if place in tiles else tile


def join_tiles(tiles, count):
    rows = tiles[0].shape[0]
    empty = jnp.zeros((rows, 128), F32)
    return jnp.concatenate([tiles.get(k, empty) for k in range(count)], axis=1)


def segments():
    found = []
    for s in range(8):
        for kind in range(3):
            low, high = max(408 * s, D * kind), min(408 * s + 408, D * kind + D)
            if low < high:
                found.append((s, low - 408 * s, high - low, kind, low - D * kind))
    return found


class Group:
    def __init__(self):
        self.batch, self.me = lax.axis_index("batch"), lax.axis_index("seq")

    def peer(self, seq):
        return {"batch": self.batch, "seq": seq}

    def other(self, step):
        return (self.me + step) % 8


def push(source, target, sems, index, peer):
    return pltpu.make_async_remote_copy(
        src_ref=source, dst_ref=target, send_sem=sems.at[(0,) + index],
        recv_sem=sems.at[(1,) + index], device_id=peer, device_id_type=MESH)


def turned(value):
    return value.astype(F32).T


def masked(scores, bounds, seq, block):
    rows = lax.broadcasted_iota(jnp.int32, scores.shape, 0)
    spot = block * 256 + lax.broadcasted_iota(jnp.int32, (1, 256), 1)
    start = jnp.zeros((1, 256), jnp.int32)
    for n in range(3):
        bound = bounds[seq, n]
        start = jnp.where(spot >= bound, bound, start)
    return jnp.where((rows <= spot) & (rows >= start), scores, -1e30)


def chances(keys, query, bounds, seq, block):
    scores = lax.dot_general(keys, query, NT, preferred_element_type=F32)
    scores = masked(scores, bounds, seq, block)
    powers = jnp.exp(scores - jnp.max(scores, axis=0, keepdims=True))
    return powers * (1.0 / jnp.sum(powers, axis=0, keepdims=True))


def head_part(value, head):
    lane = lax.broadcasted_iota(jnp.int32, value.shape, 1)
    return jnp.where((lane < 64) == (head == 0), value, jnp.zeros_like(value))


def attend(queries, keys, values, bounds, seq, heads, store):
    queries = queries * 0.125
    value_t = turned(values).astype(BF16)
    for block in range(4):
        rows = slice(block * 256, block * 256 + 256)
        size = block * 256 + 256
        parts = []
        for head in range(heads):
            low = chances(keys[:size], head_part(queries[rows], head), bounds, seq, block).astype(BF16)
            parts.append(jnp.dot(value_t[:, :size], low, preferred_element_type=F32))
        whole = parts[0] if heads == 1 else jnp.concatenate([parts[0][:64], parts[1][64:]], axis=0)
        store(block, whole.T.astype(BF16).reshape(2, 128, 128))


def fetch_blocks(ga, held, sems, low, width):
    copies = [pltpu.make_async_copy(ga.at[s, :, pl.ds(low, width)], held.at[s], sems.at[s])
              for s in range(8)]
    for copy in copies:
        copy.start()
    return copies


def attend_kernel(hidden, lines, ga, bounds, att, got, got8, normed_t, weights, pack, out, out8,
                  weight_sems, in_sems, in8_sems, back_sems, back8_sems):
    g = Group()
    copies = fetch_blocks(ga, weights, weight_sems, 0, 512)
    unit, _ = normalize(hidden[...].astype(F32).reshape(256, D))
    normed = unit * lines[0:1, :D] + lines[2:3, :D]
    normed_t[...] = normed.T.astype(BF16)
    normed = normed.astype(BF16)
    tiles = ({}, {}, {})
    blocks = []
    for s in range(8):
        copies[s].wait()
        blocks.append(dot(normed, weights[s]))
        for seg, low, width, kind, spot in segments():
            if seg == s:
                shift_lanes(tiles[kind], blocks[s], low, width, spot)
    for kind, row in ((0, 4), (1, None), (2, 5)):
        for p in range(9):
            tile = tiles[kind][p]
            if row is not None:
                tile = tile + lines[row : row + 1, 128 * p : 128 * p + 128]
            pack[p, kind] = tile.astype(BF16).reshape(2, 128, 128)
    greet([g.peer(g.other(step)) for step in range(1, 8)])

    def in_copy(step):
        return push(pack.at[g.other(step)], got.at[g.me], in_sems, (step - 1,), g.peer(g.other(step)))

    def in8_copy(extra, source):
        return pltpu.make_async_remote_copy(
            src_ref=pack.at[8, :, extra], dst_ref=got8.at[source], send_sem=in8_sems.at[8 + extra],
            recv_sem=in8_sems.at[source], device_id=g.peer(4 * extra), device_id_type=MESH)

    for step in (4, 3, 5, 2, 6, 1, 7):
        in_copy(step).start()
    for extra in (0, 1):
        @pl.when(g.me != 4 * extra)
        def _():
            in8_copy(extra, g.me).start()

        @pl.when(g.me == 4 * extra)
        def _():
            got8[g.me] = pack[8, :, extra]
    got[g.me] = pack[g.me]
    for step in range(1, 8):
        in_copy(step).wait_recv()

    def back_copy(seq, step):
        return push(out.at[g.other(step), seq], att.at[g.me, seq], back_sems, (seq, step - 1),
                    g.peer(g.other(step)))

    def pair(seq, carry):
        def store(block, value):
            out[pl.ds(2 * block, 2), seq] = value
        part = lambda kind: got[:, kind, seq].reshape(1024, 128)
        attend(part(0), part(1), part(2), bounds, seq, 2, store)
        for step in (4, 3, 5, 2, 6, 1, 7):
            back_copy(seq, step).start()
        return carry

    lax.fori_loop(0, 2, pair, 0)
    att[g.me] = out[g.me]

    def back8_copy(extra, step):
        return pltpu.make_async_remote_copy(
            src_ref=out8.at[g.other(step)], dst_ref=att.at[8, extra], send_sem=back8_sems.at[1 + step],
            recv_sem=back8_sems.at[extra], device_id=g.peer(g.other(step)), device_id_type=MESH)

    for extra in (0, 1):
        @pl.when(g.me == 4 * extra)
        def _():
            for step in range(1, 8):
                in8_copy(extra, g.other(step)).wait_recv()

            def store(block, value):
                out8[pl.ds(2 * block, 2)] = value
            part = lambda kind: got8[:, kind].reshape(1024, 128)
            attend(part(0), part(1), part(2), bounds, extra, 1, store)
            for step in range(1, 8):
                back8_copy(extra, step).start()
            att[8, extra] = out8[g.me]
            for step in range(1, 8):
                back8_copy(extra, step).wait_send()

        @pl.when(g.me != 4 * extra)
        def _():
            in8_copy(extra, g.me).wait_send()
            back8_copy(extra, 1).wait_recv()
    for step in range(1, 8):
        in_copy(step).wait_send()
        for seq in (0, 1):
            back_copy(seq, step).wait_recv()
            back_copy(seq, step).wait_send()


def attend_forward(hidden, lines, ga, bounds):
    tile = (128, 128)
    vmem = pltpu.VMEM
    return pl.pallas_call(
        attend_kernel,
        out_shape=(jax.ShapeDtypeStruct((9, 2) + tile, BF16),
                   jax.ShapeDtypeStruct((8, 3, 2) + tile, BF16),
                   jax.ShapeDtypeStruct((8, 3) + tile, BF16),
                   jax.ShapeDtypeStruct((D, 256), BF16)),
        in_specs=[pl.BlockSpec(memory_space=vmem)] * 2 + [
            pl.BlockSpec(memory_space=pl.ANY), pl.BlockSpec(memory_space=pltpu.SMEM)],
        out_specs=(pl.BlockSpec(memory_space=vmem),) * 4,
        scratch_shapes=[
            vmem((8, D, 512), BF16), vmem((9, 3, 2) + tile, BF16), vmem((8, 2) + tile, BF16), vmem((8,) + tile, BF16),
            pltpu.SemaphoreType.DMA((8,)),
            pltpu.SemaphoreType.DMA((2, 7)), pltpu.SemaphoreType.DMA((10,)),
            pltpu.SemaphoreType.DMA((2, 2, 7)), pltpu.SemaphoreType.DMA((9,))],
        compiler_params=pltpu.CompilerParams(
            collective_id=1, has_side_effects=True, vmem_limit_bytes=56 * 2**20),
    )(hidden, lines, ga, bounds)


def attend_pull(queries, keys, values, grads, bounds, seq, heads, key_sum, value_sum, store):
    queries = queries * 0.125
    key_t = turned(keys).astype(BF16)
    key_sum[...] = jnp.zeros_like(key_sum)
    value_sum[...] = jnp.zeros_like(value_sum)
    for block in range(4):
        rows = slice(block * 256, block * 256 + 256)
        size = block * 256 + 256
        parts = []
        for head in range(heads):
            query, grad = head_part(queries[rows], head), head_part(grads[rows], head)
            probs = chances(keys[:size], query, bounds, seq, block)
            change = lax.dot_general(values[:size], grad, NT, preferred_element_type=F32)
            inner = jnp.sum(probs * change, axis=0, keepdims=True)
            slope = (probs * (change - inner)).astype(BF16)
            value_sum[:size] += jnp.dot(probs.astype(BF16), grad, preferred_element_type=F32)
            key_sum[:size] += jnp.dot(slope, query, preferred_element_type=F32)
            parts.append(jnp.dot(key_t[:, :size], slope, preferred_element_type=F32))
        whole = parts[0] if heads == 1 else jnp.concatenate([parts[0][:64], parts[1][64:]], axis=0)
        store(0, block, (whole.T * 0.125).astype(BF16).reshape(2, 128, 128))
    for kind, total in ((1, key_sum), (2, value_sum)):
        for block in range(4):
            store(kind, block, total[block * 256 : block * 256 + 256].astype(BF16).reshape(2, 128, 128))


def pull_kernel(pack, got, got8, hidden, middle_grad, lines, ga, bounds, placed, input_grad, sums,
                weights, back, grad, grad8, out, out8, key_sum, value_sum,
                weight_sems, in_sems, in8_sems, back_sems, back8_sems):
    g = Group()
    copies = fetch_blocks(ga, weights, weight_sems, 0, 512)
    greet([g.peer(g.other(step)) for step in range(1, 8)])

    def in_copy(step):
        return push(pack.at[g.other(step)], grad.at[g.me], in_sems, (step - 1,), g.peer(g.other(step)))

    def in8_copy(extra, source):
        return pltpu.make_async_remote_copy(
            src_ref=pack.at[8, extra], dst_ref=grad8.at[source], send_sem=in8_sems.at[8 + extra],
            recv_sem=in8_sems.at[source], device_id=g.peer(4 * extra), device_id_type=MESH)

    for step in (4, 3, 5, 2, 6, 1, 7):
        in_copy(step).start()
    for extra in (0, 1):
        @pl.when(g.me != 4 * extra)
        def _():
            in8_copy(extra, g.me).start()

        @pl.when(g.me == 4 * extra)
        def _():
            grad8[g.me] = pack[8, extra]
    grad[g.me] = pack[g.me]
    for step in range(1, 8):
        in_copy(step).wait_recv()

    def back_copy(seq, step):
        return push(out.at[g.other(step), seq], back.at[g.me, seq], back_sems, (seq, step - 1),
                    g.peer(g.other(step)))

    def pair(seq, carry):
        def store(kind, block, value):
            out[pl.ds(2 * block, 2), seq, kind] = value
        part = lambda kind: got[:, kind, seq].reshape(1024, 128)
        attend_pull(part(0), part(1), part(2), grad[:, seq].reshape(1024, 128), bounds, seq, 2,
                    key_sum, value_sum, store)
        for step in (4, 3, 5, 2, 6, 1, 7):
            back_copy(seq, step).start()
        return carry

    lax.fori_loop(0, 2, pair, 0)
    back[g.me] = out[g.me]

    def back8_copy(extra, step):
        return pltpu.make_async_remote_copy(
            src_ref=out8.at[g.other(step)], dst_ref=back.at[8, extra], send_sem=back8_sems.at[1 + step],
            recv_sem=back8_sems.at[extra], device_id=g.peer(g.other(step)), device_id_type=MESH)

    for extra in (0, 1):
        @pl.when(g.me == 4 * extra)
        def _():
            for step in range(1, 8):
                in8_copy(extra, g.other(step)).wait_recv()

            def store(kind, block, value):
                out8[pl.ds(2 * block, 2), kind] = value
            part = lambda kind: got8[:, kind].reshape(1024, 128)
            attend_pull(part(0), part(1), part(2), grad8[...].reshape(1024, 128), bounds, extra, 1,
                        key_sum, value_sum, store)
            for step in range(1, 8):
                back8_copy(extra, step).start()
            back[8, extra] = out8[g.me]
            for step in range(1, 8):
                back8_copy(extra, step).wait_send()

        @pl.when(g.me != 4 * extra)
        def _():
            in8_copy(extra, g.me).wait_send()
            back8_copy(extra, 1).wait_recv()
    for step in range(1, 8):
        in_copy(step).wait_send()
        for seq in (0, 1):
            back_copy(seq, step).wait_recv()
            back_copy(seq, step).wait_send()

    natural = [jnp.concatenate([back[p, :, kind].reshape(256, 128) for p in range(9)],
                               axis=1).astype(F32) for kind in range(3)]
    total = None
    for s in range(8):
        tiles = {}
        for seg, low, width, kind, spot in segments():
            if seg == s:
                shift_lanes(tiles, natural[kind], spot, width, low)
        block = join_tiles(tiles, 4).astype(BF16)
        placed[s] = block
        copies[s].wait()
        term = dot_t(block, weights[s])
        total = term if total is None else total + term
    unit, scale = normalize(hidden[...].astype(F32).reshape(256, D))
    input_grad[...] = middle_grad[...] + norm_pull(total, lines[0:1, :D], unit, scale)
    sums[0:1] = jnp.sum(widen(total * unit), axis=0, keepdims=True)
    sums[1:2] = jnp.sum(widen(total), axis=0, keepdims=True)
    sums[2:3] = jnp.sum(natural[0], axis=0, keepdims=True)
    sums[3:4] = jnp.sum(natural[2], axis=0, keepdims=True)
    sums[4:8] = jnp.zeros((4, WIDE), F32)


def attend_backward(pack, got, got8, hidden, middle_grad, lines, ga, bounds):
    tile = (128, 128)
    vmem = pltpu.VMEM
    return pl.pallas_call(
        pull_kernel,
        out_shape=(jax.ShapeDtypeStruct((8, 256, 512), BF16),
                   jax.ShapeDtypeStruct((256, D), F32), jax.ShapeDtypeStruct((8, WIDE), F32)),
        in_specs=[pl.BlockSpec(memory_space=vmem)] * 6 + [
            pl.BlockSpec(memory_space=pl.ANY), pl.BlockSpec(memory_space=pltpu.SMEM)],
        out_specs=(pl.BlockSpec(memory_space=vmem),) * 3,
        scratch_shapes=[
            vmem((8, D, 512), BF16), vmem((9, 2, 3) + tile, BF16), vmem((8, 2) + tile, BF16), vmem((8,) + tile, BF16),
            vmem((8, 2, 3) + tile, BF16), vmem((8, 3) + tile, BF16),
            vmem((1024, 128), F32), vmem((1024, 128), F32),
            pltpu.SemaphoreType.DMA((8,)),
            pltpu.SemaphoreType.DMA((2, 7)), pltpu.SemaphoreType.DMA((10,)),
            pltpu.SemaphoreType.DMA((2, 2, 7)), pltpu.SemaphoreType.DMA((9,))],
        compiler_params=pltpu.CompilerParams(
            collective_id=2, has_side_effects=True, vmem_limit_bytes=60 * 2**20),
    )(pack, got, got8, hidden, middle_grad, lines, ga, bounds)


def middle_kernel(att, hidden, top, top_pad, lines, up_row, ga, gb,
                  layer_out, middle_grad, att_grad, att_t, normed_t, active, y_o, y_u, sums, up_sums,
                  held_o, held_u, held_b, normed, down_sum, norm_grad, sems_o, sems_u, sems_b):
    copies_o = [pltpu.make_async_copy(ga.at[s, :, pl.ds(384, 256)], held_o.at[s], sems_o.at[s])
                for s in range(8)]
    for copy in copies_o:
        copy.start()

    def up_copy(s):
        return pltpu.make_async_copy(ga.at[s, :, pl.ds(512, 640)], held_u.at[s], sems_u.at[s])

    def down_copy(y):
        return pltpu.make_async_copy(gb.at[y], held_b.at[y], sems_b.at[y])

    for y in range(4):
        up_copy(2 * y).start()
        up_copy(2 * y + 1).start()
        down_copy(y).start()

    attended = jnp.concatenate([att[p].reshape(256, 128) for p in range(9)], axis=1)
    att_t[...] = attended.astype(F32).T[:D].astype(BF16)
    tiles = {}
    for s in range(8):
        copies_o[s].wait()
        shift_lanes(tiles, dot(attended[:, :D], held_o[s]), 24, 136, 136 * s)
    branch = join_tiles(tiles, 9)[:, :D]
    middle = hidden[...].astype(F32).reshape(256, D) + branch + lines[6:7, :D]
    unit, scale = normalize(middle)
    value = unit * lines[1:2, :D] + lines[3:4, :D]
    normed[...] = value.astype(BF16)
    normed_t[...] = value.T.astype(BF16)
    down_sum[...] = jnp.zeros_like(down_sum)
    norm_grad[...] = jnp.zeros_like(norm_grad)

    def step(y, carry):
        tiles = {}
        for odd in (0, 1):
            up_copy(2 * y + odd).wait()
            shift_lanes(tiles, dot(normed[...], held_u[2 * y + odd]), 32, 544, 544 * odd)
        pre = join_tiles(tiles, 9)[:, :D] + up_row[y]
        cube = 0.7978845608028654 * (pre + 0.044715 * (pre * pre * pre))
        bend = jnp.tanh(cube)
        half = 0.5 * (1.0 + bend)
        acts = (pre * half).astype(BF16)
        slope = half + 0.5 * pre * (1.0 - bend * bend) * (
            0.7978845608028654 * (1.0 + 3 * 0.044715 * (pre * pre)))
        active[y] = acts
        down_copy(y).wait()
        weights = held_b[y].reshape(8 * B_ROWS, D)
        down_sum[...] += dot_t(acts, weights)
        inner = dot(top_pad[...], weights) * slope
        inner = widen(inner.astype(BF16).astype(F32))
        total = None
        for odd in (0, 1):
            tiles = {}
            shift_lanes(tiles, inner, 544 * odd, 544, 32)
            block = join_tiles(tiles, 5)
            up_sums[2 * y + odd] = jnp.sum(block, axis=0, keepdims=True)
            block = block.astype(BF16)
            y_u[2 * y + odd] = block
            term = dot_t(block, held_u[2 * y + odd])
            total = term if total is None else total + term
        norm_grad[...] += total
        return carry

    lax.fori_loop(0, 4, step, 0)
    tiles = {}
    down = down_sum[...]
    for s in range(8):
        shift_lanes(tiles, down, 144 * s, 136, 136 * s)
    out = middle + join_tiles(tiles, 9)[:, :D] + lines[7:8, :D]
    layer_out[...] = out.astype(BF16).reshape(2, 128, D)
    grad = norm_grad[...]
    cotangent = top[...].astype(F32).reshape(256, D)
    total = cotangent + norm_pull(grad, lines[1:2, :D], unit, scale)
    middle_grad[...] = total
    branch = widen(total.astype(BF16).astype(F32))
    back = None
    for s in range(8):
        tiles = {}
        shift_lanes(tiles, branch, 136 * s, 136, 24)
        block = join_tiles(tiles, 2).astype(BF16)
        y_o[s] = block
        term = dot_t(block, held_o[s])
        back = term if back is None else back + term
    back = widen(back).astype(BF16)
    for p in range(9):
        att_grad[p] = back[:, 128 * p : 128 * p + 128].reshape(2, 128, 128)
    sums[0:1] = jnp.sum(widen(grad * unit), axis=0, keepdims=True)
    sums[1:2] = jnp.sum(widen(grad), axis=0, keepdims=True)
    sums[2:3] = jnp.sum(branch, axis=0, keepdims=True)
    sums[3:4] = jnp.sum(widen(cotangent), axis=0, keepdims=True)
    sums[4:8] = jnp.zeros((4, WIDE), F32)


def middle_block(*operands):
    vmem = pltpu.VMEM
    shape = jax.ShapeDtypeStruct
    return pl.pallas_call(
        middle_kernel,
        out_shape=(
            shape((2, 128, D), BF16), shape((256, D), F32), shape((9, 2, 128, 128), BF16),
            shape((D, 256), BF16), shape((D, 256), BF16), shape((4, 256, D), BF16),
            shape((8, 256, 256), BF16), shape((8, 256, 640), BF16), shape((8, WIDE), F32),
            shape((8, 1, 640), F32)),
        in_specs=[pl.BlockSpec(memory_space=vmem)] * 6 + [pl.BlockSpec(memory_space=pl.ANY)] * 2,
        out_specs=(pl.BlockSpec(memory_space=vmem),) * 10,
        scratch_shapes=[
            vmem((8, D, 256), BF16), vmem((8, D, 640), BF16), vmem((4, 8, B_ROWS, D), BF16),
            vmem((256, D), BF16), vmem((256, WIDE), F32), vmem((256, D), F32),
            pltpu.SemaphoreType.DMA((8,)), pltpu.SemaphoreType.DMA((8,)),
            pltpu.SemaphoreType.DMA((4,))],
        compiler_params=pltpu.CompilerParams(vmem_limit_bytes=62 * 2**20),
    )(*operands)


def reduce_kernel(x_q, x_o, x_u, y_q, y_o, y_u, tt, act, extra, out_a, out_b,
                  sib_out1, sib_out2, sib_in1, sib_in2,
                  in_opp1, in_opp2, in_side1, in_side2,
                  acc1, acc2, end1, end2, in_end1, in_end2, in_mid1, in_mid2,
                  zout_a, zout_b, zin_a, zin_b,
                  sib_sems, opp_sems, side_sems, mid_sems, end_sems, z_sems):
    me = Place()
    greet(all_peers(me))

    def part1(xb, yy, parity):
        column = 2 * xb + parity
        rows = pl.ds(pl.multiple_of(yy * A_ROWS, 16), CUT)
        return outer(column, rows)

    def outer(column, rows):
        one = dot(x_q[rows], y_q[column])
        two = dot(x_o[rows], y_o[column])
        three = dot(x_u[rows], y_u[column])
        return jnp.concatenate([
            one[:, :384], one[:, 384:] + two[:, :128], two[:, 128:] + three[:, :128],
            three[:, 128:576]], axis=1)

    def part2(xb, yy, parity):
        column = 2 * xb + parity
        rows = pl.ds(pl.multiple_of(yy * A_ROWS + CUT, 16), A_ROWS - CUT)
        lower = jnp.dot(tt[column], act[yy], preferred_element_type=F32)
        lower = jnp.concatenate([lower[:136], extra[column]], axis=0)
        return jnp.concatenate([outer(column, rows), lower], axis=0)

    def turn(value, by):
        return (value + by) % 4

    def copy(source, target, sems, index, peer):
        return pltpu.make_async_remote_copy(
            src_ref=source, dst_ref=target, send_sem=sems.at[(0,) + index],
            recv_sem=sems.at[(1,) + index], device_id=peer, device_id_type=MESH)

    blocks = {
        0: dict(part=lambda step, o, par: part1(turn(me.x, step), turn(me.y, o), par),
                axes=("x", "y"), cut=96, sib_out=sib_out1, sib_in=sib_in1, in_opp=in_opp1,
                in_side=in_side1, acc=acc1, end=end1, in_end=in_end1, in_mid=in_mid1),
        1: dict(part=lambda step, o, par: part2(turn(me.x, o), turn(me.y, step), par),
                axes=("y", "x"), cut=64, sib_out=sib_out2, sib_in=sib_in2, in_opp=in_opp2,
                in_side=in_side2, acc=acc2, end=end2, in_end=in_end2, in_mid=in_mid2),
    }

    def sib_copy(half, step, o):
        b = blocks[half]
        return copy(b["sib_out"].at[o], b["sib_in"].at[step, o], sib_sems, (half, step, o), me.sibling)

    def cross(step, before):
        def body(o, carry):
            for half in (0, 1):
                b = blocks[half]
                if before is not None:
                    sib_copy(half, before, o).wait_send()
                b["sib_out"][o] = b["part"](step, o, 1 - me.c).astype(BF16)
                sib_copy(half, step, o).start()
            return carry
        lax.fori_loop(0, 4, body, 0)

    def mine(half, step, o):
        b = blocks[half]
        value = b["part"](step, o, me.c)
        sib_copy(half, step, o).wait_recv()
        return value + b["sib_in"][step, o].astype(F32)

    def ends_of(half, which):
        b = blocks[half]
        total = CUT
        return pl.ds(0, b["cut"]) if which == 0 else pl.ds(b["cut"], total - b["cut"])

    def opp_copy(half, o, which):
        b = blocks[half]
        rows = ends_of(half, which)
        return copy(b["sib_in"].at[2, o, rows], b["in_opp"].at[o, rows], opp_sems, (half, o, which),
                    me.peer(b["axes"][0], 1 if which == 0 else 3))

    def side_copy(half, o, which):
        b = blocks[half]
        return copy(b["sib_in"].at[1 + 2 * which, o], b["in_side"].at[which, o], side_sems, (half, o, which),
                    me.peer(b["axes"][0], 1 if which == 0 else 3))

    def mid_copy(half, which):
        b = blocks[half]
        rows = ends_of(half, which)
        return copy(b["end"].at[2, rows], b["in_mid"].at[rows], mid_sems, (half, which),
                    me.peer(b["axes"][1], 1 if which == 0 else 3))

    def end_copy(half, which):
        b = blocks[half]
        return copy(b["end"].at[which], b["in_end"].at[which], end_sems, (half, which),
                    me.peer(b["axes"][1], 1 if which == 0 else 3))

    def loop(body):
        lax.fori_loop(0, 4, lambda o, carry: (body(o), carry)[1], 0)

    def opposite(o):
        for half in (0, 1):
            blocks[half]["sib_in"][2, o] = mine(half, 2, o).astype(BF16)
            for which in (0, 1):
                opp_copy(half, o, which).start()

    def sides(o):
        for half in (0, 1):
            b = blocks[half]
            cut = b["cut"]
            for which in (0, 1):
                value = mine(half, 1 if which == 0 else 3, o)
                opp_copy(half, o, which).wait_recv()
                if which == 0:
                    value = jnp.concatenate(
                        [value[:cut] + b["in_opp"][o, :cut].astype(F32), value[cut:]], axis=0)
                else:
                    value = jnp.concatenate(
                        [value[:cut], value[cut:] + b["in_opp"][o, cut:].astype(F32)], axis=0)
                b["sib_in"][1 + 2 * which, o] = value.astype(BF16)
                side_copy(half, o, which).start()

    def own(o):
        for half in (0, 1):
            b = blocks[half]
            value = mine(half, 0, o)
            for which in (0, 1):
                side_copy(half, o, which).wait_recv()
                value = value + b["in_side"][which, o].astype(F32)
            b["acc"][o] = value

    cross(2, None)
    loop(opposite)
    cross(1, 2)
    cross(3, 1)
    loop(sides)
    cross(0, 3)
    loop(own)
    for half in (0, 1):
        b = blocks[half]
        b["end"][2] = b["acc"][2].astype(BF16)
        for which in (0, 1):
            mid_copy(half, which).start()
    for half in (0, 1):
        b = blocks[half]
        cut = b["cut"]
        for which in (0, 1):
            value = b["acc"][1 if which == 0 else 3]
            mid_copy(half, which).wait_recv()
            if which == 0:
                value = jnp.concatenate([value[:cut] + b["in_mid"][:cut].astype(F32), value[cut:]], axis=0)
            else:
                value = jnp.concatenate([value[:cut], value[cut:] + b["in_mid"][cut:].astype(F32)], axis=0)
            b["end"][which] = value.astype(BF16)
            end_copy(half, which).start()
    final = []
    for half in (0, 1):
        b = blocks[half]
        value = b["acc"][0]
        for which in (0, 1):
            end_copy(half, which).wait_recv()
            value = value + b["in_end"][which].astype(F32)
        final.append(value.astype(BF16))
    block_a = jnp.concatenate([final[0], final[1][:64]], axis=0)
    block_b = final[1][64:]

    def slices(z):
        row = lax.broadcasted_iota(jnp.int32, (80, A_ROWS), 0)
        col = lax.broadcasted_iota(jnp.int32, (80, A_ROWS), 1)
        pick = jnp.where((col == row + 68 * z) & (row < 68), 1.0, 0.0).astype(BF16)
        row = lax.broadcasted_iota(jnp.int32, (D, 384), 0)
        col = lax.broadcasted_iota(jnp.int32, (D, 384), 1)
        pick_b = jnp.where((row == col + 272 * z) & (col < 272), 1.0, 0.0).astype(BF16)
        lower = jnp.dot(block_b, pick_b, preferred_element_type=F32)
        row = lax.broadcasted_iota(jnp.int32, (B_ROWS, 384), 0)
        lower = jnp.where(row < 136, lower, block_b[:, :384].astype(F32))
        return jnp.dot(pick, block_a, preferred_element_type=F32), lower

    def z_copies(step):
        peer = me.peer("z", step)
        return (copy(zout_a.at[step - 1], zin_a.at[step - 1], z_sems, (0, step - 1), peer),
                copy(zout_b.at[step - 1], zin_b.at[step - 1], z_sems, (1, step - 1), peer))

    for step in (2, 1, 3):
        upper, lower = slices(turn(me.z, step))
        zout_a[step - 1] = upper.astype(BF16)
        zout_b[step - 1] = lower.astype(BF16)
        for c in z_copies(step):
            c.start()
    upper, lower = slices(me.z)
    for step in (1, 2, 3):
        for c in z_copies(step):
            c.wait_recv()
        upper = upper + zin_a[step - 1].astype(F32)
        lower = lower + zin_b[step - 1].astype(F32)
    out_a[...] = upper
    out_b[...] = lower

    def drain(o):
        for half in (0, 1):
            sib_copy(half, 0, o).wait_send()
            for which in (0, 1):
                opp_copy(half, o, which).wait_send()
                side_copy(half, o, which).wait_send()

    loop(drain)
    for half in (0, 1):
        for which in (0, 1):
            mid_copy(half, which).wait_send()
            end_copy(half, which).wait_send()
    for step in (1, 2, 3):
        for c in z_copies(step):
            c.wait_send()


def reduce_weights(*operands):
    half = (CUT, D)
    vmem = pltpu.VMEM
    pair = lambda *lead: [vmem(lead + half, BF16), vmem(lead + half, BF16)]
    return pl.pallas_call(
        reduce_kernel,
        out_shape=(jax.ShapeDtypeStruct((80, D), F32), jax.ShapeDtypeStruct((B_ROWS, 384), F32)),
        in_specs=[pl.BlockSpec(memory_space=vmem)] * 9,
        out_specs=(pl.BlockSpec(memory_space=vmem),) * 2,
        scratch_shapes=(
            pair(4) + pair(4, 4) + pair(4) + pair(2, 4)
            + [vmem((4,) + half, F32)] * 2 + pair(3) + pair(2) + pair()
            + [vmem((3, 80, D), BF16), vmem((3, B_ROWS, 384), BF16)] * 2
            + [pltpu.SemaphoreType.DMA((2, 2, 4, 4)), pltpu.SemaphoreType.DMA((2, 2, 4, 2)),
               pltpu.SemaphoreType.DMA((2, 2, 4, 2)), pltpu.SemaphoreType.DMA((2, 2, 2)),
               pltpu.SemaphoreType.DMA((2, 2, 2)), pltpu.SemaphoreType.DMA((2, 2, 3))]),
        compiler_params=pltpu.CompilerParams(
            collective_id=3, has_side_effects=True, vmem_limit_bytes=63 * 2**20),
    )(*operands)


def per_device(
    inputs, out_grad, segment_ids, qkv_weight, out_weight, up_weight, down_weight,
    norm_gains, norm_shifts, qv_bias, proj_bias, up_bias,
):
    seqs, rows, _ = inputs.shape
    tokens = seqs * rows
    batch = lax.axis_index("batch")

    blob_a = jnp.concatenate([qkv_weight, out_weight, up_weight], axis=1)
    blob_a = jnp.pad(blob_a, ((0, 12), (0, WIDE - D)))
    counts = jnp.sum(segment_ids[:, :, None] < jnp.arange(1, 4)[None, None, :], axis=1)
    counts = jnp.pad(counts.astype(BF16).reshape(1, 6), ((0, 3), (0, 130)))
    vec = jnp.concatenate([norm_gains, norm_shifts, qv_bias, proj_bias], axis=0)
    vec = jnp.concatenate(
        [vec, jnp.concatenate([up_bias.reshape(4, 136), counts], axis=0)], axis=1
    )
    blob_b = jnp.concatenate([down_weight.T, vec], axis=0)
    blob_b = jnp.pad(blob_b, ((0, 0), (0, 112)))
    whole_a, whole_b = gather_weights(blob_a, blob_b)
    vec = lax.dynamic_slice(whole_b, (batch // 4, 0, 136, 272 * (batch % 4)), (1, 8, 8, 272))
    vec = vec[0].astype(F32)
    lines = jnp.pad(vec[:, :, :136].transpose(1, 0, 2).reshape(8, D), ((0, 0), (0, WIDE - D)))
    up_row = vec[:, :4, 136:].reshape(4, 1, D)
    bounds = jnp.sum(vec[:, 4, 136:142], axis=0).astype(jnp.int32).reshape(2, 3)

    top_blocks = jnp.pad(out_grad.reshape(tokens, 8, 136), ((0, 0), (0, 0), (0, 8)))
    top_pad = top_blocks.reshape(tokens, 8 * B_ROWS)
    top_t = top_pad.T.reshape(8, B_ROWS, tokens)

    att, got, got8, normed_t = attend_forward(inputs, lines, whole_a, bounds)
    (layer_out, middle_grad, att_grad, att_t, normed_two_t, active, y_o, y_u, sums, up_sums) = (
        middle_block(att, inputs, out_grad, top_pad, lines, up_row, whole_a, whole_b)
    )
    y_q, input_grad, more_sums = attend_backward(
        att_grad, got, got8, inputs, middle_grad, lines, whole_a, bounds
    )
    sums = jnp.stack([more_sums[0], sums[0], more_sums[1], sums[1], more_sums[2], more_sums[3],
                      sums[2], sums[3]])[:, :D].reshape(8, 8, 136)
    up_sums = jnp.pad(up_sums[:, 0, 32:576].reshape(8, 4, 136), ((0, 0), (0, 4), (0, 0)))
    extra = jnp.concatenate([sums.transpose(1, 0, 2), up_sums], axis=2)
    extra = jnp.pad(extra, ((0, 0), (0, 0), (0, D - 272)))
    out_a, out_b = reduce_weights(
        normed_t, att_t, normed_two_t, y_q, y_o, y_u, top_t, active, extra
    )
    return (
        layer_out,
        input_grad.reshape(seqs, rows, D),
        out_a[:68, :408],
        out_a[:68, 408:544],
        out_a[:68, 544:],
        out_b[:136, :272].T,
        out_b[136:138, :136],
        out_b[138:140, :136],
        out_b[140:142, :136],
        out_b[142:144, :136],
        out_b[136:140, 136:272].reshape(1, 544),
    )


def solution(mesh):
    tokens = P("batch", "seq", None)
    matrix = P("batch", "seq")
    vector = P(None, "seq")
    return jax.shard_map(
        per_device,
        mesh=mesh,
        in_specs=(tokens, tokens, matrix, matrix, matrix, matrix, matrix) + (vector,) * 5,
        out_specs=(tokens, tokens, matrix, matrix, matrix, matrix) + (vector,) * 5,
        check_vma=False,
    )
```

```python
import jax
import jax.numpy as jnp
from jax import lax
from jax.experimental import pallas as pl
from jax.experimental.pallas import tpu as pltpu
from jax.sharding import PartitionSpec as P

D = 1088
WIDE = 1152
F32 = jnp.float32
BF16 = jnp.bfloat16
MESH = pl.DeviceIdType.MESH
A_ROWS, B_ROWS = 272, 144
CUT = 208


class Place:
    def __init__(self):
        batch, seq = lax.axis_index("batch"), lax.axis_index("seq")
        self.batch, self.seq = batch, seq
        self.y, self.z = batch // 4, batch % 4
        self.x, self.c = seq // 2, seq % 2
        self.sibling = {"batch": batch, "seq": self.x * 2 + 1 - self.c}

    def other(self, step):
        return (self.seq + step) % 8

    def member(self, seq):
        return {"batch": self.batch, "seq": seq}

    def peer(self, axis, step):
        spot = {"x": self.x, "y": self.y, "z": self.z}
        spot[axis] = (spot[axis] + step + 4) % 4
        return {"batch": spot["y"] * 4 + spot["z"], "seq": spot["x"] * 2 + self.c}


def greet(peers):
    barrier = pltpu.get_barrier_semaphore()
    for peer in peers:
        pl.semaphore_signal(barrier, inc=1, device_id=peer, device_id_type=MESH)
    pl.semaphore_wait(barrier, len(peers))


def all_peers(me):
    return [me.member(me.other(step)) for step in range(1, 8)] + [me.peer(axis, step) for axis, step in (
        ("y", 1), ("y", 3), ("z", 1), ("z", 2), ("z", 3))]


class Sender:
    def __init__(self, send_sems, recv_sems):
        self.send_sems, self.recv_sems, self.made = send_sems, recv_sems, []

    def __call__(self, source, target, peer):
        index = len(self.made)
        copy = pltpu.make_async_remote_copy(
            src_ref=source, dst_ref=target, send_sem=self.send_sems.at[index],
            recv_sem=self.recv_sems.at[index], device_id=peer, device_id_type=MESH)
        copy.start()
        self.made.append(copy)
        return copy


LATE = (
    [("relay", 0, 0)], [("relay", 1, 0)], [("close", 0, 0)],
    [("relay", 1, 1)], [("relay", 0, 1)], [("relay", 1, 3)], [("relay", 0, 3)], [("close", 1, 0)],
    [("relay", 1, 2)], [("relay", 0, 2)], [("close", 0, 1), ("close", 1, 1)],
    [("close", 0, 3), ("close", 1, 3)], [("close", 0, 2), ("close", 1, 2)], [("settle",)],
)


def merge_rows(stacked):
    row = lax.broadcasted_iota(jnp.int32, (A_ROWS, 320), 0)
    col = lax.broadcasted_iota(jnp.int32, (A_ROWS, 320), 1)
    pick = jnp.where(col == row + 12 * (row // 68), 1.0, 0.0).astype(BF16)
    return jnp.dot(pick, stacked, preferred_element_type=F32).astype(BF16)


def merge_columns(slots):
    total = None
    for z in range(4):
        row = lax.broadcasted_iota(jnp.int32, (384, D), 0)
        col = lax.broadcasted_iota(jnp.int32, (384, D), 1)
        pick = jnp.where((col == row + 272 * z) & (row < 272), 1.0, 0.0).astype(BF16)
        term = jnp.dot(slots[z], pick, preferred_element_type=F32)
        total = term if total is None else total + term
    return total.astype(BF16)

AXES = {0: ("x", "y"), 1: ("y", "x")}


class Rings:
    def __init__(self, me, send, whole, split, source, spot):
        self.me, self.send, self.whole, self.split = me, send, whole, split
        self.source, self.spot, self.crossed, self.sent = source, spot, [], {}

    def move(self, axis, steps, by):
        if axis == "x":
            return ((steps[0] + by) % 4, steps[1])
        return (steps[0], (steps[1] + by) % 4)

    def push(self, part, steps, peer):
        source = self.source if steps == (0, 0) else lambda part: self.spot(part, *steps)
        return self.send(source(part), self.spot(part, *steps), peer)

    def cross(self, half, steps):
        self.crossed.append(self.push(self.whole[half], steps, self.me.sibling))

    def begin(self, half, axis, steps):
        return {by: self.push(self.whole[half], steps, self.me.peer(axis, by)) for by in (1, 3)}

    def forward(self, half, axis, steps, sent, flip):
        ends = []
        for by, which in ((1, flip), (3, 1 - flip)):
            origin = self.move(axis, steps, -by)
            sent[by].wait_recv()
            ends.append(self.push(self.split[half][which], origin, self.me.peer(axis, by)))
        return ends

    def arrived(self, half, axis, steps):
        for by in (1, 3):
            self.cross(half, self.move(axis, steps, by))

    def finish(self, half, axis, steps, ends):
        for copy in ends:
            copy.wait_recv()
        self.cross(half, self.move(axis, steps, 2))

    def first(self, half):
        self.sent[half] = self.begin(half, AXES[half][0], (0, 0))

    def second(self, half):
        self.sent[half, 0] = self.begin(half, AXES[half][1], (0, 0))
        self.cross(half, (0, 0))

    def spread(self, half):
        axis = AXES[half][0]
        self.sent[half, "far"] = self.forward(half, axis, (0, 0), self.sent[half], half)
        for by in (1, 3):
            self.sent[half, by] = self.begin(half, AXES[half][1], self.move(axis, (0, 0), by))
        self.arrived(half, axis, (0, 0))

    def far(self, half):
        axis = AXES[half][0]
        self.finish(half, axis, (0, 0), self.sent[half, "far"])
        self.sent[half, 2] = self.begin(half, AXES[half][1], self.move(axis, (0, 0), 2))

    def relay(self, half, by):
        steps = self.move(AXES[half][0], (0, 0), by)
        self.sent[half, by, "end"] = self.forward(
            half, AXES[half][1], steps, self.sent[half, by], by % 2)
        self.arrived(half, AXES[half][1], steps)

    def close(self, half, by):
        steps = self.move(AXES[half][0], (0, 0), by)
        self.finish(half, AXES[half][1], steps, self.sent[half, by, "end"])

    def settle(self):
        for copy in self.crossed:
            copy.wait_recv()

    def run(self, *actions):
        for name, *rest in actions:
            getattr(self, name)(*rest)


NT = (((1,), (1,)), ((), ()))


def normalize(values):
    center = values - jnp.mean(values, axis=-1, keepdims=True)
    spread = jnp.mean(center * center, axis=-1, keepdims=True)
    scale = lax.rsqrt(spread + 1e-05)
    return center * scale, scale


def norm_pull(grad, gain, unit, scale):
    scaled = grad * gain
    return scale * (
        scaled
        - jnp.mean(scaled, axis=-1, keepdims=True)
        - unit * jnp.mean(scaled * unit, axis=-1, keepdims=True)
    )


def dot(left, right):
    return jnp.dot(left, right, preferred_element_type=F32)


def dot_t(left, right):
    return lax.dot_general(left, right, NT, preferred_element_type=F32)


def widen(value):
    return jnp.concatenate([value, jnp.zeros((value.shape[0], WIDE - D), value.dtype)], axis=1)


def shift_lanes(tiles, value, source, width, target):
    turn = (target - source) % 128
    low, high = source // 128, -(-(source + width) // 128)
    part = value[:, low * 128 : high * 128]
    if turn:
        part = jnp.concatenate([part, jnp.zeros((part.shape[0], 128), part.dtype)], axis=1)
        part = pltpu.roll(part, turn, 1)
    start = source - low * 128 + turn
    for spot in range(start // 128, -(-(start + width) // 128)):
        tile = part[:, spot * 128 : spot * 128 + 128]
        first, last = start - spot * 128, start + width - spot * 128
        if first > 0 or last < 128:
            lane = lax.broadcasted_iota(jnp.int32, tile.shape, 1)
            tile = jnp.where((lane >= first) & (lane < last), tile, 0.0)
        place = (target - start) // 128 + spot
        tiles[place] = tiles[place] + tile if place in tiles else tile


def join_tiles(tiles, count):
    rows = next(iter(tiles.values())).shape[0]
    empty = jnp.zeros((rows, 128), F32)
    return jnp.concatenate([tiles.get(k, empty) for k in range(count)], axis=1)


def segments():
    found = []
    for s in range(8):
        for kind in range(3):
            low, high = max(408 * s, D * kind), min(408 * s + 408, D * kind + D)
            if low < high:
                found.append((s, low - 408 * s, high - low, kind, low - D * kind))
    return found


class Reduce:
    def __init__(self, me, blocks, sib_sems, opp_sems, side_sems, mid_sems, end_sems):
        self.me, self.blocks = me, blocks
        self.sib_sems, self.opp_sems, self.side_sems = sib_sems, opp_sems, side_sems
        self.mid_sems, self.end_sems = mid_sems, end_sems

    def copy(self, source, target, sems, index, peer):
        return pltpu.make_async_remote_copy(
            src_ref=source, dst_ref=target, send_sem=sems.at[(0,) + index],
            recv_sem=sems.at[(1,) + index], device_id=peer, device_id_type=MESH)

    def part(self, half, step, o, parity):
        b = self.blocks[half]
        along, beside = (self.me.x, self.me.y) if half == 0 else (self.me.y, self.me.x)
        first, second = (along + step) % 4, (beside + o) % 4
        x, y = (first, second) if half == 0 else (second, first)
        return b["part"](2 * x + parity, y)

    def ends_of(self, half, which):
        b = self.blocks[half]
        return pl.ds(0, b["cut"]) if which == 0 else pl.ds(b["cut"], b["rows"] - b["cut"])

    def beside(self, half, stage, which):
        return self.me.peer(AXES[half][stage], 1 if which == 0 else 3)

    def sib_copy(self, half, step, o):
        b = self.blocks[half]
        return self.copy(b["sib_out"].at[o], b["sib_in"].at[step, o], self.sib_sems,
                         (half, step, o), self.me.sibling)

    def opp_copy(self, half, o, which):
        b = self.blocks[half]
        rows = self.ends_of(half, which)
        return self.copy(b["sib_in"].at[2, o, rows], b["in_opp"].at[o, rows], self.opp_sems,
                         (half, o, which), self.beside(half, 0, which))

    def side_copy(self, half, o, which):
        b = self.blocks[half]
        return self.copy(b["sib_in"].at[1 + 2 * which, o], b["in_side"].at[which, o],
                         self.side_sems, (half, o, which), self.beside(half, 0, which))

    def mid_copy(self, half, which):
        b = self.blocks[half]
        rows = self.ends_of(half, which)
        return self.copy(b["sib_out"].at[2, rows], b["in_mid"].at[rows], self.mid_sems,
                         (half, which), self.beside(half, 1, which))

    def end_copy(self, half, which):
        b = self.blocks[half]
        return self.copy(b["sib_out"].at[which], b["in_end"].at[which], self.end_sems,
                         (half, which), self.beside(half, 1, which))

    def loop(self, body):
        lax.fori_loop(0, 4, lambda o, carry: (body(o), carry)[1], 0)

    def cross(self, step, before):
        def body(o):
            for half in (0, 1):
                if before is not None:
                    self.sib_copy(half, before, o).wait_send()
                self.blocks[half]["sib_out"][o] = self.part(half, step, o, 1 - self.me.c).astype(BF16)
                self.sib_copy(half, step, o).start()
        self.loop(body)

    def mine(self, half, step, o):
        value = self.part(half, step, o, self.me.c)
        self.sib_copy(half, step, o).wait_recv()
        return value + self.blocks[half]["sib_in"][step, o].astype(F32)

    def opposite(self):
        def body(o):
            for half in (0, 1):
                self.blocks[half]["sib_in"][2, o] = self.mine(half, 2, o).astype(BF16)
                for which in (0, 1):
                    self.opp_copy(half, o, which).start()
        self.loop(body)

    def join(self, half, value, arrived, which):
        cut = self.blocks[half]["cut"]
        if which == 0:
            return jnp.concatenate([value[:cut] + arrived[:cut].astype(F32), value[cut:]], axis=0)
        return jnp.concatenate([value[:cut], value[cut:] + arrived[cut:].astype(F32)], axis=0)

    def sides(self, which):
        def body(o):
            for half in (0, 1):
                b = self.blocks[half]
                value = self.mine(half, 1 + 2 * which, o)
                self.opp_copy(half, o, which).wait_recv()
                value = self.join(half, value, b["in_opp"].at[o], which)
                b["sib_in"][1 + 2 * which, o] = value.astype(BF16)
                self.side_copy(half, o, which).start()
        self.loop(body)

    def own(self):
        def body(o):
            for half in (0, 1):
                b = self.blocks[half]
                value = self.mine(half, 0, o)
                for which in (0, 1):
                    self.side_copy(half, o, which).wait_recv()
                    value = value + b["in_side"][which, o].astype(F32)
                b["acc"][o] = value
        self.loop(body)

    def middle(self):
        def body(o):
            for half in (0, 1):
                self.sib_copy(half, 0, o).wait_send()
        self.loop(body)
        for half in (0, 1):
            b = self.blocks[half]
            b["sib_out"][2] = b["acc"][2].astype(BF16)
            for which in (0, 1):
                self.mid_copy(half, which).start()

    def last(self):
        for half in (0, 1):
            b = self.blocks[half]
            for which in (0, 1):
                value = b["acc"][1 + 2 * which]
                self.mid_copy(half, which).wait_recv()
                b["sib_out"][which] = self.join(half, value, b["in_mid"], which).astype(BF16)
                self.end_copy(half, which).start()

    def result(self, half):
        b = self.blocks[half]
        value = b["acc"][0]
        for which in (0, 1):
            self.end_copy(half, which).wait_recv()
            value = value + b["in_end"][which].astype(F32)
        return value

    def drain(self):
        def body(o):
            for half in (0, 1):
                for which in (0, 1):
                    self.opp_copy(half, o, which).wait_send()
                    self.side_copy(half, o, which).wait_send()
        self.loop(body)
        for half in (0, 1):
            for which in (0, 1):
                self.mid_copy(half, which).wait_send()
                self.end_copy(half, which).wait_send()


REDUCE_BUFFERS = ("sib_out", "sib_in", "in_opp", "in_side", "acc", "in_end", "in_mid")


def reduce_scratch(shapes):
    found = []
    for shape in shapes:
        for lead, kind in (((4,), BF16), ((4, 4), BF16), ((4,), BF16), ((2, 4), BF16), ((4,), F32),
                           ((2,), BF16), ((), BF16)):
            found.append(pltpu.VMEM(lead + shape, kind))
    return found + [pltpu.SemaphoreType.DMA((2, 2, 4, 4)), pltpu.SemaphoreType.DMA((2, 2, 4, 2)),
                    pltpu.SemaphoreType.DMA((2, 2, 4, 2)), pltpu.SemaphoreType.DMA((2, 2, 2)),
                    pltpu.SemaphoreType.DMA((2, 2, 2))]


REDUCE_REFS = 2 * len(REDUCE_BUFFERS) + 5


def make_reduce(me, refs, settings):
    blocks = {}
    count = len(REDUCE_BUFFERS)
    for half in (0, 1):
        part, rows, cut = settings[half]
        blocks[half] = dict(zip(REDUCE_BUFFERS, refs[half * count : half * count + count]))
        blocks[half].update(part=part, rows=rows, cut=cut)
    return Reduce(me, blocks, *refs[2 * count :])


def leave_kernel(x_q, x_o, y_q, y_o, extra, block_u, block_b, out_a, out_b,
                 zout_q, zout_u, zout_b, zin_q, zin_u, zin_b, z_sems, *refs):
    me = Place()
    greet(all_peers(me))

    def upper(column, y):
        return rows_of(column, pl.ds(pl.multiple_of(y * A_ROWS, 16), 144))

    def rows_of(column, rows):
        one = dot(x_q[rows], y_q[column])
        two = dot(x_o[rows], y_o[column, :, 0:128])
        return jnp.concatenate([one[:, :384], one[:, 384:] + two], axis=1)

    def lower(column, y):
        rows = pl.ds(pl.multiple_of(y * A_ROWS + 144, 16), 128)
        return jnp.concatenate([rows_of(column, rows), extra[column]], axis=0)

    reduce = make_reduce(me, refs, ((upper, 144, 64), (lower, 144, 64)))

    def pick_rows(z):
        row = lax.broadcasted_iota(jnp.int32, (80, A_ROWS), 0)
        col = lax.broadcasted_iota(jnp.int32, (80, A_ROWS), 1)
        return jnp.where((col == row + 68 * z) & (row < 68), 1.0, 0.0).astype(BF16)

    def pick_columns(z):
        row = lax.broadcasted_iota(jnp.int32, (D, 384), 0)
        col = lax.broadcasted_iota(jnp.int32, (D, 384), 1)
        return jnp.where((row == col + 272 * z) & (col < 272), 1.0, 0.0).astype(BF16)

    buffers = ((zout_q, zin_q), (zout_u, zin_u), (zout_b, zin_b))

    def z_copy(kind, step):
        source, target = buffers[kind]
        return reduce.copy(source.at[step - 1], target.at[step - 1], z_sems, (kind, step - 1),
                           me.peer("z", step))

    def early(step):
        z = (me.z + step) % 4
        zout_u[step - 1] = dot(pick_rows(z), block_u[...]).astype(BF16)
        zout_b[step - 1] = dot(block_b[...], pick_columns(z)).astype(BF16)
        z_copy(1, step).start()
        z_copy(2, step).start()

    reduce.cross(2, None)
    reduce.opposite()
    reduce.cross(1, 2)
    reduce.cross(3, 1)
    early(2)
    reduce.sides(0)
    reduce.sides(1)
    reduce.cross(0, 3)
    early(1)
    early(3)
    reduce.own()
    reduce.middle()
    reduce.last()
    first, second = reduce.result(0), reduce.result(1)
    block_q = jnp.concatenate([first, second[:128]], axis=0).astype(BF16)
    payload = second[128:]

    def slices(z):
        return jnp.concatenate([dot(pick_rows(z), block_q), payload], axis=0)

    for step in (2, 1, 3):
        zout_q[step - 1] = slices((me.z + step) % 4).astype(BF16)
        z_copy(0, step).start()
    near = slices(me.z)
    above = dot(pick_rows(me.z), block_u[...])
    below = dot(block_b[...], pick_columns(me.z))
    for step in (1, 2, 3):
        z_copy(1, step).wait_recv()
        z_copy(2, step).wait_recv()
        above = above + zin_u[step - 1].astype(F32)
        below = below + zin_b[step - 1].astype(F32)
    for step in (1, 2, 3):
        z_copy(0, step).wait_recv()
        near = near + zin_q[step - 1].astype(F32)
    out_a[:, :512] = near[:80]
    out_a[:, 512:] = above
    out_b[:136] = below[:136]
    out_b[136:] = near[80:88, :384]
    reduce.drain()
    for step in (1, 2, 3):
        for kind in range(3):
            z_copy(kind, step).wait_send()


def leave_block(*operands):
    vmem = pltpu.VMEM
    return pl.pallas_call(
        leave_kernel,
        out_shape=(jax.ShapeDtypeStruct((80, WIDE), F32), jax.ShapeDtypeStruct((B_ROWS, 384), F32)),
        in_specs=[pl.BlockSpec(memory_space=vmem)] * 7,
        out_specs=(pl.BlockSpec(memory_space=vmem),) * 2,
        scratch_shapes=(
            [vmem((3, 96, 512), BF16), vmem((3, 80, 640), BF16), vmem((3, B_ROWS, 384), BF16)] * 2
            + [pltpu.SemaphoreType.DMA((2, 3, 3))] + reduce_scratch(((144, 512), (144, 512)))),
        compiler_params=pltpu.CompilerParams(
            collective_id=3, has_side_effects=True, vmem_limit_bytes=60 * 2**20),
    )(*operands)


def push(source, target, sems, index, peer):
    return pltpu.make_async_remote_copy(
        src_ref=source, dst_ref=target, send_sem=sems.at[(0,) + index],
        recv_sem=sems.at[(1,) + index], device_id=peer, device_id_type=MESH)


def turned(value):
    return value.astype(F32).T


def masked(scores, bounds, seq, block):
    rows = lax.broadcasted_iota(jnp.int32, scores.shape, 0)
    spot = block * 256 + lax.broadcasted_iota(jnp.int32, (1, 256), 1)
    start = jnp.zeros((1, 256), jnp.int32)
    for n in range(3):
        bound = bounds[:, 3 * seq + n : 3 * seq + n + 1]
        start = jnp.where(spot >= bound, bound, start)
    return jnp.where((rows <= spot) & (rows >= start), scores, -1e30)


def chances(keys, query, bounds, seq, block):
    scores = lax.dot_general(keys, query, NT, preferred_element_type=F32)
    scores = masked(scores, bounds, seq, block)
    powers = jnp.exp(scores - jnp.max(scores, axis=0, keepdims=True))
    return powers * (1.0 / jnp.sum(powers, axis=0, keepdims=True))


def head_part(value, head):
    lane = lax.broadcasted_iota(jnp.int32, value.shape, 1)
    return jnp.where((lane < 64) == (head == 0), value, jnp.zeros_like(value))


def attend(queries, keys, values, bounds, seq, heads, store, pump):
    queries = queries * 0.125
    value_t = turned(values).astype(BF16)
    for block in range(4):
        rows = slice(block * 256, block * 256 + 256)
        size = block * 256 + 256
        parts = []
        for head in range(heads):
            low = chances(keys[:size], head_part(queries[rows], head), bounds, seq, block).astype(BF16)
            parts.append(dot(value_t[:, :size], low))
            pump()
        whole = parts[0] if heads == 1 else jnp.concatenate([parts[0][:64], parts[1][64:]], axis=0)
        store(block, whole.T.astype(BF16).reshape(2, 128, 128))


def fetch_blocks(source, held, sems):
    copies = [pltpu.make_async_copy(source.at[s], held.at[s], sems.at[s]) for s in range(8)]
    for copy in copies:
        copy.start()
    return copies


GATHER_COPIES = 160
COUNTS_ROW = 12


def enter_kernel(a_ref, b_ref, vec, hidden, gq, gu, gb, att, got, got8, normed_t, lines, up_row,
                 bound_row, weights, za, zb, mine_a, mine_b, vecs, pack, out, out8,
                 send_sems, recv_sems, local_sems, vec_sems, in_sems, in8_sems, back_sems, back8_sems):
    g = Place()
    greet(all_peers(g))
    send = Sender(send_sems, recv_sems)
    first = []
    left, right = pl.ds(0, 512), pl.ds(512, 640)
    for step in (2, 1, 3):
        first.append(send(a_ref.at[:, left], za.at[g.z, :, left], g.peer("z", step)))
    later = []
    for step in (2, 1, 3):
        later.append(send(a_ref.at[:, right], za.at[g.z, :, right], g.peer("z", step)))
        later.append(send(b_ref, zb.at[g.z], g.peer("z", step)))

    def vec_copy(step):
        return push(vec, vecs.at[g.seq], vec_sems, (step - 1,), g.member(g.other(step)))

    for step in range(1, 8):
        vec_copy(step).start()
    vecs[g.seq] = vec[...]
    za[g.z] = a_ref[...]
    zb[g.z] = b_ref[...]
    for copy in first:
        copy.wait_recv()
    mine_a[:, :512] = merge_rows(za[:, :, :512].reshape(320, 512))

    def spot(part, step_x, step_y):
        kind, low, rows = part
        x, y = (g.x + step_x) % 4, (g.y + step_y) % 4
        if kind == "b":
            return gb.at[y, 2 * x + g.c, pl.ds(low, rows)]
        span = pl.ds(pl.multiple_of(y * A_ROWS + low, 16), rows)
        return (weights if kind == "q" else gu).at[2 * x + g.c, span]

    def source(part):
        kind, low, rows = part
        if kind == "b":
            return mine_b.at[pl.ds(low, rows)]
        return mine_a.at[pl.ds(low, rows), left if kind == "q" else right]

    near = Rings(g, send, {0: ("q", 0, 144), 1: ("q", 144, 128)},
                 {0: [("q", 0, 64), ("q", 64, 80)], 1: [("q", 144, 64), ("q", 208, 64)]}, source, spot)
    rest = Rings(g, send, {0: ("u", 0, 272), 1: ("b", 0, 144)},
                 {0: [("u", 0, 128), ("u", 128, 144)], 1: [("b", 0, 64), ("b", 64, 80)]}, source, spot)
    near.run(("first", 0), ("first", 1), ("second", 0), ("second", 1))
    own = [pltpu.make_async_copy(source(part), spot(part, 0, 0), local_sems.at[k])
           for k, part in enumerate((("q", 0, A_ROWS), ("u", 0, A_ROWS), ("b", 0, B_ROWS)))]
    own[0].start()
    for step in range(1, 8):
        vec_copy(step).wait_recv()
    tiles = {}
    counts = jnp.zeros((1, 128), F32)
    for s in range(8):
        value = vecs[s].astype(F32)
        shift_lanes(tiles, value, 0, 136, 136 * s)
        counts = counts + value[COUNTS_ROW : COUNTS_ROW + 1, :128]
    table = join_tiles(tiles, 9)
    lines[...] = table[:8]
    bound_row[...] = counts.astype(jnp.int32)
    bounds = bound_row[...]
    for y in range(4):
        tiles = {}
        for odd in (0, 1):
            value = vecs[2 * y + odd].astype(F32)
            for row in range(4):
                shift_lanes(tiles, value[8 + row : 9 + row], 0, 136, 544 * odd + 136 * row)
        up_row[y] = join_tiles(tiles, 9)[:, :D]
    unit, _ = normalize(hidden[...].astype(F32).reshape(256, D))
    normed = unit * table[0:1, :D] + table[2:3, :D]
    normed_t[...] = normed.T.astype(BF16)
    normed = normed.astype(BF16)
    near.run(("spread", 0), ("spread", 1), ("relay", 0, 0), ("relay", 1, 0))
    for copy in later:
        copy.wait_recv()
    mine_a[:, 512:] = merge_rows(za[:, :, 512:].reshape(320, 640))
    mine_b[...] = merge_columns(zb)
    own[1].start()
    own[2].start()
    near.run(("far", 0), ("far", 1), ("relay", 0, 1), ("relay", 1, 1), ("close", 0, 0),
             ("close", 1, 0), ("relay", 0, 3), ("relay", 1, 3), ("relay", 0, 2), ("relay", 1, 2))
    rest.run(("first", 1), ("first", 0), ("second", 0))
    near.run(*[("close", half, by) for by in (1, 3, 2) for half in (0, 1)], ("settle",))
    own[0].wait()
    kept = pltpu.make_async_copy(weights, gq, local_sems.at[3])
    kept.start()
    tiles = ({}, {}, {})
    for s in range(8):
        block = dot(normed, weights[s])
        for seg, low, width, kind, place in segments():
            if seg == s:
                shift_lanes(tiles[kind], block, low, width, place)
    for kind, row in ((0, 4), (1, None), (2, 5)):
        for p in range(9):
            tile = tiles[kind][p]
            if row is not None:
                tile = tile + table[row : row + 1, 128 * p : 128 * p + 128]
            pack[p, kind] = tile.astype(BF16).reshape(2, 128, 128)

    rest_events = list(LATE)

    def pump():
        if rest_events:
            rest.run(*rest_events.pop(0))

    def in_copy(step):
        return push(pack.at[g.other(step)], got.at[g.seq], in_sems, (step - 1,), g.member(g.other(step)))

    def in8_copy(extra, source):
        return pltpu.make_async_remote_copy(
            src_ref=pack.at[8, :, extra], dst_ref=got8.at[source], send_sem=in8_sems.at[8 + extra],
            recv_sem=in8_sems.at[source], device_id=g.member(4 * extra), device_id_type=MESH)

    for step in (4, 3, 5, 2, 6, 1, 7):
        in_copy(step).start()
    for extra in (0, 1):
        @pl.when(g.seq != 4 * extra)
        def _():
            in8_copy(extra, g.seq).start()

        @pl.when(g.seq == 4 * extra)
        def _():
            got8[g.seq] = pack[8, :, extra]
    got[g.seq] = pack[g.seq]
    rest.run(("spread", 1), ("spread", 0), ("second", 1), ("far", 1), ("far", 0))
    for step in range(1, 8):
        in_copy(step).wait_recv()

    def back_copy(seq, step):
        return push(out.at[g.other(step), seq], att.at[g.seq, seq], back_sems, (seq, step - 1),
                    g.member(g.other(step)))

    def pair(seq):
        def store(block, value):
            out[pl.ds(2 * block, 2), seq] = value
        part = lambda kind: got[:, kind, seq].reshape(1024, 128)
        attend(part(0), part(1), part(2), bounds, seq, 2, store, pump)
        for step in (4, 3, 5, 2, 6, 1, 7):
            back_copy(seq, step).start()

    for seq in (0, 1):
        pair(seq)
    att[g.seq] = out[g.seq]

    def back8_copy(extra, step):
        return pltpu.make_async_remote_copy(
            src_ref=out8.at[g.other(step)], dst_ref=att.at[8, extra], send_sem=back8_sems.at[1 + step],
            recv_sem=back8_sems.at[extra], device_id=g.member(g.other(step)), device_id_type=MESH)

    for extra in (0, 1):
        @pl.when(g.seq == 4 * extra)
        def _():
            for step in range(1, 8):
                in8_copy(extra, g.other(step)).wait_recv()

            def store(block, value):
                out8[pl.ds(2 * block, 2)] = value
            part = lambda kind: got8[:, kind].reshape(1024, 128)
            attend(part(0), part(1), part(2), bounds, extra, 1, store, lambda: None)
            for step in range(1, 8):
                back8_copy(extra, step).start()
            att[8, extra] = out8[g.seq]
            for step in range(1, 8):
                back8_copy(extra, step).wait_send()

        @pl.when(g.seq != 4 * extra)
        def _():
            in8_copy(extra, g.seq).wait_send()
            back8_copy(extra, 1).wait_recv()
    for step in range(1, 8):
        in_copy(step).wait_send()
        for seq in (0, 1):
            back_copy(seq, step).wait_recv()
            back_copy(seq, step).wait_send()
    while rest_events:
        rest.run(*rest_events.pop(0))
    for copy in send.made:
        copy.wait_send()
    for step in range(1, 8):
        vec_copy(step).wait_send()
    own[1].wait()
    own[2].wait()
    kept.wait()


def enter_block(*operands):
    tile = (128, 128)
    vmem = pltpu.VMEM
    shape = jax.ShapeDtypeStruct
    return pl.pallas_call(
        enter_kernel,
        out_shape=(
            shape((8, D, 512), BF16), shape((8, D, 640), BF16), shape((4, 8, B_ROWS, D), BF16),
            shape((9, 2) + tile, BF16), shape((8, 3, 2) + tile, BF16), shape((8, 3) + tile, BF16),
            shape((D, 256), BF16), shape((8, WIDE), F32), shape((4, 1, D), F32),
            shape((1, 128), jnp.int32)),
        in_specs=[pl.BlockSpec(memory_space=vmem)] * 4,
        out_specs=(pl.BlockSpec(memory_space=pl.ANY),) * 3 + (pl.BlockSpec(memory_space=vmem),) * 7,
        scratch_shapes=[
            vmem((8, D, 512), BF16), vmem((4, 80, WIDE), BF16), vmem((4, B_ROWS, 384), BF16),
            vmem((A_ROWS, WIDE), BF16), vmem((B_ROWS, D), BF16), vmem((8, 16, 256), BF16),
            vmem((9, 3, 2) + tile, BF16), vmem((8, 2) + tile, BF16), vmem((8,) + tile, BF16),
            pltpu.SemaphoreType.DMA((GATHER_COPIES,)), pltpu.SemaphoreType.DMA((GATHER_COPIES,)),
            pltpu.SemaphoreType.DMA((4,)), pltpu.SemaphoreType.DMA((2, 7)),
            pltpu.SemaphoreType.DMA((2, 7)), pltpu.SemaphoreType.DMA((10,)),
            pltpu.SemaphoreType.DMA((2, 2, 7)), pltpu.SemaphoreType.DMA((9,))],
        compiler_params=pltpu.CompilerParams(
            collective_id=1, has_side_effects=True, vmem_limit_bytes=60 * 2**20),
    )(*operands)


def attend_pull(queries, keys, values, grads, bounds, seq, heads, key_sum, value_sum, store, pump):
    queries = queries * 0.125
    key_t = turned(keys).astype(BF16)
    key_sum[...] = jnp.zeros_like(key_sum)
    value_sum[...] = jnp.zeros_like(value_sum)
    for block in range(4):
        rows = slice(block * 256, block * 256 + 256)
        size = block * 256 + 256
        parts = []
        for head in range(heads):
            query, grad = head_part(queries[rows], head), head_part(grads[rows], head)
            probs = chances(keys[:size], query, bounds, seq, block)
            change = lax.dot_general(values[:size], grad, NT, preferred_element_type=F32)
            inner = jnp.sum(probs * change, axis=0, keepdims=True)
            slope = (probs * (change - inner)).astype(BF16)
            value_sum[:size] += jnp.dot(probs.astype(BF16), grad, preferred_element_type=F32)
            key_sum[:size] += jnp.dot(slope, query, preferred_element_type=F32)
            parts.append(dot(key_t[:, :size], slope))
            pump()
        whole = parts[0] if heads == 1 else jnp.concatenate([parts[0][:64], parts[1][64:]], axis=0)
        store(0, block, (whole.T * 0.125).astype(BF16).reshape(2, 128, 128))
    for kind, total in ((1, key_sum), (2, value_sum)):
        for block in range(4):
            store(kind, block, total[block * 256 : block * 256 + 256].astype(BF16).reshape(2, 128, 128))


def pull_kernel(pack, got, got8, hidden, middle_grad, lines, bound_row, x_o, x_u, y_o, y_u, tt, act,
                sums, up_sums, ga, placed, input_grad, extra, block_u, block_b,
                weights, back, grad, grad8, out, out8, key_sum, value_sum,
                weight_sems, in_sems, in8_sems, back_sems, back8_sems, *refs):
    g = Place()
    bounds = bound_row[...]
    greet(all_peers(g))

    def part_u(column, y):
        rows = pl.ds(pl.multiple_of(y * A_ROWS, 16), A_ROWS)
        three = dot(x_u[rows], y_u[column])
        two = dot(x_o[rows], y_o[column, :, 128:256])
        return jnp.concatenate([three[:, :128] + two, three[:, 128:]], axis=1)

    def part_b(column, y):
        return dot(tt[column], act[y])

    reduce = make_reduce(g, refs, ((part_u, A_ROWS, 128), (part_b, B_ROWS, 64)))
    plan = {1: lambda: reduce.cross(0, 3), 14: reduce.own}
    ticks = [0]

    def pump():
        ticks[0] += 1
        if ticks[0] in plan:
            plan[ticks[0]]()

    def fetch(s):
        return pltpu.make_async_copy(ga.at[s], weights.at[s % 2], weight_sems.at[s % 2])

    fetch(0).start()
    fetch(1).start()

    def in_copy(step):
        return push(pack.at[g.other(step)], grad.at[g.seq], in_sems, (step - 1,), g.member(g.other(step)))

    def in8_copy(which, source):
        return pltpu.make_async_remote_copy(
            src_ref=pack.at[8, which], dst_ref=grad8.at[source], send_sem=in8_sems.at[8 + which],
            recv_sem=in8_sems.at[source], device_id=g.member(4 * which), device_id_type=MESH)

    for step in (4, 3, 5, 2, 6, 1, 7):
        in_copy(step).start()
    for which in (0, 1):
        @pl.when(g.seq != 4 * which)
        def _():
            in8_copy(which, g.seq).start()

        @pl.when(g.seq == 4 * which)
        def _():
            grad8[g.seq] = pack[8, which]
    grad[g.seq] = pack[g.seq]
    reduce.cross(2, None)
    reduce.opposite()
    reduce.cross(1, 2)
    reduce.cross(3, 1)
    reduce.sides(0)
    reduce.sides(1)
    for step in range(1, 8):
        in_copy(step).wait_recv()

    def back_copy(seq, step):
        return push(out.at[g.other(step), seq], back.at[g.seq, seq], back_sems, (seq, step - 1),
                    g.member(g.other(step)))

    def pair(seq, carry):
        def store(kind, block, value):
            out[pl.ds(2 * block, 2), seq, kind] = value
        part = lambda kind: got[:, kind, seq].reshape(1024, 128)
        attend_pull(part(0), part(1), part(2), grad[:, seq].reshape(1024, 128), bounds, seq, 2,
                    key_sum, value_sum, store, pump)
        for step in (4, 3, 5, 2, 6, 1, 7):
            back_copy(seq, step).start()
        return carry

    for seq in (0, 1):
        pair(seq, 0)
    back[g.seq] = out[g.seq]

    def back8_copy(which, step):
        return pltpu.make_async_remote_copy(
            src_ref=out8.at[g.other(step)], dst_ref=back.at[8, which], send_sem=back8_sems.at[1 + step],
            recv_sem=back8_sems.at[which], device_id=g.member(g.other(step)), device_id_type=MESH)

    for which in (0, 1):
        @pl.when(g.seq == 4 * which)
        def _():
            for step in range(1, 8):
                in8_copy(which, g.other(step)).wait_recv()

            def store(kind, block, value):
                out8[pl.ds(2 * block, 2), kind] = value
            part = lambda kind: got8[:, kind].reshape(1024, 128)
            attend_pull(part(0), part(1), part(2), grad8[...].reshape(1024, 128), bounds, which, 1,
                        key_sum, value_sum, store, lambda: None)
            for step in range(1, 8):
                back8_copy(which, step).start()
            back[8, which] = out8[g.seq]
            for step in range(1, 8):
                back8_copy(which, step).wait_send()

        @pl.when(g.seq != 4 * which)
        def _():
            in8_copy(which, g.seq).wait_send()
            back8_copy(which, 1).wait_recv()
    reduce.middle()
    for step in range(1, 8):
        in_copy(step).wait_send()
        for seq in (0, 1):
            back_copy(seq, step).wait_recv()
            back_copy(seq, step).wait_send()

    natural = [jnp.concatenate([back[p, :, kind].reshape(256, 128) for p in range(9)],
                               axis=1).astype(F32) for kind in range(3)]
    total = None
    for s in range(8):
        tiles = {}
        for seg, low, width, kind, spot in segments():
            if seg == s:
                shift_lanes(tiles, natural[kind], spot, width, low)
        block = join_tiles(tiles, 4).astype(BF16)
        placed[s] = block
        fetch(s).wait()
        term = dot_t(block, weights[s % 2])
        if s < 6:
            fetch(s + 2).start()
        total = term if total is None else total + term
    reduce.last()
    unit, scale = normalize(hidden[...].astype(F32).reshape(256, D))
    input_grad[...] = middle_grad[...] + norm_pull(total, lines[0:1, :D], unit, scale)

    def column_sum(value):
        return jnp.sum(value, axis=0, keepdims=True)

    table = jnp.concatenate([
        column_sum(widen(total * unit)), sums[0:1], column_sum(widen(total)), sums[1:2],
        column_sum(natural[0]), column_sum(natural[2]), sums[2:4]], axis=0)
    for s in range(8):
        tiles = {}
        shift_lanes(tiles, table, 136 * s, 136, 0)
        first = join_tiles(tiles, 4)
        rows = []
        for row in range(4):
            tiles = {}
            shift_lanes(tiles, up_sums[s], 32 + 136 * row, 136, 136)
            rows.append(join_tiles(tiles, 4))
        second = jnp.concatenate(rows + [jnp.zeros((4, 512), F32)], axis=0)
        extra[s] = jnp.concatenate([first + second, jnp.zeros((8, 512), F32)], axis=0)
    block_u[...] = reduce.result(0).astype(BF16)
    block_b[...] = reduce.result(1).astype(BF16)
    reduce.drain()


def attend_backward(*operands):
    tile = (128, 128)
    vmem = pltpu.VMEM
    return pl.pallas_call(
        pull_kernel,
        out_shape=(jax.ShapeDtypeStruct((8, 256, 512), BF16),
                   jax.ShapeDtypeStruct((256, D), F32), jax.ShapeDtypeStruct((8, 16, 512), F32),
                   jax.ShapeDtypeStruct((A_ROWS, 640), BF16), jax.ShapeDtypeStruct((B_ROWS, D), BF16)),
        in_specs=[pl.BlockSpec(memory_space=vmem)] * 15 + [pl.BlockSpec(memory_space=pl.ANY)],
        out_specs=(pl.BlockSpec(memory_space=vmem),) * 5,
        scratch_shapes=[
            vmem((2, D, 512), BF16), vmem((9, 2, 3) + tile, BF16), vmem((8, 2) + tile, BF16), vmem((8,) + tile, BF16),
            vmem((8, 2, 3) + tile, BF16), vmem((8, 3) + tile, BF16),
            vmem((1024, 128), F32), vmem((1024, 128), F32),
            pltpu.SemaphoreType.DMA((2,)),
            pltpu.SemaphoreType.DMA((2, 7)), pltpu.SemaphoreType.DMA((10,)),
            pltpu.SemaphoreType.DMA((2, 2, 7)), pltpu.SemaphoreType.DMA((9,)),
        ] + reduce_scratch(((A_ROWS, 640), (B_ROWS, D))),
        compiler_params=pltpu.CompilerParams(
            collective_id=2, has_side_effects=True, vmem_limit_bytes=63 * 2**20),
    )(*operands)


def middle_kernel(att, hidden, top, lines, up_row, gq, gu, gb,
                  layer_out, middle_grad, att_grad, att_t, normed_t, active, y_o, y_u, sums, up_sums, top_t,
                  held_o, held_u, held_b, normed, down_sum, norm_grad, top_pad, sems_o, sems_u, sems_b):
    copies_o = []
    for s in range(8):
        copies_o.append(pltpu.make_async_copy(
            gq.at[s, :, pl.ds(384, 128)], held_o.at[s, :, pl.ds(0, 128)], sems_o.at[0, s]))
        copies_o.append(pltpu.make_async_copy(
            gu.at[s, :, pl.ds(0, 128)], held_o.at[s, :, pl.ds(128, 128)], sems_o.at[1, s]))
    for copy in copies_o:
        copy.start()

    def up_copy(s):
        return pltpu.make_async_copy(gu.at[s], held_u.at[s], sems_u.at[s])

    def down_copy(y):
        return pltpu.make_async_copy(gb.at[y], held_b.at[y], sems_b.at[y])

    for y in range(4):
        up_copy(2 * y).start()
        up_copy(2 * y + 1).start()
        down_copy(y).start()

    tiles = {}
    for s in range(8):
        shift_lanes(tiles, widen(top[...].reshape(256, D)).astype(F32), 136 * s, 136, 144 * s)
    padded = join_tiles(tiles, 9)
    top_pad[...] = padded.astype(BF16)
    top_t[...] = padded.T.astype(BF16).reshape(8, B_ROWS, 256)
    attended = jnp.concatenate([att[p].reshape(256, 128) for p in range(9)], axis=1)
    att_t[...] = attended.astype(F32).T[:D].astype(BF16)
    tiles = {}
    for s in range(8):
        copies_o[2 * s].wait()
        copies_o[2 * s + 1].wait()
        shift_lanes(tiles, dot(attended[:, :D], held_o[s]), 24, 136, 136 * s)
    branch = join_tiles(tiles, 9)[:, :D]
    middle = hidden[...].astype(F32).reshape(256, D) + branch + lines[6:7, :D]
    unit, scale = normalize(middle)
    value = unit * lines[1:2, :D] + lines[3:4, :D]
    normed[...] = value.astype(BF16)
    normed_t[...] = value.T.astype(BF16)
    down_sum[...] = jnp.zeros_like(down_sum)
    norm_grad[...] = jnp.zeros_like(norm_grad)

    def step(y, carry):
        tiles = {}
        for odd in (0, 1):
            up_copy(2 * y + odd).wait()
            shift_lanes(tiles, dot(normed[...], held_u[2 * y + odd]), 32, 544, 544 * odd)
        pre = join_tiles(tiles, 9)[:, :D] + up_row[y]
        cube = 0.7978845608028654 * (pre + 0.044715 * (pre * pre * pre))
        bend = jnp.tanh(cube)
        half = 0.5 * (1.0 + bend)
        acts = (pre * half).astype(BF16)
        slope = half + 0.5 * pre * (1.0 - bend * bend) * (
            0.7978845608028654 * (1.0 + 3 * 0.044715 * (pre * pre)))
        active[y] = acts
        down_copy(y).wait()
        weights = held_b[y].reshape(8 * B_ROWS, D)
        down_sum[...] += dot_t(acts, weights)
        inner = dot(top_pad[...], weights) * slope
        inner = widen(inner.astype(BF16).astype(F32))
        total = None
        for odd in (0, 1):
            tiles = {}
            shift_lanes(tiles, inner, 544 * odd, 544, 32)
            block = join_tiles(tiles, 5)
            up_sums[2 * y + odd] = jnp.sum(block, axis=0, keepdims=True)
            block = block.astype(BF16)
            y_u[2 * y + odd] = block
            term = dot_t(block, held_u[2 * y + odd])
            total = term if total is None else total + term
        norm_grad[...] += total
        return carry

    lax.fori_loop(0, 4, step, 0)
    tiles = {}
    down = down_sum[...]
    for s in range(8):
        shift_lanes(tiles, down, 144 * s, 136, 136 * s)
    out = middle + join_tiles(tiles, 9)[:, :D] + lines[7:8, :D]
    layer_out[...] = out.astype(BF16).reshape(2, 128, D)
    grad = norm_grad[...]
    cotangent = top[...].astype(F32).reshape(256, D)
    total = cotangent + norm_pull(grad, lines[1:2, :D], unit, scale)
    middle_grad[...] = total
    branch = widen(total.astype(BF16).astype(F32))
    back = None
    for s in range(8):
        tiles = {}
        shift_lanes(tiles, branch, 136 * s, 136, 24)
        block = join_tiles(tiles, 2).astype(BF16)
        y_o[s] = block
        term = dot_t(block, held_o[s])
        back = term if back is None else back + term
    back = widen(back).astype(BF16)
    for p in range(9):
        att_grad[p] = back[:, 128 * p : 128 * p + 128].reshape(2, 128, 128)
    sums[0:1] = jnp.sum(widen(grad * unit), axis=0, keepdims=True)
    sums[1:2] = jnp.sum(widen(grad), axis=0, keepdims=True)
    sums[2:3] = jnp.sum(branch, axis=0, keepdims=True)
    sums[3:4] = jnp.sum(widen(cotangent), axis=0, keepdims=True)
    sums[4:8] = jnp.zeros((4, WIDE), F32)


def middle_block(*operands):
    vmem = pltpu.VMEM
    shape = jax.ShapeDtypeStruct
    return pl.pallas_call(
        middle_kernel,
        out_shape=(
            shape((2, 128, D), BF16), shape((256, D), F32), shape((9, 2, 128, 128), BF16),
            shape((D, 256), BF16), shape((D, 256), BF16), shape((4, 256, D), BF16),
            shape((8, 256, 256), BF16), shape((8, 256, 640), BF16), shape((8, WIDE), F32),
            shape((8, 1, 640), F32), shape((8, B_ROWS, 256), BF16)),
        in_specs=[pl.BlockSpec(memory_space=vmem)] * 5 + [pl.BlockSpec(memory_space=pl.ANY)] * 3,
        out_specs=(pl.BlockSpec(memory_space=vmem),) * 11,
        scratch_shapes=[
            vmem((8, D, 256), BF16), vmem((8, D, 640), BF16), vmem((4, 8, B_ROWS, D), BF16),
            vmem((256, D), BF16), vmem((256, WIDE), F32), vmem((256, D), F32), vmem((256, WIDE), BF16),
            pltpu.SemaphoreType.DMA((2, 8)), pltpu.SemaphoreType.DMA((8,)),
            pltpu.SemaphoreType.DMA((4,))],
        compiler_params=pltpu.CompilerParams(vmem_limit_bytes=62 * 2**20),
    )(*operands)


def per_device(
    inputs, out_grad, segment_ids, qkv_weight, out_weight, up_weight, down_weight,
    norm_gains, norm_shifts, qv_bias, proj_bias, up_bias,
):
    seqs, rows, _ = inputs.shape

    blob_a = jnp.concatenate([qkv_weight, out_weight, up_weight], axis=1)
    blob_a = jnp.pad(blob_a, ((0, 12), (0, WIDE - D)))
    counts = jnp.sum(segment_ids[:, :, None] < jnp.arange(1, 4)[None, None, :], axis=1)
    counts = jnp.pad(counts.astype(BF16).reshape(1, 6), ((0, 3), (0, 130)))
    vec = jnp.concatenate(
        [norm_gains, norm_shifts, qv_bias, proj_bias, up_bias.reshape(4, 136), counts], axis=0
    )
    vec = jnp.pad(vec, ((0, 0), (0, 120)))
    blob_b = jnp.pad(down_weight.T, ((0, 8), (0, 112)))

    (w_q, w_u, w_b, att, got, got8, normed_t, lines, up_row, bounds) = enter_block(
        blob_a, blob_b, vec, inputs
    )
    (layer_out, middle_grad, att_grad, att_t, normed_two_t, active, y_o, y_u, sums, up_sums, top_t) = (
        middle_block(att, inputs, out_grad, lines, up_row, w_q, w_u, w_b)
    )
    y_q, input_grad, extra, block_u, block_b = attend_backward(
        att_grad, got, got8, inputs, middle_grad, lines, bounds, att_t, normed_two_t, y_o, y_u,
        top_t, active, sums, up_sums, w_q
    )
    out_a, out_b = leave_block(normed_t, att_t, y_q, y_o, extra, block_u, block_b)
    return (
        layer_out,
        input_grad.reshape(seqs, rows, D),
        out_a[:68, :408],
        out_a[:68, 408:544],
        out_a[:68, 544:D],
        out_b[:136, :272].T,
        out_b[136:138, :136],
        out_b[138:140, :136],
        out_b[140:142, :136],
        out_b[142:144, :136],
        out_b[136:140, 136:272].reshape(1, 544),
    )


def solution(mesh):
    tokens = P("batch", "seq", None)
    matrix = P("batch", "seq")
    vector = P(None, "seq")
    return jax.shard_map(
        per_device,
        mesh=mesh,
        in_specs=(tokens, tokens, matrix, matrix, matrix, matrix, matrix) + (vector,) * 5,
        out_specs=(tokens, tokens, matrix, matrix, matrix, matrix) + (vector,) * 5,
        check_vma=False,
    )
```

```python
import jax
import jax.numpy as jnp
from jax import lax
from jax.experimental import pallas as pl
from jax.experimental.pallas import tpu as pltpu
from jax.sharding import PartitionSpec as P

D = 1088
WIDE = 1152
F32 = jnp.float32
BF16 = jnp.bfloat16
MESH = pl.DeviceIdType.MESH
A_ROWS, B_ROWS = 272, 144
CUT = 208


class Place:
    def __init__(self):
        batch, seq = lax.axis_index("batch"), lax.axis_index("seq")
        self.batch, self.seq = batch, seq
        self.y, self.z = batch // 4, batch % 4
        self.x, self.c = seq // 2, seq % 2
        self.sibling = {"batch": batch, "seq": self.x * 2 + 1 - self.c}

    def other(self, step):
        return (self.seq + step) % 8

    def member(self, seq):
        return {"batch": self.batch, "seq": seq}

    def peer(self, axis, step):
        spot = {"x": self.x, "y": self.y, "z": self.z}
        spot[axis] = (spot[axis] + step + 4) % 4
        return {"batch": spot["y"] * 4 + spot["z"], "seq": spot["x"] * 2 + self.c}


def greet(peers):
    barrier = pltpu.get_barrier_semaphore()
    for peer in peers:
        pl.semaphore_signal(barrier, inc=1, device_id=peer, device_id_type=MESH)
    pl.semaphore_wait(barrier, len(peers))


def all_peers(me):
    return [me.member(me.other(step)) for step in range(1, 8)] + [me.peer(axis, step) for axis, step in (
        ("y", 1), ("y", 3), ("z", 1), ("z", 2), ("z", 3))]


class Sender:
    def __init__(self, send_sems, recv_sems):
        self.send_sems, self.recv_sems, self.made = send_sems, recv_sems, []

    def __call__(self, source, target, peer):
        index = len(self.made)
        copy = pltpu.make_async_remote_copy(
            src_ref=source, dst_ref=target, send_sem=self.send_sems.at[index],
            recv_sem=self.recv_sems.at[index], device_id=peer, device_id_type=MESH)
        copy.start()
        self.made.append(copy)
        return copy


EARLY = [("first", 1), ("first", 0), ("second", 0)]
LATE = {
    0: [("spread", 1), ("second", 2), ("first", 2), ("second", 1), ("spread", 0), ("relay", 0, 0), ("far", 1), ("relay", 2, 0), ("relay", 0, 1)],
    4: [("relay", 1, 1)],
    5: [("relay", 0, 3)],
    6: [("relay", 1, 3), ("spread", 2), ("close", 0, 0), ("close", 2, 0)],
    7: [("close", 0, 1), ("relay", 1, 0)],
    8: [("close", 0, 3)],
    9: [("far", 0), ("relay", 2, 1)],
    11: [("relay", 1, 2), ("relay", 2, 3)],
    12: [("close", 1, 1)],
    13: [("close", 1, 3)],
    14: [("far", 2), ("relay", 0, 2), ("close", 2, 1), ("close", 1, 0), ("close", 2, 3)],
    16: [("relay", 2, 2), ("close", 1, 2), ("close", 0, 2), ("close", 2, 2)],
}


def merge_rows(stacked):
    row = lax.broadcasted_iota(jnp.int32, (A_ROWS, 320), 0)
    col = lax.broadcasted_iota(jnp.int32, (A_ROWS, 320), 1)
    pick = jnp.where(col == row + 12 * (row // 68), 1.0, 0.0).astype(BF16)
    return jnp.dot(pick, stacked, preferred_element_type=F32).astype(BF16)


def merge_columns(slots):
    total = None
    for z in range(4):
        row = lax.broadcasted_iota(jnp.int32, (384, D), 0)
        col = lax.broadcasted_iota(jnp.int32, (384, D), 1)
        pick = jnp.where((col == row + 272 * z) & (row < 272), 1.0, 0.0).astype(BF16)
        term = jnp.dot(slots[z], pick, preferred_element_type=F32)
        total = term if total is None else total + term
    return total.astype(BF16)

AXES = {0: ("x", "y"), 1: ("y", "x")}


class Rings:
    def __init__(self, me, send, axes, whole, split, source, spot):
        self.me, self.send, self.axes, self.whole, self.split = me, send, axes, whole, split
        self.source, self.spot, self.crossed, self.sent = source, spot, [], {}

    def move(self, axis, steps, by):
        if axis == "x":
            return ((steps[0] + by) % 4, steps[1])
        return (steps[0], (steps[1] + by) % 4)

    def push(self, part, steps, peer):
        source = self.source if steps == (0, 0) else lambda part: self.spot(part, *steps)
        return self.send(source(part), self.spot(part, *steps), peer)

    def cross(self, half, steps):
        self.crossed.append(self.push(self.whole[half], steps, self.me.sibling))

    def begin(self, half, axis, steps):
        return {by: self.push(self.whole[half], steps, self.me.peer(axis, by)) for by in (1, 3)}

    def forward(self, half, axis, steps, sent, flip):
        ends = []
        for by, which in ((1, flip), (3, 1 - flip)):
            origin = self.move(axis, steps, -by)
            sent[by].wait_recv()
            ends.append(self.push(self.split[half][which], origin, self.me.peer(axis, by)))
        return ends

    def arrived(self, half, axis, steps):
        for by in (1, 3):
            self.cross(half, self.move(axis, steps, by))

    def finish(self, half, axis, steps, ends):
        for copy in ends:
            copy.wait_recv()
        self.cross(half, self.move(axis, steps, 2))

    def first(self, half):
        self.sent[half] = self.begin(half, self.axes[half][0], (0, 0))

    def second(self, half):
        self.sent[half, 0] = self.begin(half, self.axes[half][1], (0, 0))
        self.cross(half, (0, 0))

    def spread(self, half):
        axis = self.axes[half][0]
        self.sent[half, "far"] = self.forward(half, axis, (0, 0), self.sent[half], half % 2)
        for by in (1, 3):
            self.sent[half, by] = self.begin(half, self.axes[half][1], self.move(axis, (0, 0), by))
        self.arrived(half, axis, (0, 0))

    def far(self, half):
        axis = self.axes[half][0]
        self.finish(half, axis, (0, 0), self.sent[half, "far"])
        self.sent[half, 2] = self.begin(half, self.axes[half][1], self.move(axis, (0, 0), 2))

    def relay(self, half, by):
        steps = self.move(self.axes[half][0], (0, 0), by)
        self.sent[half, by, "end"] = self.forward(
            half, self.axes[half][1], steps, self.sent[half, by], by % 2)
        self.arrived(half, self.axes[half][1], steps)

    def close(self, half, by):
        steps = self.move(self.axes[half][0], (0, 0), by)
        self.finish(half, self.axes[half][1], steps, self.sent[half, by, "end"])

    def settle(self):
        for copy in self.crossed:
            copy.wait_recv()

    def run(self, *actions):
        for name, *rest in actions:
            getattr(self, name)(*rest)


NT = (((1,), (1,)), ((), ()))


def normalize(values):
    center = values - jnp.mean(values, axis=-1, keepdims=True)
    spread = jnp.mean(center * center, axis=-1, keepdims=True)
    scale = lax.rsqrt(spread + 1e-05)
    return center * scale, scale


def norm_pull(grad, gain, unit, scale):
    scaled = grad * gain
    return scale * (
        scaled
        - jnp.mean(scaled, axis=-1, keepdims=True)
        - unit * jnp.mean(scaled * unit, axis=-1, keepdims=True)
    )


def dot(left, right):
    return jnp.dot(left, right, preferred_element_type=F32)


def dot_t(left, right):
    return lax.dot_general(left, right, NT, preferred_element_type=F32)


def widen(value):
    return jnp.concatenate([value, jnp.zeros((value.shape[0], WIDE - D), value.dtype)], axis=1)


def shift_lanes(tiles, value, source, width, target):
    turn = (target - source) % 128
    low, high = source // 128, -(-(source + width) // 128)
    part = value[:, low * 128 : high * 128]
    if turn:
        part = jnp.concatenate([part, jnp.zeros((part.shape[0], 128), part.dtype)], axis=1)
        part = pltpu.roll(part, turn, 1)
    start = source - low * 128 + turn
    for spot in range(start // 128, -(-(start + width) // 128)):
        tile = part[:, spot * 128 : spot * 128 + 128]
        first, last = start - spot * 128, start + width - spot * 128
        if first > 0 or last < 128:
            lane = lax.broadcasted_iota(jnp.int32, tile.shape, 1)
            tile = jnp.where((lane >= first) & (lane < last), tile, 0.0)
        place = (target - start) // 128 + spot
        tiles[place] = tiles[place] + tile if place in tiles else tile


def join_tiles(tiles, count):
    rows = next(iter(tiles.values())).shape[0]
    empty = jnp.zeros((rows, 128), F32)
    return jnp.concatenate([tiles.get(k, empty) for k in range(count)], axis=1)


def segments():
    found = []
    for s in range(8):
        for kind in range(3):
            low, high = max(408 * s, D * kind), min(408 * s + 408, D * kind + D)
            if low < high:
                found.append((s, low - 408 * s, high - low, kind, low - D * kind))
    return found


class Reduce:
    def __init__(self, me, blocks, sib_sems, opp_sems, side_sems, mid_sems, end_sems):
        self.me, self.blocks = me, blocks
        self.sib_sems, self.opp_sems, self.side_sems = sib_sems, opp_sems, side_sems
        self.mid_sems, self.end_sems = mid_sems, end_sems

    def copy(self, source, target, sems, index, peer):
        return pltpu.make_async_remote_copy(
            src_ref=source, dst_ref=target, send_sem=sems.at[(0,) + index],
            recv_sem=sems.at[(1,) + index], device_id=peer, device_id_type=MESH)

    def part(self, half, step, o, parity):
        b = self.blocks[half]
        along, beside = (self.me.x, self.me.y) if half == 0 else (self.me.y, self.me.x)
        first, second = (along + step) % 4, (beside + o) % 4
        x, y = (first, second) if half == 0 else (second, first)
        return b["part"](2 * x + parity, y)

    def ends_of(self, half, which):
        b = self.blocks[half]
        return pl.ds(0, b["cut"]) if which == 0 else pl.ds(b["cut"], b["rows"] - b["cut"])

    def beside(self, half, stage, which):
        return self.me.peer(AXES[half][stage], 1 if which == 0 else 3)

    def sib_copy(self, half, step, o):
        b = self.blocks[half]
        return self.copy(b["sib_out"].at[o], b["sib_in"].at[step, o], self.sib_sems,
                         (half, step, o), self.me.sibling)

    def opp_copy(self, half, o, which):
        b = self.blocks[half]
        rows = self.ends_of(half, which)
        return self.copy(b["sib_in"].at[2, o, rows], b["in_opp"].at[o, rows], self.opp_sems,
                         (half, o, which), self.beside(half, 0, which))

    def side_copy(self, half, o, which):
        b = self.blocks[half]
        return self.copy(b["sib_in"].at[1 + 2 * which, o], b["in_side"].at[which, o],
                         self.side_sems, (half, o, which), self.beside(half, 0, which))

    def mid_copy(self, half, which):
        b = self.blocks[half]
        rows = self.ends_of(half, which)
        return self.copy(b["sib_out"].at[2, rows], b["in_mid"].at[rows], self.mid_sems,
                         (half, which), self.beside(half, 1, which))

    def end_copy(self, half, which):
        b = self.blocks[half]
        return self.copy(b["sib_out"].at[which], b["in_end"].at[which], self.end_sems,
                         (half, which), self.beside(half, 1, which))

    def loop(self, body):
        lax.fori_loop(0, 4, lambda o, carry: (body(o), carry)[1], 0)

    def cross(self, step, before):
        def body(o):
            for half in (0, 1):
                if before is not None:
                    self.sib_copy(half, before, o).wait_send()
                self.blocks[half]["sib_out"][o] = self.part(half, step, o, 1 - self.me.c).astype(BF16)
                self.sib_copy(half, step, o).start()
        self.loop(body)

    def mine(self, half, step, o):
        value = self.part(half, step, o, self.me.c)
        self.sib_copy(half, step, o).wait_recv()
        return value + self.blocks[half]["sib_in"][step, o].astype(F32)

    def opposite(self):
        def body(o):
            for half in (0, 1):
                self.blocks[half]["sib_in"][2, o] = self.mine(half, 2, o).astype(BF16)
                for which in (0, 1):
                    self.opp_copy(half, o, which).start()
        self.loop(body)

    def join(self, half, value, arrived, which):
        cut = self.blocks[half]["cut"]
        if which == 0:
            return jnp.concatenate([value[:cut] + arrived[:cut].astype(F32), value[cut:]], axis=0)
        return jnp.concatenate([value[:cut], value[cut:] + arrived[cut:].astype(F32)], axis=0)

    def sides(self, which):
        def body(o):
            for half in (0, 1):
                b = self.blocks[half]
                value = self.mine(half, 1 + 2 * which, o)
                self.opp_copy(half, o, which).wait_recv()
                value = self.join(half, value, b["in_opp"].at[o], which)
                b["sib_in"][1 + 2 * which, o] = value.astype(BF16)
                self.side_copy(half, o, which).start()
        self.loop(body)

    def own(self):
        def body(o):
            for half in (0, 1):
                b = self.blocks[half]
                value = self.mine(half, 0, o)
                for which in (0, 1):
                    self.side_copy(half, o, which).wait_recv()
                    value = value + b["in_side"][which, o].astype(F32)
                b["acc"][o] = value
        self.loop(body)

    def middle(self):
        def body(o):
            for half in (0, 1):
                self.sib_copy(half, 0, o).wait_send()
        self.loop(body)
        for half in (0, 1):
            b = self.blocks[half]
            b["sib_out"][2] = b["acc"][2].astype(BF16)
            for which in (0, 1):
                self.mid_copy(half, which).start()

    def last(self):
        for half in (0, 1):
            b = self.blocks[half]
            for which in (0, 1):
                value = b["acc"][1 + 2 * which]
                self.mid_copy(half, which).wait_recv()
                b["sib_out"][which] = self.join(half, value, b["in_mid"], which).astype(BF16)
                self.end_copy(half, which).start()

    def result(self, half):
        b = self.blocks[half]
        value = b["acc"][0]
        for which in (0, 1):
            self.end_copy(half, which).wait_recv()
            value = value + b["in_end"][which].astype(F32)
        return value

    def drain(self):
        def body(o):
            for half in (0, 1):
                for which in (0, 1):
                    self.opp_copy(half, o, which).wait_send()
                    self.side_copy(half, o, which).wait_send()
        self.loop(body)
        for half in (0, 1):
            for which in (0, 1):
                self.mid_copy(half, which).wait_send()
                self.end_copy(half, which).wait_send()


REDUCE_BUFFERS = ("sib_out", "sib_in", "in_opp", "in_side", "acc", "in_end", "in_mid")


def reduce_scratch(shapes):
    found = []
    for shape in shapes:
        for lead, kind in (((4,), BF16), ((4, 4), BF16), ((4,), BF16), ((2, 4), BF16), ((4,), F32),
                           ((2,), BF16), ((), BF16)):
            found.append(pltpu.VMEM(lead + shape, kind))
    return found + [pltpu.SemaphoreType.DMA((2, 2, 4, 4)), pltpu.SemaphoreType.DMA((2, 2, 4, 2)),
                    pltpu.SemaphoreType.DMA((2, 2, 4, 2)), pltpu.SemaphoreType.DMA((2, 2, 2)),
                    pltpu.SemaphoreType.DMA((2, 2, 2))]


REDUCE_REFS = 2 * len(REDUCE_BUFFERS) + 5


def make_reduce(me, refs, settings):
    blocks = {}
    count = len(REDUCE_BUFFERS)
    for half in (0, 1):
        part, rows, cut = settings[half]
        blocks[half] = dict(zip(REDUCE_BUFFERS, refs[half * count : half * count + count]))
        blocks[half].update(part=part, rows=rows, cut=cut)
    return Reduce(me, blocks, *refs[2 * count :])


def leave_kernel(x_q, x_o, y_q, y_o, extra, block_u, block_b, out_a, out_b,
                 zout_q, zout_u, zout_b, zin_q, zin_u, zin_b, z_sems, *refs):
    me = Place()
    greet(all_peers(me))

    def upper(column, y):
        return rows_of(column, pl.ds(pl.multiple_of(y * A_ROWS, 16), 144))

    def rows_of(column, rows):
        one = dot(x_q[rows], y_q[column])
        two = dot(x_o[rows], y_o[column, :, 0:128])
        return jnp.concatenate([one[:, :384], one[:, 384:] + two], axis=1)

    def lower(column, y):
        rows = pl.ds(pl.multiple_of(y * A_ROWS + 144, 16), 128)
        return jnp.concatenate([rows_of(column, rows), extra[column]], axis=0)

    reduce = make_reduce(me, refs, ((upper, 144, 64), (lower, 144, 64)))

    def pick_rows(z):
        row = lax.broadcasted_iota(jnp.int32, (80, A_ROWS), 0)
        col = lax.broadcasted_iota(jnp.int32, (80, A_ROWS), 1)
        return jnp.where((col == row + 68 * z) & (row < 68), 1.0, 0.0).astype(BF16)

    def pick_columns(z):
        row = lax.broadcasted_iota(jnp.int32, (D, 384), 0)
        col = lax.broadcasted_iota(jnp.int32, (D, 384), 1)
        return jnp.where((row == col + 272 * z) & (col < 272), 1.0, 0.0).astype(BF16)

    buffers = ((zout_q, zin_q), (zout_u, zin_u), (zout_b, zin_b))

    def z_copy(kind, step):
        source, target = buffers[kind]
        return reduce.copy(source.at[step - 1], target.at[step - 1], z_sems, (kind, step - 1),
                           me.peer("z", step))

    def early(step):
        z = (me.z + step) % 4
        zout_u[step - 1] = dot(pick_rows(z), block_u[...]).astype(BF16)
        zout_b[step - 1] = dot(block_b[...], pick_columns(z)).astype(BF16)
        z_copy(1, step).start()
        z_copy(2, step).start()

    reduce.cross(2, None)
    reduce.opposite()
    reduce.cross(1, 2)
    reduce.cross(3, 1)
    early(2)
    reduce.sides(0)
    reduce.sides(1)
    reduce.cross(0, 3)
    early(1)
    early(3)
    reduce.own()
    reduce.middle()
    reduce.last()
    first, second = reduce.result(0), reduce.result(1)
    block_q = jnp.concatenate([first, second[:128]], axis=0).astype(BF16)
    payload = second[128:]

    def slices(z):
        return jnp.concatenate([dot(pick_rows(z), block_q), payload], axis=0)

    for step in (2, 1, 3):
        zout_q[step - 1] = slices((me.z + step) % 4).astype(BF16)
        z_copy(0, step).start()
    near = slices(me.z)
    above = dot(pick_rows(me.z), block_u[...])
    below = dot(block_b[...], pick_columns(me.z))
    for step in (1, 2, 3):
        z_copy(1, step).wait_recv()
        z_copy(2, step).wait_recv()
        above = above + zin_u[step - 1].astype(F32)
        below = below + zin_b[step - 1].astype(F32)
    for step in (1, 2, 3):
        z_copy(0, step).wait_recv()
        near = near + zin_q[step - 1].astype(F32)
    out_a[:, :512] = near[:80]
    out_a[:, 512:] = above
    out_b[:136] = below[:136]
    out_b[136:] = near[80:88, :384]
    reduce.drain()
    for step in (1, 2, 3):
        for kind in range(3):
            z_copy(kind, step).wait_send()


def leave_block(*operands):
    vmem = pltpu.VMEM
    return pl.pallas_call(
        leave_kernel,
        out_shape=(jax.ShapeDtypeStruct((80, WIDE), F32), jax.ShapeDtypeStruct((B_ROWS, 384), F32)),
        in_specs=[pl.BlockSpec(memory_space=vmem)] * 7,
        out_specs=(pl.BlockSpec(memory_space=vmem),) * 2,
        scratch_shapes=(
            [vmem((3, 96, 512), BF16), vmem((3, 80, 640), BF16), vmem((3, B_ROWS, 384), BF16)] * 2
            + [pltpu.SemaphoreType.DMA((2, 3, 3))] + reduce_scratch(((144, 512), (144, 512)))),
        compiler_params=pltpu.CompilerParams(
            collective_id=3, has_side_effects=True, vmem_limit_bytes=60 * 2**20),
    )(*operands)


def push(source, target, sems, index, peer):
    return pltpu.make_async_remote_copy(
        src_ref=source, dst_ref=target, send_sem=sems.at[(0,) + index],
        recv_sem=sems.at[(1,) + index], device_id=peer, device_id_type=MESH)


def turned(value):
    return value.astype(F32).T


def masked(scores, bounds, seq, block):
    rows = lax.broadcasted_iota(jnp.int32, scores.shape, 0)
    spot = block * 256 + lax.broadcasted_iota(jnp.int32, (1, 256), 1)
    start = jnp.zeros((1, 256), jnp.int32)
    for n in range(3):
        bound = bounds[:, 3 * seq + n : 3 * seq + n + 1]
        start = jnp.where(spot >= bound, bound, start)
    return jnp.where((rows <= spot) & (rows >= start), scores, -1e30)


def chances(keys, query, bounds, seq, block):
    scores = lax.dot_general(keys, query, NT, preferred_element_type=F32)
    scores = masked(scores, bounds, seq, block)
    powers = jnp.exp(scores - jnp.max(scores, axis=0, keepdims=True))
    return powers * (1.0 / jnp.sum(powers, axis=0, keepdims=True))


def head_part(value, head):
    lane = lax.broadcasted_iota(jnp.int32, value.shape, 1)
    return jnp.where((lane < 64) == (head == 0), value, jnp.zeros_like(value))


def attend(queries, keys, values, bounds, seq, heads, store, pump):
    queries = queries * 0.125
    value_t = turned(values).astype(BF16)
    for block in range(4):
        rows = slice(block * 256, block * 256 + 256)
        size = block * 256 + 256
        parts = []
        for head in range(heads):
            low = chances(keys[:size], head_part(queries[rows], head), bounds, seq, block).astype(BF16)
            parts.append(dot(value_t[:, :size], low))
            pump()
        whole = parts[0] if heads == 1 else jnp.concatenate([parts[0][:64], parts[1][64:]], axis=0)
        store(block, whole.T.astype(BF16).reshape(2, 128, 128))


def fetch_blocks(source, held, sems):
    copies = [pltpu.make_async_copy(source.at[s], held.at[s], sems.at[s]) for s in range(8)]
    for copy in copies:
        copy.start()
    return copies


GATHER_COPIES = 200
COUNTS_ROW = 12


def enter_kernel(a_ref, b_ref, vec, hidden, gq, gu, gb, att, got, got8, normed_t, lines, up_row,
                 bound_row, weights, za, zb, mine_a, mine_b, vecs, pack, out, out8,
                 send_sems, recv_sems, local_sems, vec_sems, in_sems, in8_sems, back_sems, back8_sems):
    g = Place()
    greet(all_peers(g))
    send = Sender(send_sems, recv_sems)
    first = []
    left, right = pl.ds(0, 512), pl.ds(512, 640)
    for step in (2, 1, 3):
        first.append(send(a_ref.at[:, left], za.at[g.z, :, left], g.peer("z", step)))
    later = []
    for step in (2, 1, 3):
        later.append(send(a_ref.at[:, right], za.at[g.z, :, right], g.peer("z", step)))
        later.append(send(b_ref, zb.at[g.z], g.peer("z", step)))

    def vec_copy(step):
        return push(vec, vecs.at[g.seq], vec_sems, (step - 1,), g.member(g.other(step)))

    for step in range(1, 8):
        vec_copy(step).start()
    vecs[g.seq] = vec[...]
    za[g.z] = a_ref[...]
    zb[g.z] = b_ref[...]
    for copy in first:
        copy.wait_recv()
    mine_a[:, :512] = merge_rows(za[:, :, :512].reshape(320, 512))

    def spot(part, step_x, step_y):
        kind, low, rows = part
        x, y = (g.x + step_x) % 4, (g.y + step_y) % 4
        if kind == "b":
            return gb.at[y, 2 * x + g.c, pl.ds(low, rows)]
        span = pl.ds(pl.multiple_of(y * A_ROWS + low, 16), rows)
        return (weights if kind == "q" else gu).at[2 * x + g.c, span]

    def source(part):
        kind, low, rows = part
        if kind == "b":
            return mine_b.at[pl.ds(low, rows)]
        return mine_a.at[pl.ds(low, rows), left if kind == "q" else right]

    near = Rings(g, send, AXES, {0: ("q", 0, 144), 1: ("q", 144, 128)},
                 {0: [("q", 0, 64), ("q", 64, 80)], 1: [("q", 144, 64), ("q", 208, 64)]}, source, spot)
    rest = Rings(g, send, {0: ("x", "y"), 1: ("y", "x"), 2: ("x", "y")},
                 {0: ("u", 0, 272), 1: ("b", 48, 96), 2: ("b", 0, 48)},
                 {0: [("u", 0, 128), ("u", 128, 144)], 1: [("b", 48, 48), ("b", 96, 48)],
                  2: [("b", 0, 16), ("b", 16, 32)]}, source, spot)
    near.run(("first", 0), ("first", 1), ("second", 0), ("second", 1))
    own = [pltpu.make_async_copy(source(part), spot(part, 0, 0), local_sems.at[k])
           for k, part in enumerate((("q", 0, A_ROWS), ("u", 0, A_ROWS), ("b", 0, B_ROWS)))]
    own[0].start()
    for step in range(1, 8):
        vec_copy(step).wait_recv()
    tiles = {}
    counts = jnp.zeros((1, 128), F32)
    for s in range(8):
        value = vecs[s].astype(F32)
        shift_lanes(tiles, value, 0, 136, 136 * s)
        counts = counts + value[COUNTS_ROW : COUNTS_ROW + 1, :128]
    table = join_tiles(tiles, 9)
    lines[...] = table[:8]
    bound_row[...] = counts.astype(jnp.int32)
    bounds = bound_row[...]
    for y in range(4):
        tiles = {}
        for odd in (0, 1):
            value = vecs[2 * y + odd].astype(F32)
            for row in range(4):
                shift_lanes(tiles, value[8 + row : 9 + row], 0, 136, 544 * odd + 136 * row)
        up_row[y] = join_tiles(tiles, 9)[:, :D]
    unit, _ = normalize(hidden[...].astype(F32).reshape(256, D))
    normed = unit * table[0:1, :D] + table[2:3, :D]
    normed_t[...] = normed.T.astype(BF16)
    normed = normed.astype(BF16)
    near.run(("spread", 0), ("spread", 1), ("relay", 0, 0), ("relay", 1, 0))
    for copy in later:
        copy.wait_recv()
    mine_a[:, 512:] = merge_rows(za[:, :, 512:].reshape(320, 640))
    mine_b[...] = merge_columns(zb)
    own[1].start()
    own[2].start()
    near.run(("far", 0), ("far", 1), ("relay", 0, 1), ("relay", 1, 1), ("close", 0, 0),
             ("close", 1, 0), ("relay", 0, 3), ("relay", 1, 3), ("relay", 0, 2), ("relay", 1, 2))
    rest.run(*EARLY)
    near.run(*[("close", half, by) for by in (1, 3, 2) for half in (0, 1)], ("settle",))
    own[0].wait()
    kept = pltpu.make_async_copy(weights, gq, local_sems.at[3])
    kept.start()
    tiles = ({}, {}, {})
    for s in range(8):
        block = dot(normed, weights[s])
        for seg, low, width, kind, place in segments():
            if seg == s:
                shift_lanes(tiles[kind], block, low, width, place)
    for kind, row in ((0, 4), (1, None), (2, 5)):
        for p in range(9):
            tile = tiles[kind][p]
            if row is not None:
                tile = tile + table[row : row + 1, 128 * p : 128 * p + 128]
            pack[p, kind] = tile.astype(BF16).reshape(2, 128, 128)

    ticks = [0]

    def pump():
        ticks[0] += 1
        rest.run(*LATE.get(ticks[0], ()))

    def in_copy(step):
        return push(pack.at[g.other(step)], got.at[g.seq], in_sems, (step - 1,), g.member(g.other(step)))

    def in8_copy(extra, source):
        return pltpu.make_async_remote_copy(
            src_ref=pack.at[8, :, extra], dst_ref=got8.at[source], send_sem=in8_sems.at[8 + extra],
            recv_sem=in8_sems.at[source], device_id=g.member(4 * extra), device_id_type=MESH)

    for step in (4, 3, 5, 2, 6, 1, 7):
        in_copy(step).start()
    for extra in (0, 1):
        @pl.when(g.seq != 4 * extra)
        def _():
            in8_copy(extra, g.seq).start()

        @pl.when(g.seq == 4 * extra)
        def _():
            got8[g.seq] = pack[8, :, extra]
    got[g.seq] = pack[g.seq]
    rest.run(*LATE[0])
    for step in range(1, 8):
        in_copy(step).wait_recv()

    def back_copy(seq, step):
        return push(out.at[g.other(step), seq], att.at[g.seq, seq], back_sems, (seq, step - 1),
                    g.member(g.other(step)))

    def pair(seq):
        def store(block, value):
            out[pl.ds(2 * block, 2), seq] = value
        part = lambda kind: got[:, kind, seq].reshape(1024, 128)
        attend(part(0), part(1), part(2), bounds, seq, 2, store, pump)
        for step in (4, 3, 5, 2, 6, 1, 7):
            back_copy(seq, step).start()

    for seq in (0, 1):
        pair(seq)
    att[g.seq] = out[g.seq]

    def back8_copy(extra, step):
        return pltpu.make_async_remote_copy(
            src_ref=out8.at[g.other(step)], dst_ref=att.at[8, extra], send_sem=back8_sems.at[1 + step],
            recv_sem=back8_sems.at[extra], device_id=g.member(g.other(step)), device_id_type=MESH)

    for extra in (0, 1):
        @pl.when(g.seq == 4 * extra)
        def _():
            for step in range(1, 8):
                in8_copy(extra, g.other(step)).wait_recv()

            def store(block, value):
                out8[pl.ds(2 * block, 2)] = value
            part = lambda kind: got8[:, kind].reshape(1024, 128)
            attend(part(0), part(1), part(2), bounds, extra, 1, store, lambda: None)
            for step in range(1, 8):
                back8_copy(extra, step).start()
            att[8, extra] = out8[g.seq]
            for step in range(1, 8):
                back8_copy(extra, step).wait_send()

        @pl.when(g.seq != 4 * extra)
        def _():
            in8_copy(extra, g.seq).wait_send()
            back8_copy(extra, 1).wait_recv()
    for step in range(1, 8):
        in_copy(step).wait_send()
        for seq in (0, 1):
            back_copy(seq, step).wait_recv()
            back_copy(seq, step).wait_send()
    rest.run(("settle",))
    for copy in send.made:
        copy.wait_send()
    for step in range(1, 8):
        vec_copy(step).wait_send()
    own[1].wait()
    own[2].wait()
    kept.wait()


def enter_block(*operands):
    tile = (128, 128)
    vmem = pltpu.VMEM
    shape = jax.ShapeDtypeStruct
    return pl.pallas_call(
        enter_kernel,
        out_shape=(
            shape((8, D, 512), BF16), shape((8, D, 640), BF16), shape((4, 8, B_ROWS, D), BF16),
            shape((9, 2) + tile, BF16), shape((8, 3, 2) + tile, BF16), shape((8, 3) + tile, BF16),
            shape((D, 256), BF16), shape((8, WIDE), F32), shape((4, 1, D), F32),
            shape((1, 128), jnp.int32)),
        in_specs=[pl.BlockSpec(memory_space=vmem)] * 4,
        out_specs=(pl.BlockSpec(memory_space=pl.ANY),) * 3 + (pl.BlockSpec(memory_space=vmem),) * 7,
        scratch_shapes=[
            vmem((8, D, 512), BF16), vmem((4, 80, WIDE), BF16), vmem((4, B_ROWS, 384), BF16),
            vmem((A_ROWS, WIDE), BF16), vmem((B_ROWS, D), BF16), vmem((8, 16, 256), BF16),
            vmem((9, 3, 2) + tile, BF16), vmem((8, 2) + tile, BF16), vmem((8,) + tile, BF16),
            pltpu.SemaphoreType.DMA((GATHER_COPIES,)), pltpu.SemaphoreType.DMA((GATHER_COPIES,)),
            pltpu.SemaphoreType.DMA((4,)), pltpu.SemaphoreType.DMA((2, 7)),
            pltpu.SemaphoreType.DMA((2, 7)), pltpu.SemaphoreType.DMA((10,)),
            pltpu.SemaphoreType.DMA((2, 2, 7)), pltpu.SemaphoreType.DMA((9,))],
        compiler_params=pltpu.CompilerParams(
            collective_id=1, has_side_effects=True, vmem_limit_bytes=60 * 2**20),
    )(*operands)


def attend_pull(queries, keys, values, grads, bounds, seq, heads, key_sum, value_sum, store, pump):
    queries = queries * 0.125
    key_t = turned(keys).astype(BF16)
    key_sum[...] = jnp.zeros_like(key_sum)
    value_sum[...] = jnp.zeros_like(value_sum)
    for block in range(4):
        rows = slice(block * 256, block * 256 + 256)
        size = block * 256 + 256
        parts = []
        for head in range(heads):
            query, grad = head_part(queries[rows], head), head_part(grads[rows], head)
            probs = chances(keys[:size], query, bounds, seq, block)
            change = lax.dot_general(values[:size], grad, NT, preferred_element_type=F32)
            inner = jnp.sum(probs * change, axis=0, keepdims=True)
            slope = (probs * (change - inner)).astype(BF16)
            value_sum[:size] += jnp.dot(probs.astype(BF16), grad, preferred_element_type=F32)
            key_sum[:size] += jnp.dot(slope, query, preferred_element_type=F32)
            parts.append(dot(key_t[:, :size], slope))
            pump()
        whole = parts[0] if heads == 1 else jnp.concatenate([parts[0][:64], parts[1][64:]], axis=0)
        store(0, block, (whole.T * 0.125).astype(BF16).reshape(2, 128, 128))
    for kind, total in ((1, key_sum), (2, value_sum)):
        for block in range(4):
            store(kind, block, total[block * 256 : block * 256 + 256].astype(BF16).reshape(2, 128, 128))


def pull_kernel(pack, got, got8, hidden, middle_grad, lines, bound_row, x_o, x_u, y_o, y_u, tt, act,
                sums, up_sums, ga, placed, input_grad, extra, block_u, block_b,
                weights, back, grad, grad8, out, out8, key_sum, value_sum,
                weight_sems, in_sems, in8_sems, back_sems, back8_sems, *refs):
    g = Place()
    bounds = bound_row[...]
    greet(all_peers(g))

    def part_u(column, y):
        rows = pl.ds(pl.multiple_of(y * A_ROWS, 16), A_ROWS)
        three = dot(x_u[rows], y_u[column])
        two = dot(x_o[rows], y_o[column, :, 128:256])
        return jnp.concatenate([three[:, :128] + two, three[:, 128:]], axis=1)

    def part_b(column, y):
        return dot(tt[column], act[y])

    reduce = make_reduce(g, refs, ((part_u, A_ROWS, 128), (part_b, B_ROWS, 64)))
    plan = {1: lambda: reduce.cross(0, 3), 14: reduce.own}
    ticks = [0]

    def pump():
        ticks[0] += 1
        if ticks[0] in plan:
            plan[ticks[0]]()

    def fetch(s):
        return pltpu.make_async_copy(ga.at[s], weights.at[s % 2], weight_sems.at[s % 2])

    fetch(0).start()
    fetch(1).start()

    def in_copy(step):
        return push(pack.at[g.other(step)], grad.at[g.seq], in_sems, (step - 1,), g.member(g.other(step)))

    def in8_copy(which, source):
        return pltpu.make_async_remote_copy(
            src_ref=pack.at[8, which], dst_ref=grad8.at[source], send_sem=in8_sems.at[8 + which],
            recv_sem=in8_sems.at[source], device_id=g.member(4 * which), device_id_type=MESH)

    for step in (4, 3, 5, 2, 6, 1, 7):
        in_copy(step).start()
    for which in (0, 1):
        @pl.when(g.seq != 4 * which)
        def _():
            in8_copy(which, g.seq).start()

        @pl.when(g.seq == 4 * which)
        def _():
            grad8[g.seq] = pack[8, which]
    grad[g.seq] = pack[g.seq]
    reduce.cross(2, None)
    reduce.opposite()
    reduce.cross(1, 2)
    reduce.cross(3, 1)
    reduce.sides(0)
    reduce.sides(1)
    for step in range(1, 8):
        in_copy(step).wait_recv()

    def back_copy(seq, step):
        return push(out.at[g.other(step), seq], back.at[g.seq, seq], back_sems, (seq, step - 1),
                    g.member(g.other(step)))

    def pair(seq, carry):
        def store(kind, block, value):
            out[pl.ds(2 * block, 2), seq, kind] = value
        part = lambda kind: got[:, kind, seq].reshape(1024, 128)
        attend_pull(part(0), part(1), part(2), grad[:, seq].reshape(1024, 128), bounds, seq, 2,
                    key_sum, value_sum, store, pump)
        for step in (4, 3, 5, 2, 6, 1, 7):
            back_copy(seq, step).start()
        return carry

    for seq in (0, 1):
        pair(seq, 0)
    back[g.seq] = out[g.seq]

    def back8_copy(which, step):
        return pltpu.make_async_remote_copy(
            src_ref=out8.at[g.other(step)], dst_ref=back.at[8, which], send_sem=back8_sems.at[1 + step],
            recv_sem=back8_sems.at[which], device_id=g.member(g.other(step)), device_id_type=MESH)

    for which in (0, 1):
        @pl.when(g.seq == 4 * which)
        def _():
            for step in range(1, 8):
                in8_copy(which, g.other(step)).wait_recv()

            def store(kind, block, value):
                out8[pl.ds(2 * block, 2), kind] = value
            part = lambda kind: got8[:, kind].reshape(1024, 128)
            attend_pull(part(0), part(1), part(2), grad8[...].reshape(1024, 128), bounds, which, 1,
                        key_sum, value_sum, store, lambda: None)
            for step in range(1, 8):
                back8_copy(which, step).start()
            back[8, which] = out8[g.seq]
            for step in range(1, 8):
                back8_copy(which, step).wait_send()

        @pl.when(g.seq != 4 * which)
        def _():
            in8_copy(which, g.seq).wait_send()
            back8_copy(which, 1).wait_recv()
    reduce.middle()
    for step in range(1, 8):
        in_copy(step).wait_send()
        for seq in (0, 1):
            back_copy(seq, step).wait_recv()
            back_copy(seq, step).wait_send()

    natural = [jnp.concatenate([back[p, :, kind].reshape(256, 128) for p in range(9)],
                               axis=1).astype(F32) for kind in range(3)]
    total = None
    for s in range(8):
        tiles = {}
        for seg, low, width, kind, spot in segments():
            if seg == s:
                shift_lanes(tiles, natural[kind], spot, width, low)
        block = join_tiles(tiles, 4).astype(BF16)
        placed[s] = block
        fetch(s).wait()
        term = dot_t(block, weights[s % 2])
        if s < 6:
            fetch(s + 2).start()
        total = term if total is None else total + term
    reduce.last()
    unit, scale = normalize(hidden[...].astype(F32).reshape(256, D))
    input_grad[...] = middle_grad[...] + norm_pull(total, lines[0:1, :D], unit, scale)

    def column_sum(value):
        return jnp.sum(value, axis=0, keepdims=True)

    table = jnp.concatenate([
        column_sum(widen(total * unit)), sums[0:1], column_sum(widen(total)), sums[1:2],
        column_sum(natural[0]), column_sum(natural[2]), sums[2:4]], axis=0)
    for s in range(8):
        tiles = {}
        shift_lanes(tiles, table, 136 * s, 136, 0)
        first = join_tiles(tiles, 4)
        rows = []
        for row in range(4):
            tiles = {}
            shift_lanes(tiles, up_sums[s], 32 + 136 * row, 136, 136)
            rows.append(join_tiles(tiles, 4))
        second = jnp.concatenate(rows + [jnp.zeros((4, 512), F32)], axis=0)
        extra[s] = jnp.concatenate([first + second, jnp.zeros((8, 512), F32)], axis=0)
    block_u[...] = reduce.result(0).astype(BF16)
    block_b[...] = reduce.result(1).astype(BF16)
    reduce.drain()


def attend_backward(*operands):
    tile = (128, 128)
    vmem = pltpu.VMEM
    return pl.pallas_call(
        pull_kernel,
        out_shape=(jax.ShapeDtypeStruct((8, 256, 512), BF16),
                   jax.ShapeDtypeStruct((256, D), F32), jax.ShapeDtypeStruct((8, 16, 512), F32),
                   jax.ShapeDtypeStruct((A_ROWS, 640), BF16), jax.ShapeDtypeStruct((B_ROWS, D), BF16)),
        in_specs=[pl.BlockSpec(memory_space=vmem)] * 15 + [pl.BlockSpec(memory_space=pl.ANY)],
        out_specs=(pl.BlockSpec(memory_space=vmem),) * 5,
        scratch_shapes=[
            vmem((2, D, 512), BF16), vmem((9, 2, 3) + tile, BF16), vmem((8, 2) + tile, BF16), vmem((8,) + tile, BF16),
            vmem((8, 2, 3) + tile, BF16), vmem((8, 3) + tile, BF16),
            vmem((1024, 128), F32), vmem((1024, 128), F32),
            pltpu.SemaphoreType.DMA((2,)),
            pltpu.SemaphoreType.DMA((2, 7)), pltpu.SemaphoreType.DMA((10,)),
            pltpu.SemaphoreType.DMA((2, 2, 7)), pltpu.SemaphoreType.DMA((9,)),
        ] + reduce_scratch(((A_ROWS, 640), (B_ROWS, D))),
        compiler_params=pltpu.CompilerParams(
            collective_id=2, has_side_effects=True, vmem_limit_bytes=63 * 2**20),
    )(*operands)


def middle_kernel(att, hidden, top, lines, up_row, gq, gu, gb,
                  layer_out, middle_grad, att_grad, att_t, normed_t, active, y_o, y_u, sums, up_sums, top_t,
                  held_o, held_u, held_b, normed, down_sum, norm_grad, top_pad, sems_o, sems_u, sems_b):
    copies_o = []
    for s in range(8):
        copies_o.append(pltpu.make_async_copy(
            gq.at[s, :, pl.ds(384, 128)], held_o.at[s, :, pl.ds(0, 128)], sems_o.at[0, s]))
        copies_o.append(pltpu.make_async_copy(
            gu.at[s, :, pl.ds(0, 128)], held_o.at[s, :, pl.ds(128, 128)], sems_o.at[1, s]))
    for copy in copies_o:
        copy.start()

    def up_copy(s):
        return pltpu.make_async_copy(gu.at[s], held_u.at[s], sems_u.at[s])

    def down_copy(y):
        return pltpu.make_async_copy(gb.at[y], held_b.at[y], sems_b.at[y])

    for y in range(4):
        up_copy(2 * y).start()
        up_copy(2 * y + 1).start()
        down_copy(y).start()

    tiles = {}
    for s in range(8):
        shift_lanes(tiles, widen(top[...].reshape(256, D)).astype(F32), 136 * s, 136, 144 * s)
    padded = join_tiles(tiles, 9)
    top_pad[...] = padded.astype(BF16)
    top_t[...] = padded.T.astype(BF16).reshape(8, B_ROWS, 256)
    attended = jnp.concatenate([att[p].reshape(256, 128) for p in range(9)], axis=1)
    att_t[...] = attended.astype(F32).T[:D].astype(BF16)
    tiles = {}
    for s in range(8):
        copies_o[2 * s].wait()
        copies_o[2 * s + 1].wait()
        shift_lanes(tiles, dot(attended[:, :D], held_o[s]), 24, 136, 136 * s)
    branch = join_tiles(tiles, 9)[:, :D]
    middle = hidden[...].astype(F32).reshape(256, D) + branch + lines[6:7, :D]
    unit, scale = normalize(middle)
    value = unit * lines[1:2, :D] + lines[3:4, :D]
    normed[...] = value.astype(BF16)
    normed_t[...] = value.T.astype(BF16)
    down_sum[...] = jnp.zeros_like(down_sum)
    norm_grad[...] = jnp.zeros_like(norm_grad)

    def step(y, carry):
        tiles = {}
        for odd in (0, 1):
            up_copy(2 * y + odd).wait()
            shift_lanes(tiles, dot(normed[...], held_u[2 * y + odd]), 32, 544, 544 * odd)
        pre = join_tiles(tiles, 9)[:, :D] + up_row[y]
        cube = 0.7978845608028654 * (pre + 0.044715 * (pre * pre * pre))
        bend = jnp.tanh(cube)
        half = 0.5 * (1.0 + bend)
        acts = (pre * half).astype(BF16)
        slope = half + 0.5 * pre * (1.0 - bend * bend) * (
            0.7978845608028654 * (1.0 + 3 * 0.044715 * (pre * pre)))
        active[y] = acts
        down_copy(y).wait()
        weights = held_b[y].reshape(8 * B_ROWS, D)
        down_sum[...] += dot_t(acts, weights)
        inner = dot(top_pad[...], weights) * slope
        inner = widen(inner.astype(BF16).astype(F32))
        total = None
        for odd in (0, 1):
            tiles = {}
            shift_lanes(tiles, inner, 544 * odd, 544, 32)
            block = join_tiles(tiles, 5)
            up_sums[2 * y + odd] = jnp.sum(block, axis=0, keepdims=True)
            block = block.astype(BF16)
            y_u[2 * y + odd] = block
            term = dot_t(block, held_u[2 * y + odd])
            total = term if total is None else total + term
        norm_grad[...] += total
        return carry

    lax.fori_loop(0, 4, step, 0)
    tiles = {}
    down = down_sum[...]
    for s in range(8):
        shift_lanes(tiles, down, 144 * s, 136, 136 * s)
    out = middle + join_tiles(tiles, 9)[:, :D] + lines[7:8, :D]
    layer_out[...] = out.astype(BF16).reshape(2, 128, D)
    grad = norm_grad[...]
    cotangent = top[...].astype(F32).reshape(256, D)
    total = cotangent + norm_pull(grad, lines[1:2, :D], unit, scale)
    middle_grad[...] = total
    branch = widen(total.astype(BF16).astype(F32))
    back = None
    for s in range(8):
        tiles = {}
        shift_lanes(tiles, branch, 136 * s, 136, 24)
        block = join_tiles(tiles, 2).astype(BF16)
        y_o[s] = block
        term = dot_t(block, held_o[s])
        back = term if back is None else back + term
    back = widen(back).astype(BF16)
    for p in range(9):
        att_grad[p] = back[:, 128 * p : 128 * p + 128].reshape(2, 128, 128)
    sums[0:1] = jnp.sum(widen(grad * unit), axis=0, keepdims=True)
    sums[1:2] = jnp.sum(widen(grad), axis=0, keepdims=True)
    sums[2:3] = jnp.sum(branch, axis=0, keepdims=True)
    sums[3:4] = jnp.sum(widen(cotangent), axis=0, keepdims=True)
    sums[4:8] = jnp.zeros((4, WIDE), F32)


def middle_block(*operands):
    vmem = pltpu.VMEM
    shape = jax.ShapeDtypeStruct
    return pl.pallas_call(
        middle_kernel,
        out_shape=(
            shape((2, 128, D), BF16), shape((256, D), F32), shape((9, 2, 128, 128), BF16),
            shape((D, 256), BF16), shape((D, 256), BF16), shape((4, 256, D), BF16),
            shape((8, 256, 256), BF16), shape((8, 256, 640), BF16), shape((8, WIDE), F32),
            shape((8, 1, 640), F32), shape((8, B_ROWS, 256), BF16)),
        in_specs=[pl.BlockSpec(memory_space=vmem)] * 5 + [pl.BlockSpec(memory_space=pl.ANY)] * 3,
        out_specs=(pl.BlockSpec(memory_space=vmem),) * 11,
        scratch_shapes=[
            vmem((8, D, 256), BF16), vmem((8, D, 640), BF16), vmem((4, 8, B_ROWS, D), BF16),
            vmem((256, D), BF16), vmem((256, WIDE), F32), vmem((256, D), F32), vmem((256, WIDE), BF16),
            pltpu.SemaphoreType.DMA((2, 8)), pltpu.SemaphoreType.DMA((8,)),
            pltpu.SemaphoreType.DMA((4,))],
        compiler_params=pltpu.CompilerParams(vmem_limit_bytes=62 * 2**20),
    )(*operands)


def per_device(
    inputs, out_grad, segment_ids, qkv_weight, out_weight, up_weight, down_weight,
    norm_gains, norm_shifts, qv_bias, proj_bias, up_bias,
):
    seqs, rows, _ = inputs.shape

    blob_a = jnp.concatenate([qkv_weight, out_weight, up_weight], axis=1)
    blob_a = jnp.pad(blob_a, ((0, 12), (0, WIDE - D)))
    counts = jnp.sum(segment_ids[:, :, None] < jnp.arange(1, 4)[None, None, :], axis=1)
    counts = jnp.pad(counts.astype(BF16).reshape(1, 6), ((0, 3), (0, 130)))
    vec = jnp.concatenate(
        [norm_gains, norm_shifts, qv_bias, proj_bias, up_bias.reshape(4, 136), counts], axis=0
    )
    vec = jnp.pad(vec, ((0, 0), (0, 120)))
    blob_b = jnp.pad(down_weight.T, ((0, 8), (0, 112)))

    (w_q, w_u, w_b, att, got, got8, normed_t, lines, up_row, bounds) = enter_block(
        blob_a, blob_b, vec, inputs
    )
    (layer_out, middle_grad, att_grad, att_t, normed_two_t, active, y_o, y_u, sums, up_sums, top_t) = (
        middle_block(att, inputs, out_grad, lines, up_row, w_q, w_u, w_b)
    )
    y_q, input_grad, extra, block_u, block_b = attend_backward(
        att_grad, got, got8, inputs, middle_grad, lines, bounds, att_t, normed_two_t, y_o, y_u,
        top_t, active, sums, up_sums, w_q
    )
    out_a, out_b = leave_block(normed_t, att_t, y_q, y_o, extra, block_u, block_b)
    return (
        layer_out,
        input_grad.reshape(seqs, rows, D),
        out_a[:68, :408],
        out_a[:68, 408:544],
        out_a[:68, 544:D],
        out_b[:136, :272].T,
        out_b[136:138, :136],
        out_b[138:140, :136],
        out_b[140:142, :136],
        out_b[142:144, :136],
        out_b[136:140, 136:272].reshape(1, 544),
    )


def solution(mesh):
    tokens = P("batch", "seq", None)
    matrix = P("batch", "seq")
    vector = P(None, "seq")
    return jax.shard_map(
        per_device,
        mesh=mesh,
        in_specs=(tokens, tokens, matrix, matrix, matrix, matrix, matrix) + (vector,) * 5,
        out_specs=(tokens, tokens, matrix, matrix, matrix, matrix) + (vector,) * 5,
        check_vma=False,
    )
```

```python
import jax
import jax.numpy as jnp
from jax import lax
from jax.experimental import pallas as pl
from jax.experimental.pallas import tpu as pltpu
from jax.sharding import PartitionSpec as P

D = 1088
WIDE = 1152
F32 = jnp.float32
BF16 = jnp.bfloat16
MESH = pl.DeviceIdType.MESH
A_ROWS, B_ROWS = 272, 144
CUT = 208


class Place:
    def __init__(self):
        batch, seq = lax.axis_index("batch"), lax.axis_index("seq")
        self.batch, self.seq = batch, seq
        self.y, self.z = batch // 4, batch % 4
        self.x, self.c = seq // 2, seq % 2
        self.sibling = {"batch": batch, "seq": self.x * 2 + 1 - self.c}

    def other(self, step):
        return (self.seq + step) % 8

    def member(self, seq):
        return {"batch": self.batch, "seq": seq}

    def peer(self, axis, step):
        spot = {"x": self.x, "y": self.y, "z": self.z}
        spot[axis] = (spot[axis] + step + 4) % 4
        return {"batch": spot["y"] * 4 + spot["z"], "seq": spot["x"] * 2 + self.c}


def greet(peers):
    barrier = pltpu.get_barrier_semaphore()
    for peer in peers:
        pl.semaphore_signal(barrier, inc=1, device_id=peer, device_id_type=MESH)
    pl.semaphore_wait(barrier, len(peers))


def all_peers(me):
    return [me.member(me.other(step)) for step in range(1, 8)] + [me.peer(axis, step) for axis, step in (
        ("y", 1), ("y", 3), ("z", 1), ("z", 2), ("z", 3))]


class Sender:
    def __init__(self, send_sems, recv_sems):
        self.send_sems, self.recv_sems, self.made = send_sems, recv_sems, []

    def __call__(self, source, target, peer):
        index = len(self.made)
        copy = pltpu.make_async_remote_copy(
            src_ref=source, dst_ref=target, send_sem=self.send_sems.at[index],
            recv_sem=self.recv_sems.at[index], device_id=peer, device_id_type=MESH)
        copy.start()
        self.made.append(copy)
        return copy


EARLY = [("first", 1), ("first", 0), ("second", 0)]
LATE = {
    0: [("spread", 1), ("second", 2), ("first", 2), ("second", 1), ("spread", 0), ("relay", 0, 0), ("far", 1), ("relay", 2, 0), ("relay", 0, 1)],
    4: [("relay", 1, 1)],
    5: [("relay", 0, 3)],
    6: [("relay", 1, 3), ("spread", 2), ("close", 0, 0), ("close", 2, 0)],
    7: [("close", 0, 1), ("relay", 1, 0)],
    8: [("close", 0, 3)],
    9: [("far", 0), ("relay", 2, 1)],
    11: [("relay", 1, 2), ("relay", 2, 3)],
    12: [("close", 1, 1)],
    13: [("close", 1, 3)],
    14: [("far", 2), ("relay", 0, 2), ("close", 2, 1), ("close", 1, 0), ("close", 2, 3)],
    16: [("relay", 2, 2), ("close", 1, 2), ("close", 0, 2), ("close", 2, 2)],
}


def merge_rows(stacked):
    row = lax.broadcasted_iota(jnp.int32, (A_ROWS, 320), 0)
    col = lax.broadcasted_iota(jnp.int32, (A_ROWS, 320), 1)
    pick = jnp.where(col == row + 12 * (row // 68), 1.0, 0.0).astype(BF16)
    return jnp.dot(pick, stacked, preferred_element_type=F32).astype(BF16)


def merge_columns(slots):
    total = None
    for z in range(4):
        row = lax.broadcasted_iota(jnp.int32, (384, D), 0)
        col = lax.broadcasted_iota(jnp.int32, (384, D), 1)
        pick = jnp.where((col == row + 272 * z) & (row < 272), 1.0, 0.0).astype(BF16)
        term = jnp.dot(slots[z], pick, preferred_element_type=F32)
        total = term if total is None else total + term
    return total.astype(BF16)

AXES = {0: ("x", "y"), 1: ("y", "x")}


class Rings:
    def __init__(self, me, send, axes, whole, split, source, spot):
        self.me, self.send, self.axes, self.whole, self.split = me, send, axes, whole, split
        self.source, self.spot, self.crossed, self.sent = source, spot, [], {}

    def move(self, axis, steps, by):
        if axis == "x":
            return ((steps[0] + by) % 4, steps[1])
        return (steps[0], (steps[1] + by) % 4)

    def push(self, part, steps, peer):
        source = self.source if steps == (0, 0) else lambda part: self.spot(part, *steps)
        return self.send(source(part), self.spot(part, *steps), peer)

    def cross(self, half, steps):
        self.crossed.append(self.push(self.whole[half], steps, self.me.sibling))

    def begin(self, half, axis, steps):
        return {by: self.push(self.whole[half], steps, self.me.peer(axis, by)) for by in (1, 3)}

    def forward(self, half, axis, steps, sent, flip):
        ends = []
        for by, which in ((1, flip), (3, 1 - flip)):
            origin = self.move(axis, steps, -by)
            sent[by].wait_recv()
            ends.append(self.push(self.split[half][which], origin, self.me.peer(axis, by)))
        return ends

    def arrived(self, half, axis, steps):
        for by in (1, 3):
            self.cross(half, self.move(axis, steps, by))

    def finish(self, half, axis, steps, ends):
        for copy in ends:
            copy.wait_recv()
        self.cross(half, self.move(axis, steps, 2))

    def first(self, half):
        self.sent[half] = self.begin(half, self.axes[half][0], (0, 0))

    def second(self, half):
        self.sent[half, 0] = self.begin(half, self.axes[half][1], (0, 0))
        self.cross(half, (0, 0))

    def spread(self, half):
        axis = self.axes[half][0]
        self.sent[half, "far"] = self.forward(half, axis, (0, 0), self.sent[half], half % 2)
        for by in (1, 3):
            self.sent[half, by] = self.begin(half, self.axes[half][1], self.move(axis, (0, 0), by))
        self.arrived(half, axis, (0, 0))

    def far(self, half):
        axis = self.axes[half][0]
        self.finish(half, axis, (0, 0), self.sent[half, "far"])
        self.sent[half, 2] = self.begin(half, self.axes[half][1], self.move(axis, (0, 0), 2))

    def relay(self, half, by):
        steps = self.move(self.axes[half][0], (0, 0), by)
        self.sent[half, by, "end"] = self.forward(
            half, self.axes[half][1], steps, self.sent[half, by], by % 2)
        self.arrived(half, self.axes[half][1], steps)

    def close(self, half, by):
        steps = self.move(self.axes[half][0], (0, 0), by)
        self.finish(half, self.axes[half][1], steps, self.sent[half, by, "end"])

    def settle(self):
        for copy in self.crossed:
            copy.wait_recv()

    def run(self, *actions):
        for name, *rest in actions:
            getattr(self, name)(*rest)


NT = (((1,), (1,)), ((), ()))


def normalize(values):
    center = values - jnp.mean(values, axis=-1, keepdims=True)
    spread = jnp.mean(center * center, axis=-1, keepdims=True)
    scale = lax.rsqrt(spread + 1e-05)
    return center * scale, scale


def norm_pull(grad, gain, unit, scale):
    scaled = grad * gain
    return scale * (
        scaled
        - jnp.mean(scaled, axis=-1, keepdims=True)
        - unit * jnp.mean(scaled * unit, axis=-1, keepdims=True)
    )


def dot(left, right):
    return jnp.dot(left, right, preferred_element_type=F32)


def dot_t(left, right):
    return lax.dot_general(left, right, NT, preferred_element_type=F32)


def widen(value):
    return jnp.concatenate([value, jnp.zeros((value.shape[0], WIDE - D), value.dtype)], axis=1)


def shift_lanes(tiles, value, source, width, target):
    turn = (target - source) % 128
    low, high = source // 128, -(-(source + width) // 128)
    part = value[:, low * 128 : high * 128]
    if turn:
        part = jnp.concatenate([part, jnp.zeros((part.shape[0], 128), part.dtype)], axis=1)
        part = pltpu.roll(part, turn, 1)
    start = source - low * 128 + turn
    for spot in range(start // 128, -(-(start + width) // 128)):
        tile = part[:, spot * 128 : spot * 128 + 128]
        first, last = start - spot * 128, start + width - spot * 128
        if first > 0 or last < 128:
            lane = lax.broadcasted_iota(jnp.int32, tile.shape, 1)
            tile = jnp.where((lane >= first) & (lane < last), tile, 0.0)
        place = (target - start) // 128 + spot
        tiles[place] = tiles[place] + tile if place in tiles else tile


def join_tiles(tiles, count):
    rows = next(iter(tiles.values())).shape[0]
    empty = jnp.zeros((rows, 128), F32)
    return jnp.concatenate([tiles.get(k, empty) for k in range(count)], axis=1)


def segments():
    found = []
    for s in range(8):
        for kind in range(3):
            low, high = max(408 * s, D * kind), min(408 * s + 408, D * kind + D)
            if low < high:
                found.append((s, low - 408 * s, high - low, kind, low - D * kind))
    return found


class Reduce:
    def __init__(self, me, blocks, sib_sems, opp_sems, side_sems, mid_sems, end_sems):
        self.me, self.blocks = me, blocks
        self.sib_sems, self.opp_sems, self.side_sems = sib_sems, opp_sems, side_sems
        self.mid_sems, self.end_sems = mid_sems, end_sems

    def copy(self, source, target, sems, index, peer):
        return pltpu.make_async_remote_copy(
            src_ref=source, dst_ref=target, send_sem=sems.at[(0,) + index],
            recv_sem=sems.at[(1,) + index], device_id=peer, device_id_type=MESH)

    def part(self, half, step, o, parity):
        b = self.blocks[half]
        along, beside = (self.me.x, self.me.y) if half == 0 else (self.me.y, self.me.x)
        first, second = (along + step) % 4, (beside + o) % 4
        x, y = (first, second) if half == 0 else (second, first)
        return b["part"](2 * x + parity, y)

    def ends_of(self, half, which):
        b = self.blocks[half]
        return pl.ds(0, b["cut"]) if which == 0 else pl.ds(b["cut"], b["rows"] - b["cut"])

    def beside(self, half, stage, which):
        return self.me.peer(AXES[half][stage], 1 if which == 0 else 3)

    def sib_copy(self, half, step, o):
        b = self.blocks[half]
        return self.copy(b["sib_out"].at[o], b["sib_in"].at[step, o], self.sib_sems,
                         (half, step, o), self.me.sibling)

    def opp_copy(self, half, o, which):
        b = self.blocks[half]
        rows = self.ends_of(half, which)
        return self.copy(b["sib_in"].at[2, o, rows], b["in_opp"].at[o, rows], self.opp_sems,
                         (half, o, which), self.beside(half, 0, which))

    def side_copy(self, half, o, which):
        b = self.blocks[half]
        return self.copy(b["sib_in"].at[1 + 2 * which, o], b["in_side"].at[which, o],
                         self.side_sems, (half, o, which), self.beside(half, 0, which))

    def mid_copy(self, half, which):
        b = self.blocks[half]
        rows = self.ends_of(half, which)
        return self.copy(b["sib_out"].at[2, rows], b["in_mid"].at[rows], self.mid_sems,
                         (half, which), self.beside(half, 1, which))

    def end_copy(self, half, which):
        b = self.blocks[half]
        return self.copy(b["sib_out"].at[which], b["in_end"].at[which], self.end_sems,
                         (half, which), self.beside(half, 1, which))

    def loop(self, body):
        lax.fori_loop(0, 4, lambda o, carry: (body(o), carry)[1], 0)

    def cross(self, step, before):
        def body(o):
            for half in (0, 1):
                if before is not None:
                    self.sib_copy(half, before, o).wait_send()
                self.blocks[half]["sib_out"][o] = self.part(half, step, o, 1 - self.me.c).astype(BF16)
                self.sib_copy(half, step, o).start()
        self.loop(body)

    def mine(self, half, step, o):
        value = self.part(half, step, o, self.me.c)
        self.sib_copy(half, step, o).wait_recv()
        return value + self.blocks[half]["sib_in"][step, o].astype(F32)

    def opposite(self):
        def body(o):
            for half in (0, 1):
                self.blocks[half]["sib_in"][2, o] = self.mine(half, 2, o).astype(BF16)
                for which in (0, 1):
                    self.opp_copy(half, o, which).start()
        self.loop(body)

    def join(self, half, value, arrived, which):
        cut = self.blocks[half]["cut"]
        if which == 0:
            return jnp.concatenate([value[:cut] + arrived[:cut].astype(F32), value[cut:]], axis=0)
        return jnp.concatenate([value[:cut], value[cut:] + arrived[cut:].astype(F32)], axis=0)

    def sides(self):
        def body(o):
            for half in (0, 1):
                b = self.blocks[half]
                for which in (0, 1):
                    value = self.mine(half, 1 + 2 * which, o)
                    self.opp_copy(half, o, which).wait_recv()
                    value = self.join(half, value, b["in_opp"].at[o], which)
                    b["sib_in"][1 + 2 * which, o] = value.astype(BF16)
                    self.side_copy(half, o, which).start()
        self.loop(body)

    def own(self):
        def body(o):
            for half in (0, 1):
                b = self.blocks[half]
                value = self.mine(half, 0, o)
                for which in (0, 1):
                    self.side_copy(half, o, which).wait_recv()
                    value = value + b["in_side"][which, o].astype(F32)
                b["acc"][o] = value
        self.loop(body)

    def middle(self):
        def body(o):
            for half in (0, 1):
                self.sib_copy(half, 0, o).wait_send()
        self.loop(body)
        for half in (0, 1):
            b = self.blocks[half]
            b["sib_out"][2] = b["acc"][2].astype(BF16)
            for which in (0, 1):
                self.mid_copy(half, which).start()

    def last(self):
        for half in (0, 1):
            b = self.blocks[half]
            for which in (0, 1):
                value = b["acc"][1 + 2 * which]
                self.mid_copy(half, which).wait_recv()
                b["sib_out"][which] = self.join(half, value, b["in_mid"], which).astype(BF16)
                self.end_copy(half, which).start()

    def result(self, half):
        b = self.blocks[half]
        value = b["acc"][0]
        for which in (0, 1):
            self.end_copy(half, which).wait_recv()
            value = value + b["in_end"][which].astype(F32)
        return value

    def drain(self):
        def body(o):
            for half in (0, 1):
                for which in (0, 1):
                    self.opp_copy(half, o, which).wait_send()
                    self.side_copy(half, o, which).wait_send()
        self.loop(body)
        for half in (0, 1):
            for which in (0, 1):
                self.mid_copy(half, which).wait_send()
                self.end_copy(half, which).wait_send()


REDUCE_BUFFERS = ("sib_out", "sib_in", "in_opp", "in_side", "acc", "in_end", "in_mid")


def reduce_scratch(shapes):
    found = []
    for shape in shapes:
        for lead, kind in (((4,), BF16), ((4, 4), BF16), ((4,), BF16), ((2, 4), BF16), ((4,), F32),
                           ((2,), BF16), ((), BF16)):
            found.append(pltpu.VMEM(lead + shape, kind))
    return found + [pltpu.SemaphoreType.DMA((2, 2, 4, 4)), pltpu.SemaphoreType.DMA((2, 2, 4, 2)),
                    pltpu.SemaphoreType.DMA((2, 2, 4, 2)), pltpu.SemaphoreType.DMA((2, 2, 2)),
                    pltpu.SemaphoreType.DMA((2, 2, 2))]


REDUCE_REFS = 2 * len(REDUCE_BUFFERS) + 5


def make_reduce(me, refs, settings):
    blocks = {}
    count = len(REDUCE_BUFFERS)
    for half in (0, 1):
        part, rows, cut = settings[half]
        blocks[half] = dict(zip(REDUCE_BUFFERS, refs[half * count : half * count + count]))
        blocks[half].update(part=part, rows=rows, cut=cut)
    return Reduce(me, blocks, *refs[2 * count :])


def leave_kernel(x_q, x_o, y_q, y_o, extra, block_u, block_b, out_a, out_b,
                 zout_q, zout_u, zout_b, zin_q, zin_u, zin_b, z_sems, *refs):
    me = Place()
    greet(all_peers(me))

    def upper(column, y):
        return rows_of(column, pl.ds(pl.multiple_of(y * A_ROWS, 16), 144))

    def rows_of(column, rows):
        one = dot(x_q[rows], y_q[column])
        two = dot(x_o[rows], y_o[column, :, 0:128])
        return jnp.concatenate([one[:, :384], one[:, 384:] + two], axis=1)

    def lower(column, y):
        rows = pl.ds(pl.multiple_of(y * A_ROWS + 144, 16), 128)
        return jnp.concatenate([rows_of(column, rows), extra[column]], axis=0)

    reduce = make_reduce(me, refs, ((upper, 144, 64), (lower, 144, 64)))

    def pick_rows(z):
        row = lax.broadcasted_iota(jnp.int32, (80, A_ROWS), 0)
        col = lax.broadcasted_iota(jnp.int32, (80, A_ROWS), 1)
        return jnp.where((col == row + 68 * z) & (row < 68), 1.0, 0.0).astype(BF16)

    def pick_columns(z):
        row = lax.broadcasted_iota(jnp.int32, (D, 384), 0)
        col = lax.broadcasted_iota(jnp.int32, (D, 384), 1)
        return jnp.where((row == col + 272 * z) & (col < 272), 1.0, 0.0).astype(BF16)

    buffers = ((zout_q, zin_q), (zout_u, zin_u), (zout_b, zin_b))

    def z_copy(kind, step):
        source, target = buffers[kind]
        return reduce.copy(source.at[step - 1], target.at[step - 1], z_sems, (kind, step - 1),
                           me.peer("z", step))

    def early(step):
        z = (me.z + step) % 4
        zout_u[step - 1] = dot(pick_rows(z), block_u[...]).astype(BF16)
        zout_b[step - 1] = dot(block_b[...], pick_columns(z)).astype(BF16)
        z_copy(1, step).start()
        z_copy(2, step).start()

    reduce.cross(2, None)
    reduce.opposite()
    reduce.cross(1, 2)
    reduce.cross(3, 1)
    early(2)
    reduce.sides()
    reduce.cross(0, 3)
    early(1)
    early(3)
    reduce.own()
    reduce.middle()
    reduce.last()
    first, second = reduce.result(0), reduce.result(1)
    block_q = jnp.concatenate([first, second[:128]], axis=0).astype(BF16)
    payload = second[128:]

    def slices(z):
        return jnp.concatenate([dot(pick_rows(z), block_q), payload], axis=0)

    for step in (2, 1, 3):
        zout_q[step - 1] = slices((me.z + step) % 4).astype(BF16)
        z_copy(0, step).start()
    near = slices(me.z)
    above = dot(pick_rows(me.z), block_u[...])
    below = dot(block_b[...], pick_columns(me.z))
    for step in (1, 2, 3):
        z_copy(1, step).wait_recv()
        z_copy(2, step).wait_recv()
        above = above + zin_u[step - 1].astype(F32)
        below = below + zin_b[step - 1].astype(F32)
    for step in (1, 2, 3):
        z_copy(0, step).wait_recv()
        near = near + zin_q[step - 1].astype(F32)
    out_a[:, :512] = near[:80]
    out_a[:, 512:] = above
    out_b[:136] = below[:136]
    out_b[136:] = near[80:88, :384]
    reduce.drain()
    for step in (1, 2, 3):
        for kind in range(3):
            z_copy(kind, step).wait_send()


def leave_block(*operands):
    vmem = pltpu.VMEM
    return pl.pallas_call(
        leave_kernel,
        out_shape=(jax.ShapeDtypeStruct((80, WIDE), F32), jax.ShapeDtypeStruct((B_ROWS, 384), F32)),
        in_specs=[pl.BlockSpec(memory_space=vmem)] * 7,
        out_specs=(pl.BlockSpec(memory_space=vmem),) * 2,
        scratch_shapes=(
            [vmem((3, 96, 512), BF16), vmem((3, 80, 640), BF16), vmem((3, B_ROWS, 384), BF16)] * 2
            + [pltpu.SemaphoreType.DMA((2, 3, 3))] + reduce_scratch(((144, 512), (144, 512)))),
        compiler_params=pltpu.CompilerParams(
            collective_id=3, has_side_effects=True, vmem_limit_bytes=60 * 2**20),
    )(*operands)


def push(source, target, sems, index, peer):
    return pltpu.make_async_remote_copy(
        src_ref=source, dst_ref=target, send_sem=sems.at[(0,) + index],
        recv_sem=sems.at[(1,) + index], device_id=peer, device_id_type=MESH)


def turned(value):
    return value.astype(F32).T


def masked(scores, bounds, seq, block):
    rows = lax.broadcasted_iota(jnp.int32, scores.shape, 0)
    spot = block * 256 + lax.broadcasted_iota(jnp.int32, (1, 256), 1)
    start = jnp.zeros((1, 256), jnp.int32)
    for n in range(3):
        bound = bounds[:, 3 * seq + n : 3 * seq + n + 1]
        start = jnp.where(spot >= bound, bound, start)
    return jnp.where((rows <= spot) & (rows >= start), scores, -1e30)


def chances(keys, query, bounds, seq, block):
    scores = lax.dot_general(keys, query, NT, preferred_element_type=F32)
    scores = masked(scores, bounds, seq, block)
    powers = jnp.exp(scores - jnp.max(scores, axis=0, keepdims=True))
    return powers * (1.0 / jnp.sum(powers, axis=0, keepdims=True))


def head_part(value, head):
    lane = lax.broadcasted_iota(jnp.int32, value.shape, 1)
    return jnp.where((lane < 64) == (head == 0), value, jnp.zeros_like(value))


def attend(queries, keys, values, bounds, seq, heads, store, pump):
    queries = queries * 0.125
    value_t = turned(values).astype(BF16)
    for block in range(4):
        rows = slice(block * 256, block * 256 + 256)
        size = block * 256 + 256
        parts = []
        for head in range(heads):
            low = chances(keys[:size], head_part(queries[rows], head), bounds, seq, block).astype(BF16)
            parts.append(dot(value_t[:, :size], low))
            pump()
        whole = parts[0] if heads == 1 else jnp.concatenate([parts[0][:64], parts[1][64:]], axis=0)
        store(block, whole.T.astype(BF16).reshape(2, 128, 128))


def fetch_blocks(source, held, sems):
    copies = [pltpu.make_async_copy(source.at[s], held.at[s], sems.at[s]) for s in range(8)]
    for copy in copies:
        copy.start()
    return copies


GATHER_COPIES = 200
COUNTS_ROW = 12


def enter_kernel(a_ref, b_ref, vec, hidden, gq, gu, gb, att, got, got8, normed_t, lines, up_row,
                 bound_row, weights, za, zb, mine_a, mine_b, vecs, pack, out, out8,
                 send_sems, recv_sems, local_sems, vec_sems, in_sems, in8_sems, back_sems, back8_sems):
    g = Place()
    greet(all_peers(g))
    send = Sender(send_sems, recv_sems)
    first = []
    left, right = pl.ds(0, 512), pl.ds(512, 640)
    for step in (2, 1, 3):
        first.append(send(a_ref.at[:, left], za.at[g.z, :, left], g.peer("z", step)))
    later = []
    for step in (2, 1, 3):
        later.append(send(a_ref.at[:, right], za.at[g.z, :, right], g.peer("z", step)))
        later.append(send(b_ref, zb.at[g.z], g.peer("z", step)))

    def vec_copy(step):
        return push(vec, vecs.at[g.seq], vec_sems, (step - 1,), g.member(g.other(step)))

    for step in range(1, 8):
        vec_copy(step).start()
    vecs[g.seq] = vec[...]
    za[g.z] = a_ref[...]
    zb[g.z] = b_ref[...]
    for copy in first:
        copy.wait_recv()
    mine_a[:, :512] = merge_rows(za[:, :, :512].reshape(320, 512))

    def spot(part, step_x, step_y):
        kind, low, rows = part
        x, y = (g.x + step_x) % 4, (g.y + step_y) % 4
        if kind == "b":
            return gb.at[y, 2 * x + g.c, pl.ds(low, rows)]
        span = pl.ds(pl.multiple_of(y * A_ROWS + low, 16), rows)
        return (weights if kind == "q" else gu).at[2 * x + g.c, span]

    def source(part):
        kind, low, rows = part
        if kind == "b":
            return mine_b.at[pl.ds(low, rows)]
        return mine_a.at[pl.ds(low, rows), left if kind == "q" else right]

    near = Rings(g, send, AXES, {0: ("q", 0, 144), 1: ("q", 144, 128)},
                 {0: [("q", 0, 64), ("q", 64, 80)], 1: [("q", 144, 64), ("q", 208, 64)]}, source, spot)
    rest = Rings(g, send, {0: ("x", "y"), 1: ("y", "x"), 2: ("x", "y")},
                 {0: ("u", 0, 272), 1: ("b", 48, 96), 2: ("b", 0, 48)},
                 {0: [("u", 0, 128), ("u", 128, 144)], 1: [("b", 48, 48), ("b", 96, 48)],
                  2: [("b", 0, 16), ("b", 16, 32)]}, source, spot)
    near.run(("first", 0), ("first", 1), ("second", 0), ("second", 1))
    own = [pltpu.make_async_copy(source(part), spot(part, 0, 0), local_sems.at[k])
           for k, part in enumerate((("q", 0, A_ROWS), ("u", 0, A_ROWS), ("b", 0, B_ROWS)))]
    own[0].start()
    for step in range(1, 8):
        vec_copy(step).wait_recv()
    tiles = {}
    counts = jnp.zeros((1, 128), F32)
    for s in range(8):
        value = vecs[s].astype(F32)
        shift_lanes(tiles, value, 0, 136, 136 * s)
        counts = counts + value[COUNTS_ROW : COUNTS_ROW + 1, :128]
    table = join_tiles(tiles, 9)
    lines[...] = table[:8]
    bound_row[...] = counts.astype(jnp.int32)
    bounds = bound_row[...]
    for y in range(4):
        tiles = {}
        for odd in (0, 1):
            value = vecs[2 * y + odd].astype(F32)
            for row in range(4):
                shift_lanes(tiles, value[8 + row : 9 + row], 0, 136, 544 * odd + 136 * row)
        up_row[y] = join_tiles(tiles, 9)[:, :D]
    unit, _ = normalize(hidden[...].astype(F32).reshape(256, D))
    normed = unit * table[0:1, :D] + table[2:3, :D]
    normed_t[...] = normed.T.astype(BF16)
    normed = normed.astype(BF16)
    near.run(("spread", 0), ("spread", 1), ("relay", 0, 0), ("relay", 1, 0))
    for copy in later:
        copy.wait_recv()
    mine_a[:, 512:] = merge_rows(za[:, :, 512:].reshape(320, 640))
    mine_b[...] = merge_columns(zb)
    own[1].start()
    own[2].start()
    near.run(("far", 0), ("far", 1), ("relay", 0, 1), ("relay", 1, 1), ("close", 0, 0),
             ("close", 1, 0), ("relay", 0, 3), ("relay", 1, 3), ("relay", 0, 2), ("relay", 1, 2))
    rest.run(*EARLY)
    near.run(*[("close", half, by) for by in (1, 3, 2) for half in (0, 1)], ("settle",))
    own[0].wait()
    kept = pltpu.make_async_copy(weights, gq, local_sems.at[3])
    kept.start()
    tiles = ({}, {}, {})
    for s in range(8):
        block = dot(normed, weights[s])
        for seg, low, width, kind, place in segments():
            if seg == s:
                shift_lanes(tiles[kind], block, low, width, place)
    for kind, row in ((0, 4), (1, None), (2, 5)):
        for p in range(9):
            tile = tiles[kind][p]
            if row is not None:
                tile = tile + table[row : row + 1, 128 * p : 128 * p + 128]
            pack[p, kind] = tile.astype(BF16).reshape(2, 128, 128)

    ticks = [0]

    def pump():
        ticks[0] += 1
        rest.run(*LATE.get(ticks[0], ()))

    def in_copy(step):
        return push(pack.at[g.other(step)], got.at[g.seq], in_sems, (step - 1,), g.member(g.other(step)))

    def in8_copy(extra, source):
        return pltpu.make_async_remote_copy(
            src_ref=pack.at[8, :, extra], dst_ref=got8.at[source], send_sem=in8_sems.at[8 + extra],
            recv_sem=in8_sems.at[source], device_id=g.member(4 * extra), device_id_type=MESH)

    for step in (4, 3, 5, 2, 6, 1, 7):
        in_copy(step).start()
    for extra in (0, 1):
        @pl.when(g.seq != 4 * extra)
        def _():
            in8_copy(extra, g.seq).start()

        @pl.when(g.seq == 4 * extra)
        def _():
            got8[g.seq] = pack[8, :, extra]
    got[g.seq] = pack[g.seq]
    rest.run(*LATE[0])
    for step in range(1, 8):
        in_copy(step).wait_recv()

    def back_copy(seq, step):
        return push(out.at[g.other(step), seq], att.at[g.seq, seq], back_sems, (seq, step - 1),
                    g.member(g.other(step)))

    def pair(seq):
        def store(block, value):
            out[pl.ds(2 * block, 2), seq] = value
        part = lambda kind: got[:, kind, seq].reshape(1024, 128)
        attend(part(0), part(1), part(2), bounds, seq, 2, store, pump)
        for step in (4, 3, 5, 2, 6, 1, 7):
            back_copy(seq, step).start()

    for seq in (0, 1):
        pair(seq)
    att[g.seq] = out[g.seq]

    def back8_copy(extra, step):
        return pltpu.make_async_remote_copy(
            src_ref=out8.at[g.other(step)], dst_ref=att.at[8, extra], send_sem=back8_sems.at[1 + step],
            recv_sem=back8_sems.at[extra], device_id=g.member(g.other(step)), device_id_type=MESH)

    for extra in (0, 1):
        @pl.when(g.seq == 4 * extra)
        def _():
            for step in range(1, 8):
                in8_copy(extra, g.other(step)).wait_recv()

            def store(block, value):
                out8[pl.ds(2 * block, 2)] = value
            part = lambda kind: got8[:, kind].reshape(1024, 128)
            attend(part(0), part(1), part(2), bounds, extra, 1, store, lambda: None)
            for step in range(1, 8):
                back8_copy(extra, step).start()
            att[8, extra] = out8[g.seq]
            for step in range(1, 8):
                back8_copy(extra, step).wait_send()

        @pl.when(g.seq != 4 * extra)
        def _():
            in8_copy(extra, g.seq).wait_send()
            back8_copy(extra, 1).wait_recv()
    for step in range(1, 8):
        in_copy(step).wait_send()
        for seq in (0, 1):
            back_copy(seq, step).wait_recv()
            back_copy(seq, step).wait_send()
    rest.run(("settle",))
    for copy in send.made:
        copy.wait_send()
    for step in range(1, 8):
        vec_copy(step).wait_send()
    own[1].wait()
    own[2].wait()
    kept.wait()


def enter_block(*operands):
    tile = (128, 128)
    vmem = pltpu.VMEM
    shape = jax.ShapeDtypeStruct
    return pl.pallas_call(
        enter_kernel,
        out_shape=(
            shape((8, D, 512), BF16), shape((8, D, 640), BF16), shape((4, 8, B_ROWS, D), BF16),
            shape((9, 2) + tile, BF16), shape((8, 3, 2) + tile, BF16), shape((8, 3) + tile, BF16),
            shape((D, 256), BF16), shape((8, WIDE), F32), shape((4, 1, D), F32),
            shape((1, 128), jnp.int32)),
        in_specs=[pl.BlockSpec(memory_space=vmem)] * 4,
        out_specs=(pl.BlockSpec(memory_space=pl.ANY),) * 3 + (pl.BlockSpec(memory_space=vmem),) * 7,
        scratch_shapes=[
            vmem((8, D, 512), BF16), vmem((4, 80, WIDE), BF16), vmem((4, B_ROWS, 384), BF16),
            vmem((A_ROWS, WIDE), BF16), vmem((B_ROWS, D), BF16), vmem((8, 16, 256), BF16),
            vmem((9, 3, 2) + tile, BF16), vmem((8, 2) + tile, BF16), vmem((8,) + tile, BF16),
            pltpu.SemaphoreType.DMA((GATHER_COPIES,)), pltpu.SemaphoreType.DMA((GATHER_COPIES,)),
            pltpu.SemaphoreType.DMA((4,)), pltpu.SemaphoreType.DMA((2, 7)),
            pltpu.SemaphoreType.DMA((2, 7)), pltpu.SemaphoreType.DMA((10,)),
            pltpu.SemaphoreType.DMA((2, 2, 7)), pltpu.SemaphoreType.DMA((9,))],
        compiler_params=pltpu.CompilerParams(
            collective_id=1, has_side_effects=True, vmem_limit_bytes=60 * 2**20),
    )(*operands)


def attend_pull(queries, keys, values, grads, bounds, seq, heads, key_sum, value_sum, store, pump):
    queries = queries * 0.125
    key_t = turned(keys).astype(BF16)
    key_sum[...] = jnp.zeros_like(key_sum)
    value_sum[...] = jnp.zeros_like(value_sum)
    for block in range(4):
        rows = slice(block * 256, block * 256 + 256)
        size = block * 256 + 256
        parts = []
        for head in range(heads):
            query, grad = head_part(queries[rows], head), head_part(grads[rows], head)
            probs = chances(keys[:size], query, bounds, seq, block)
            change = lax.dot_general(values[:size], grad, NT, preferred_element_type=F32)
            inner = jnp.sum(probs * change, axis=0, keepdims=True)
            slope = (probs * (change - inner)).astype(BF16)
            value_sum[:size] += jnp.dot(probs.astype(BF16), grad, preferred_element_type=F32)
            key_sum[:size] += jnp.dot(slope, query, preferred_element_type=F32)
            parts.append(dot(key_t[:, :size], slope))
            pump()
        whole = parts[0] if heads == 1 else jnp.concatenate([parts[0][:64], parts[1][64:]], axis=0)
        store(0, block, (whole.T * 0.125).astype(BF16).reshape(2, 128, 128))
    for kind, total in ((1, key_sum), (2, value_sum)):
        for block in range(4):
            store(kind, block, total[block * 256 : block * 256 + 256].astype(BF16).reshape(2, 128, 128))


def pull_kernel(pack, got, got8, hidden, middle_grad, lines, bound_row, x_o, x_u, y_o, y_u, tt, act,
                sums, up_sums, ga, placed, input_grad, extra, block_u, block_b,
                weights, back, grad, grad8, out, out8, key_sum, value_sum,
                weight_sems, in_sems, in8_sems, back_sems, back8_sems, *refs):
    g = Place()
    bounds = bound_row[...]
    greet(all_peers(g))

    def part_u(column, y):
        rows = pl.ds(pl.multiple_of(y * A_ROWS, 16), A_ROWS)
        three = dot(x_u[rows], y_u[column])
        two = dot(x_o[rows], y_o[column, :, 128:256])
        return jnp.concatenate([three[:, :128] + two, three[:, 128:]], axis=1)

    def part_b(column, y):
        return dot(tt[column], act[y])

    reduce = make_reduce(g, refs, ((part_u, A_ROWS, 128), (part_b, B_ROWS, 64)))
    plan = {1: lambda: reduce.cross(0, 3), 14: reduce.own}
    ticks = [0]

    def pump():
        ticks[0] += 1
        if ticks[0] in plan:
            plan[ticks[0]]()

    def fetch(s):
        return pltpu.make_async_copy(ga.at[s], weights.at[s % 2], weight_sems.at[s % 2])

    fetch(0).start()
    fetch(1).start()

    def in_copy(step):
        return push(pack.at[g.other(step)], grad.at[g.seq], in_sems, (step - 1,), g.member(g.other(step)))

    def in8_copy(which, source):
        return pltpu.make_async_remote_copy(
            src_ref=pack.at[8, which], dst_ref=grad8.at[source], send_sem=in8_sems.at[8 + which],
            recv_sem=in8_sems.at[source], device_id=g.member(4 * which), device_id_type=MESH)

    for step in (4, 3, 5, 2, 6, 1, 7):
        in_copy(step).start()
    for which in (0, 1):
        @pl.when(g.seq != 4 * which)
        def _():
            in8_copy(which, g.seq).start()

        @pl.when(g.seq == 4 * which)
        def _():
            grad8[g.seq] = pack[8, which]
    grad[g.seq] = pack[g.seq]
    reduce.cross(2, None)
    reduce.opposite()
    reduce.cross(1, 2)
    reduce.cross(3, 1)
    reduce.sides()
    for step in range(1, 8):
        in_copy(step).wait_recv()

    def back_copy(seq, step):
        return push(out.at[g.other(step), seq], back.at[g.seq, seq], back_sems, (seq, step - 1),
                    g.member(g.other(step)))

    def pair(seq, carry):
        def store(kind, block, value):
            out[pl.ds(2 * block, 2), seq, kind] = value
        part = lambda kind: got[:, kind, seq].reshape(1024, 128)
        attend_pull(part(0), part(1), part(2), grad[:, seq].reshape(1024, 128), bounds, seq, 2,
                    key_sum, value_sum, store, pump)
        for step in (4, 3, 5, 2, 6, 1, 7):
            back_copy(seq, step).start()
        return carry

    for seq in (0, 1):
        pair(seq, 0)
    back[g.seq] = out[g.seq]

    def back8_copy(which, step):
        return pltpu.make_async_remote_copy(
            src_ref=out8.at[g.other(step)], dst_ref=back.at[8, which], send_sem=back8_sems.at[1 + step],
            recv_sem=back8_sems.at[which], device_id=g.member(g.other(step)), device_id_type=MESH)

    for which in (0, 1):
        @pl.when(g.seq == 4 * which)
        def _():
            for step in range(1, 8):
                in8_copy(which, g.other(step)).wait_recv()

            def store(kind, block, value):
                out8[pl.ds(2 * block, 2), kind] = value
            part = lambda kind: got8[:, kind].reshape(1024, 128)
            attend_pull(part(0), part(1), part(2), grad8[...].reshape(1024, 128), bounds, which, 1,
                        key_sum, value_sum, store, lambda: None)
            for step in range(1, 8):
                back8_copy(which, step).start()
            back[8, which] = out8[g.seq]
            for step in range(1, 8):
                back8_copy(which, step).wait_send()

        @pl.when(g.seq != 4 * which)
        def _():
            in8_copy(which, g.seq).wait_send()
            back8_copy(which, 1).wait_recv()
    reduce.middle()
    for step in range(1, 8):
        in_copy(step).wait_send()
        for seq in (0, 1):
            back_copy(seq, step).wait_recv()
            back_copy(seq, step).wait_send()

    natural = [jnp.concatenate([back[p, :, kind].reshape(256, 128) for p in range(9)],
                               axis=1).astype(F32) for kind in range(3)]
    total = None
    for s in range(8):
        tiles = {}
        for seg, low, width, kind, spot in segments():
            if seg == s:
                shift_lanes(tiles, natural[kind], spot, width, low)
        block = join_tiles(tiles, 4).astype(BF16)
        placed[s] = block
        fetch(s).wait()
        term = dot_t(block, weights[s % 2])
        if s < 6:
            fetch(s + 2).start()
        total = term if total is None else total + term
    reduce.last()
    unit, scale = normalize(hidden[...].astype(F32).reshape(256, D))
    input_grad[...] = middle_grad[...] + norm_pull(total, lines[0:1, :D], unit, scale)

    def column_sum(value):
        return jnp.sum(value, axis=0, keepdims=True)

    table = jnp.concatenate([
        column_sum(widen(total * unit)), sums[0:1], column_sum(widen(total)), sums[1:2],
        column_sum(natural[0]), column_sum(natural[2]), sums[2:4]], axis=0)
    for s in range(8):
        tiles = {}
        shift_lanes(tiles, table, 136 * s, 136, 0)
        first = join_tiles(tiles, 4)
        rows = []
        for row in range(4):
            tiles = {}
            shift_lanes(tiles, up_sums[s], 32 + 136 * row, 136, 136)
            rows.append(join_tiles(tiles, 4))
        second = jnp.concatenate(rows + [jnp.zeros((4, 512), F32)], axis=0)
        extra[s] = jnp.concatenate([first + second, jnp.zeros((8, 512), F32)], axis=0)
    block_u[...] = reduce.result(0).astype(BF16)
    block_b[...] = reduce.result(1).astype(BF16)
    reduce.drain()


def attend_backward(*operands):
    tile = (128, 128)
    vmem = pltpu.VMEM
    return pl.pallas_call(
        pull_kernel,
        out_shape=(jax.ShapeDtypeStruct((8, 256, 512), BF16),
                   jax.ShapeDtypeStruct((256, D), F32), jax.ShapeDtypeStruct((8, 16, 512), F32),
                   jax.ShapeDtypeStruct((A_ROWS, 640), BF16), jax.ShapeDtypeStruct((B_ROWS, D), BF16)),
        in_specs=[pl.BlockSpec(memory_space=vmem)] * 15 + [pl.BlockSpec(memory_space=pl.ANY)],
        out_specs=(pl.BlockSpec(memory_space=vmem),) * 5,
        scratch_shapes=[
            vmem((2, D, 512), BF16), vmem((9, 2, 3) + tile, BF16), vmem((8, 2) + tile, BF16), vmem((8,) + tile, BF16),
            vmem((8, 2, 3) + tile, BF16), vmem((8, 3) + tile, BF16),
            vmem((1024, 128), F32), vmem((1024, 128), F32),
            pltpu.SemaphoreType.DMA((2,)),
            pltpu.SemaphoreType.DMA((2, 7)), pltpu.SemaphoreType.DMA((10,)),
            pltpu.SemaphoreType.DMA((2, 2, 7)), pltpu.SemaphoreType.DMA((9,)),
        ] + reduce_scratch(((A_ROWS, 640), (B_ROWS, D))),
        compiler_params=pltpu.CompilerParams(
            collective_id=2, has_side_effects=True, vmem_limit_bytes=63 * 2**20),
    )(*operands)


def middle_kernel(att, hidden, top, lines, up_row, gq, gu, gb,
                  layer_out, middle_grad, att_grad, att_t, normed_t, active, y_o, y_u, sums, up_sums, top_t,
                  held_o, held_u, held_b, normed, down_sum, norm_grad, top_pad, sems_o, sems_u, sems_b):
    copies_o = []
    for s in range(8):
        copies_o.append(pltpu.make_async_copy(
            gq.at[s, :, pl.ds(384, 128)], held_o.at[s, :, pl.ds(0, 128)], sems_o.at[0, s]))
        copies_o.append(pltpu.make_async_copy(
            gu.at[s, :, pl.ds(0, 128)], held_o.at[s, :, pl.ds(128, 128)], sems_o.at[1, s]))
    for copy in copies_o:
        copy.start()

    def up_copy(s):
        return pltpu.make_async_copy(gu.at[s], held_u.at[s], sems_u.at[s])

    def down_copy(y):
        return pltpu.make_async_copy(gb.at[y], held_b.at[y], sems_b.at[y])

    for y in range(4):
        up_copy(2 * y).start()
        up_copy(2 * y + 1).start()
        down_copy(y).start()

    tiles = {}
    for s in range(8):
        shift_lanes(tiles, widen(top[...].reshape(256, D)).astype(F32), 136 * s, 136, 144 * s)
    padded = join_tiles(tiles, 9)
    top_pad[...] = padded.astype(BF16)
    top_t[...] = padded.T.astype(BF16).reshape(8, B_ROWS, 256)
    attended = jnp.concatenate([att[p].reshape(256, 128) for p in range(9)], axis=1)
    att_t[...] = attended.astype(F32).T[:D].astype(BF16)
    tiles = {}
    for s in range(8):
        copies_o[2 * s].wait()
        copies_o[2 * s + 1].wait()
        shift_lanes(tiles, dot(attended[:, :D], held_o[s]), 24, 136, 136 * s)
    branch = join_tiles(tiles, 9)[:, :D]
    middle = hidden[...].astype(F32).reshape(256, D) + branch + lines[6:7, :D]
    unit, scale = normalize(middle)
    value = unit * lines[1:2, :D] + lines[3:4, :D]
    normed[...] = value.astype(BF16)
    normed_t[...] = value.T.astype(BF16)
    down_sum[...] = jnp.zeros_like(down_sum)
    norm_grad[...] = jnp.zeros_like(norm_grad)

    def step(y, carry):
        tiles = {}
        for odd in (0, 1):
            up_copy(2 * y + odd).wait()
            shift_lanes(tiles, dot(normed[...], held_u[2 * y + odd]), 32, 544, 544 * odd)
        pre = join_tiles(tiles, 9)[:, :D] + up_row[y]
        cube = 0.7978845608028654 * (pre + 0.044715 * (pre * pre * pre))
        bend = jnp.tanh(cube)
        half = 0.5 * (1.0 + bend)
        acts = (pre * half).astype(BF16)
        slope = half + 0.5 * pre * (1.0 - bend * bend) * (
            0.7978845608028654 * (1.0 + 3 * 0.044715 * (pre * pre)))
        active[y] = acts
        down_copy(y).wait()
        weights = held_b[y].reshape(8 * B_ROWS, D)
        down_sum[...] += dot_t(acts, weights)
        inner = dot(top_pad[...], weights) * slope
        inner = widen(inner.astype(BF16).astype(F32))
        total = None
        for odd in (0, 1):
            tiles = {}
            shift_lanes(tiles, inner, 544 * odd, 544, 32)
            block = join_tiles(tiles, 5)
            up_sums[2 * y + odd] = jnp.sum(block, axis=0, keepdims=True)
            block = block.astype(BF16)
            y_u[2 * y + odd] = block
            term = dot_t(block, held_u[2 * y + odd])
            total = term if total is None else total + term
        norm_grad[...] += total
        return carry

    lax.fori_loop(0, 4, step, 0)
    tiles = {}
    down = down_sum[...]
    for s in range(8):
        shift_lanes(tiles, down, 144 * s, 136, 136 * s)
    out = middle + join_tiles(tiles, 9)[:, :D] + lines[7:8, :D]
    layer_out[...] = out.astype(BF16).reshape(2, 128, D)
    grad = norm_grad[...]
    cotangent = top[...].astype(F32).reshape(256, D)
    total = cotangent + norm_pull(grad, lines[1:2, :D], unit, scale)
    middle_grad[...] = total
    branch = widen(total.astype(BF16).astype(F32))
    back = None
    for s in range(8):
        tiles = {}
        shift_lanes(tiles, branch, 136 * s, 136, 24)
        block = join_tiles(tiles, 2).astype(BF16)
        y_o[s] = block
        term = dot_t(block, held_o[s])
        back = term if back is None else back + term
    back = widen(back).astype(BF16)
    for p in range(9):
        att_grad[p] = back[:, 128 * p : 128 * p + 128].reshape(2, 128, 128)
    sums[0:1] = jnp.sum(widen(grad * unit), axis=0, keepdims=True)
    sums[1:2] = jnp.sum(widen(grad), axis=0, keepdims=True)
    sums[2:3] = jnp.sum(branch, axis=0, keepdims=True)
    sums[3:4] = jnp.sum(widen(cotangent), axis=0, keepdims=True)
    sums[4:8] = jnp.zeros((4, WIDE), F32)


def middle_block(*operands):
    vmem = pltpu.VMEM
    shape = jax.ShapeDtypeStruct
    return pl.pallas_call(
        middle_kernel,
        out_shape=(
            shape((2, 128, D), BF16), shape((256, D), F32), shape((9, 2, 128, 128), BF16),
            shape((D, 256), BF16), shape((D, 256), BF16), shape((4, 256, D), BF16),
            shape((8, 256, 256), BF16), shape((8, 256, 640), BF16), shape((8, WIDE), F32),
            shape((8, 1, 640), F32), shape((8, B_ROWS, 256), BF16)),
        in_specs=[pl.BlockSpec(memory_space=vmem)] * 5 + [pl.BlockSpec(memory_space=pl.ANY)] * 3,
        out_specs=(pl.BlockSpec(memory_space=vmem),) * 11,
        scratch_shapes=[
            vmem((8, D, 256), BF16), vmem((8, D, 640), BF16), vmem((4, 8, B_ROWS, D), BF16),
            vmem((256, D), BF16), vmem((256, WIDE), F32), vmem((256, D), F32), vmem((256, WIDE), BF16),
            pltpu.SemaphoreType.DMA((2, 8)), pltpu.SemaphoreType.DMA((8,)),
            pltpu.SemaphoreType.DMA((4,))],
        compiler_params=pltpu.CompilerParams(vmem_limit_bytes=62 * 2**20),
    )(*operands)


def per_device(
    inputs, out_grad, segment_ids, qkv_weight, out_weight, up_weight, down_weight,
    norm_gains, norm_shifts, qv_bias, proj_bias, up_bias,
):
    seqs, rows, _ = inputs.shape

    blob_a = jnp.concatenate([qkv_weight, out_weight, up_weight], axis=1)
    blob_a = jnp.pad(blob_a, ((0, 12), (0, WIDE - D)))
    counts = jnp.sum(segment_ids[:, :, None] < jnp.arange(1, 4)[None, None, :], axis=1)
    counts = jnp.pad(counts.astype(BF16).reshape(1, 6), ((0, 3), (0, 130)))
    vec = jnp.concatenate(
        [norm_gains, norm_shifts, qv_bias, proj_bias, up_bias.reshape(4, 136), counts], axis=0
    )
    vec = jnp.pad(vec, ((0, 0), (0, 120)))
    blob_b = jnp.pad(down_weight.T, ((0, 8), (0, 112)))

    (w_q, w_u, w_b, att, got, got8, normed_t, lines, up_row, bounds) = enter_block(
        blob_a, blob_b, vec, inputs
    )
    (layer_out, middle_grad, att_grad, att_t, normed_two_t, active, y_o, y_u, sums, up_sums, top_t) = (
        middle_block(att, inputs, out_grad, lines, up_row, w_q, w_u, w_b)
    )
    y_q, input_grad, extra, block_u, block_b = attend_backward(
        att_grad, got, got8, inputs, middle_grad, lines, bounds, att_t, normed_two_t, y_o, y_u,
        top_t, active, sums, up_sums, w_q
    )
    out_a, out_b = leave_block(normed_t, att_t, y_q, y_o, extra, block_u, block_b)
    return (
        layer_out,
        input_grad.reshape(seqs, rows, D),
        out_a[:68, :408],
        out_a[:68, 408:544],
        out_a[:68, 544:D],
        out_b[:136, :272].T,
        out_b[136:138, :136],
        out_b[138:140, :136],
        out_b[140:142, :136],
        out_b[142:144, :136],
        out_b[136:140, 136:272].reshape(1, 544),
    )


def solution(mesh):
    tokens = P("batch", "seq", None)
    matrix = P("batch", "seq")
    vector = P(None, "seq")
    return jax.shard_map(
        per_device,
        mesh=mesh,
        in_specs=(tokens, tokens, matrix, matrix, matrix, matrix, matrix) + (vector,) * 5,
        out_specs=(tokens, tokens, matrix, matrix, matrix, matrix) + (vector,) * 5,
        check_vma=False,
    )
```
